32 devices in a mesh: dp: 8 (over z, y), tensor: 4 (over x, core).
Axes of the slice: x: 2, y: 2, z: 4, core: 2. Of those that a mesh axis runs over, the one named last changes fastest.
Arguments:
- input_token_ids: int32 [4, 32, 512], P(None, ('dp', 'tensor')), may hold values from 0 to 50264
- segments: int32 [4, 32, 512], P(None, ('dp', 'tensor')), may hold values from -1 to 63, as said below
- labels: float32 [4, 32, 64], P(None, ('dp', 'tensor')), may hold values from 0 to 5
- embedding: bfloat16 [768, 50265], P('tensor'), may hold values from -6 to 6
- position_embedding_table: bfloat16 [512, 768], replicated, may hold values from -3 to 3
- norm_gain_rows: float32 [3, 768], replicated, may hold values from 0.5 to 1.5
- norm_shift_rows: float32 [3, 768], replicated, may hold values from -0.3 to 0.3
- query_key_value_weight: bfloat16 [3, 768, 768], replicated, may hold values from -0.21875 to 0.21875
- attention_output_weight: bfloat16 [768, 768], replicated, may hold values from -0.625 to 0.625
- attention_bias_stack: float32 [5, 768], replicated, may hold values from -0.3 to 0.3
- feedforward_in_weight: bfloat16 [768, 3072], P(None, 'tensor'), may hold values from -0.21875 to 0.21875
- feedforward_bias: bfloat16 [3072], P('tensor'), may hold values from -0.59765625 to 0.59765625
- feedforward_out_weight: bfloat16 [3072, 768], P('tensor'), may hold values from -0.109375 to 0.109375
- adapter_down_weight: bfloat16 [2, 768, 8], replicated, may hold values from -0.21875 to 0.21875
- adapter_up_weight: float32 [2, 8, 768], replicated, may hold values from -0.3 to 0.3
- adapter_momentum: float32 [2, 8, 768], replicated, may hold values from -0.0017089844 to 0.0017089844
- head: float32 [769], replicated, may hold values from -0.21875 to 0.21875
- head_first_moment: float32 [769], replicated, may hold values from -0.015625 to 0.015625
- head_second_moment: float32 [769], replicated, may hold values from 6e-08 to 2.6e-07
Outputs:
- squared_error_sum: float32 [], replicated
- item_count: float32 [], replicated
- global_gradient_norm: float32 [], replicated
- adapter_moment_next: float32 [2, 8, 768], replicated
- adapter_up_updated: float32 [2, 8, 768], replicated
- lora_low: bfloat16 [2, 8, 768], replicated
- head_moment_next: float32 [769], replicated
- head_square_next: float32 [769], replicated
- head_updated: float32 [769], replicated
- head_low: bfloat16 [769], replicated
The draws below stay inside these ranges and needn't reach their ends.
Inputs may be any that keep to these rules, and one draw needn't show every extreme that they name: `segments`: each sequence holds whole items from its first row on, numbered 0, 1, 2, ... in order, each of 8 to 128 rows; the rows after the last item are -1. In the first micro-batch one sequence is filled entirely with items of 8 rows, so item numbers reach 63.
All inputs are finite; a program needn't handle non-finite values.
Results may differ from the reference program's by a relative error of at most 0.0055.
Values may be sent and summed in bfloat16 or wider, within the bound.
No kernel may reach another device: no remote copies, remote signals or barrier semaphores. Data moves between devices by JAX's collectives and lax.ppermute only.
A program may use at most 320 MiB of HBM per device.

```python
import math
import jax
import jax.numpy as jnp
from jax import lax

MODEL_WIDTH = 768
HEADS = 12
HEAD_DIM = 64
FF = 3072
VOCAB = 50265
ADAPTER_RANK = 8
SEQ_LEN = 512
MICRO = 4
STEP = 10
SEQS = 32
ITEMS = 64


def draw_segments(key, part):
    key = jax.random.fold_in(key, 11)
    longest = min(128, SEQ_LEN // 3)
    item_sizes = jax.random.randint(key, (MICRO, SEQS, ITEMS), 8, longest + 1)
    chosen = jax.random.randint(jax.random.fold_in(key, 1), (), 0, SEQS)
    micro_rank = jnp.arange(MICRO, dtype=jnp.int32)
    seq_rank = jnp.arange(SEQS, dtype=jnp.int32)
    filled = (micro_rank[:, None] == 0) & (seq_rank[None, :] == chosen)
    item_sizes = jnp.where(filled[:, :, None], 8, item_sizes)
    item_ends = jnp.cumsum(item_sizes, axis=-1)
    target = SEQ_LEN * (10 + 20 * seq_rank // max(SEQS - 1, 1)) // 30
    target = jnp.where(filled, SEQ_LEN, target[None, :])
    live_end = jnp.max(jnp.where(item_ends <= target[:, :, None], item_ends, 0), axis=-1)
    row_index = jnp.arange(SEQ_LEN, dtype=jnp.int32)
    number = jnp.sum((item_ends[:, :, None, :] <= row_index[None, None, :, None]).astype(jnp.int32), axis=-1)
    return jnp.where(row_index[None, None, :] < live_end[:, :, None], number, -1).astype(jnp.int32)


def with_ends(entries, stream_key, smallest, high):
    extent = entries.shape
    place = [jax.random.randint(jax.random.fold_in(stream_key, axis), (), 0, extent[axis]) for axis in range(len(extent))]
    entries = entries.at[tuple(place)].set(smallest)
    longest = extent.index(max(extent))
    place[longest] = (place[longest] + 1) % extent[longest]
    return entries.at[tuple(place)].set(high)


def steps_of(key, shape, pieces, low, top_value):
    level, own = 1.0, jax.random.fold_in(key, 6)
    for position, blocks in pieces:
        steps = jnp.exp(jax.random.uniform(jax.random.fold_in(own, position), (blocks,), jnp.float32, low / len(pieces), top_value / len(pieces)))
        level = level * jnp.repeat(steps, shape[position] // blocks).reshape([-1 if axis == position else 1 for axis in range(len(shape))])
    return level


def gaussian(own_key, dims, width, reach, split=(), kind=jnp.bfloat16):
    level = steps_of(own_key, dims, split, -0.22, 0.18) if split else 1.0
    entries = jax.random.normal(own_key, dims, jnp.float32) * width * level
    return jnp.minimum(jnp.maximum(entries, -reach), reach).astype(kind)


def setup_inputs(seed: int = 0) -> dict:
    keys = jax.random.split(jax.random.key(seed), 20)
    input_token_ids = with_ends(jax.random.randint(keys[0], (MICRO, SEQS, SEQ_LEN), 0, VOCAB), jax.random.fold_in(keys[0], 1), 0, VOCAB - 1).astype(jnp.int32)
    segments = draw_segments(jax.random.fold_in(keys[19], 71), 0)
    labels = jnp.clip(5.0 * jax.random.uniform(keys[2], (MICRO, SEQS, ITEMS), jnp.float32) ** steps_of(keys[2], (MICRO, SEQS, ITEMS), ((1, 32),), -0.2, 0.2), 0.0, 5.0)
    embedding = gaussian(keys[3], (MODEL_WIDTH, VOCAB), 1.0, 6.0, ((0, 4),))
    position_embedding_table = gaussian(keys[4], (SEQ_LEN, MODEL_WIDTH), 0.5, 3.0)
    norm_gain_rows = jnp.clip(1.0 + 0.1 * jax.random.normal(keys[5], (3, MODEL_WIDTH), jnp.float32), 0.5, 1.5)
    norm_shift_rows = gaussian(keys[6], (3, MODEL_WIDTH), 0.05, 0.3, (), jnp.float32)
    query_key_value_weight = gaussian(keys[7], (3, MODEL_WIDTH, MODEL_WIDTH), MODEL_WIDTH ** -0.5, 0.21875)
    attention_output_weight = gaussian(keys[8], (MODEL_WIDTH, MODEL_WIDTH), (MODEL_WIDTH // 8) ** -0.5, 0.625)
    attention_bias_stack = gaussian(keys[9], (5, MODEL_WIDTH), 0.05, 0.3, (), jnp.float32)
    feedforward_in_weight = gaussian(keys[10], (MODEL_WIDTH, FF), MODEL_WIDTH ** -0.5, 0.21875, ((1, 4),))
    feedforward_bias = gaussian(keys[11], (FF,), 0.1, 0.59765625, ((0, 4),))
    feedforward_out_weight = gaussian(keys[12], (FF, MODEL_WIDTH), FF ** -0.5, 0.109375, ((0, 4),))
    adapter_down_weight = gaussian(keys[13], (2, MODEL_WIDTH, ADAPTER_RANK), MODEL_WIDTH ** -0.5, 0.21875)
    adapter_up_weight = gaussian(keys[14], (2, ADAPTER_RANK, MODEL_WIDTH), 0.05, 0.3, (), jnp.float32)
    adapter_momentum = gaussian(keys[15], (2, ADAPTER_RANK, MODEL_WIDTH), (0.03 * (MICRO * SEQS * SEQ_LEN) ** -0.5), 0.0017089844, (), jnp.float32)
    head = gaussian(keys[16], (MODEL_WIDTH + 1,), MODEL_WIDTH ** -0.5, 0.21875, (), jnp.float32)
    head_first_moment = gaussian(keys[17], (MODEL_WIDTH + 1,), 0.001, 0.015625, (), jnp.float32)
    head_second_moment = jnp.clip(jnp.exp(jax.random.uniform(keys[18], (MODEL_WIDTH + 1,), jnp.float32, math.log(5.99999978589949e-08), math.log(2.6000000730164174e-07))), 5.99999978589949e-08, 2.6000000730164174e-07)
    return {"input_token_ids": input_token_ids, "segments": segments, "labels": labels, "embedding": embedding, "position_embedding_table": position_embedding_table, "norm_gain_rows": norm_gain_rows, "norm_shift_rows": norm_shift_rows, "query_key_value_weight": query_key_value_weight, "attention_output_weight": attention_output_weight, "attention_bias_stack": attention_bias_stack, "feedforward_in_weight": feedforward_in_weight, "feedforward_bias": feedforward_bias, "feedforward_out_weight": feedforward_out_weight, "adapter_down_weight": adapter_down_weight, "adapter_up_weight": adapter_up_weight, "adapter_momentum": adapter_momentum, "head": head, "head_first_moment": head_first_moment, "head_second_moment": head_second_moment}


@jax.custom_vjp
def lowered_input(v):
    return lax.optimization_barrier(v.astype(jnp.bfloat16)).astype(jnp.float32)

@jax.custom_vjp
def low_back(v):
    return v

def low_keep(v):
    return (lowered_input(v), None)

def low_pass(kept, grad):
    return (grad,)

def back_keep(v):
    return (v, None)

def back_low(kept, grad):
    return (lowered_input(grad),)
lowered_input.defvjp(low_keep, low_pass)
low_back.defvjp(back_keep, back_low)
LN_EPS = 1e-05
CLIP_NORM = 0.5
ADAPTER_SCALE = 2.0
ORTHO_MOMENTUM = 0.5
ORTHO_STEP_SIZE = 1.0
NS_A = 3.4445
NS_B = -4.775
NS_C = 2.0315
BETA_ONE = 0.9
BETA_TWO = 0.999
ADAM_RATE = 0.05
ADAM_EPS = 1e-08
DECAY = 0.01
TOP_PRECISION = lax.Precision.HIGHEST

def matrix_product(left, right):
    return jnp.dot(left, right, precision=TOP_PRECISION)

def layer_norm(value_rows, gain_row, shift_row):
    center = lax.optimization_barrier(jnp.mean(value_rows, -1, keepdims=True))
    offset = value_rows - center
    spread = lax.optimization_barrier(jnp.mean(offset * offset, -1, keepdims=True))
    return offset * lax.rsqrt(spread + LN_EPS) * gain_row + shift_row

def within_item(segment):
    sequence_length = segment.shape[-1]
    column = jnp.arange(sequence_length, dtype=jnp.int32)
    before = jnp.concatenate([jnp.full(segment.shape[:-1] + (1,), -2, jnp.int32), segment[..., :-1]], -1)
    opening = jnp.where(segment != before, column, 0).astype(jnp.int32)
    return column - lax.cummax(opening, axis=segment.ndim - 1)

def exact_gelu(value_rows):
    return jax.nn.gelu(value_rows, approximate=False)

def sequence_loss(trained_params, frozen_params, start_rows, segment, label):
    adapter_up_weight, head = trained_params
    norm_gain_row, norm_shift_row, query_key_value, output_projection, attention_biases, input_weight, input_bias, output_weight, adapter_down_weight = frozen_params
    sequence_length = start_rows.shape[0]
    normed0 = layer_norm(start_rows, norm_gain_row[0], norm_shift_row[0])
    lowered_input0 = lowered_input(normed0)
    reduced_query_gradient = lowered_input(matrix_product(lowered_input0, adapter_down_weight[0]))
    reduced_value_gradient = lowered_input(matrix_product(lowered_input0, adapter_down_weight[1]))
    adapter_lowered_up = lowered_input(adapter_up_weight)
    query_rows = matrix_product(lowered_input0, query_key_value[0]) + attention_biases[0] + ADAPTER_SCALE * matrix_product(reduced_query_gradient, adapter_lowered_up[0])
    key_rows = matrix_product(lowered_input0, query_key_value[1]) + attention_biases[1]
    value_rows = matrix_product(lowered_input0, query_key_value[2]) + attention_biases[2] + ADAPTER_SCALE * matrix_product(reduced_value_gradient, adapter_lowered_up[1])
    query_r = lowered_input(low_back(query_rows)).reshape(sequence_length, HEADS, HEAD_DIM)
    key_r = lowered_input(key_rows).reshape(sequence_length, HEADS, HEAD_DIM)
    value_r = lowered_input(low_back(value_rows)).reshape(sequence_length, HEADS, HEAD_DIM)
    raw = low_back(jnp.einsum('qhd,khd->hqk', query_r, key_r, precision=TOP_PRECISION))
    allowed = segment[:, None] == segment[None, :]
    scores = jnp.where(allowed[None], raw * HEAD_DIM ** (-0.5), -1000000000.0)
    attn_probs = jax.nn.softmax(scores, axis=-1)
    mixed = jnp.einsum('hqk,khd->qhd', lowered_input(attn_probs), value_r, precision=TOP_PRECISION).reshape(sequence_length, -1)
    attended = low_back(matrix_product(lowered_input(low_back(mixed)), output_projection) + attention_biases[3])
    resid1 = normed0 + attended
    normed1 = layer_norm(resid1, norm_gain_row[1], norm_shift_row[1])
    pre_act = low_back(matrix_product(lowered_input(normed1), input_weight) + input_bias)
    ffn_part = low_back(matrix_product(lowered_input(exact_gelu(pre_act)), output_weight) + attention_biases[4])
    resid2 = normed1 + ffn_part
    normalized_second = layer_norm(resid2, norm_gain_row[2], norm_shift_row[2])
    batch_member = (segment[None, :] == jnp.arange(ITEMS, dtype=jnp.int32)[:, None]).astype(jnp.float32)
    counts = lax.optimization_barrier(jnp.sum(batch_member, 1))
    pooled = matrix_product(batch_member, normalized_second) / jnp.maximum(counts, 1.0)[:, None]
    predicted = matrix_product(pooled, head[:-1]) + head[-1]
    pred_error = jnp.where(counts > 0, predicted - label, 0.0)
    return jnp.sum(pred_error * pred_error)

def newton_schulz_orthogonal(moment):
    basis = moment / (jnp.sqrt(jnp.sum(moment * moment)) + 1e-07)
    for sweep in range(5):
        gram = matrix_product(basis, basis.T)
        poly = NS_B * gram + NS_C * matrix_product(gram, gram)
        basis = NS_A * basis + matrix_product(poly, basis)
    return basis

def reference(input_token_ids, segments, labels, embedding, position_embedding_table, norm_gain_rows, norm_shift_rows, query_key_value_weight, attention_output_weight, attention_bias_stack, feedforward_in_weight, feedforward_bias, feedforward_out_weight, adapter_down_weight, adapter_up_weight, adapter_momentum, head, head_first_moment, head_second_moment):
    item_gradient_sum = jnp.sum(lax.optimization_barrier(jnp.max(segments, axis=-1)) + 1).astype(jnp.float32)
    frozen_params = (norm_gain_rows, norm_shift_rows, query_key_value_weight.astype(jnp.float32), attention_output_weight.astype(jnp.float32), attention_bias_stack, feedforward_in_weight.astype(jnp.float32), feedforward_bias.astype(jnp.float32), feedforward_out_weight.astype(jnp.float32), adapter_down_weight.astype(jnp.float32))
    flattened_token_ids = input_token_ids.reshape(-1, SEQ_LEN)
    flattened_segment = segments.reshape(-1, SEQ_LEN)
    flattened_labels = labels.reshape(-1, ITEMS)

    def single_sequence(running, inputs):
        ids_row, seg_row, lab_row = inputs
        start_rows = jnp.take(embedding, ids_row, axis=1).T.astype(jnp.float32) + jnp.take(position_embedding_table, within_item(seg_row), axis=0).astype(jnp.float32)

        def compute_loss(trained_params):
            return sequence_loss(trained_params, frozen_params, start_rows, seg_row, lab_row)
        squared_error, backward_function = jax.vjp(compute_loss, (adapter_up_weight, head))
        (grad_b, grad_h), = backward_function(1.0 / item_gradient_sum)
        return ((running[0] + squared_error, running[1] + grad_b, running[2] + grad_h), None)
    initial_values = (jnp.zeros((), jnp.float32), jnp.zeros(adapter_up_weight.shape, jnp.float32), jnp.zeros(head.shape, jnp.float32))
    (squared_error_sum, adapter_gradient, head_gradient), unused_value = lax.scan(single_sequence, initial_values, (flattened_token_ids, flattened_segment, flattened_labels))
    global_gradient_norm = jnp.sqrt(jnp.sum(adapter_gradient * adapter_gradient) + jnp.sum(head_gradient * head_gradient))
    scale_factor = jnp.minimum(1.0, CLIP_NORM / (global_gradient_norm + 1e-06))
    adapter_moment_next = ORTHO_MOMENTUM * adapter_momentum + scale_factor * adapter_gradient
    orthogonal_update = jnp.stack([newton_schulz_orthogonal(adapter_moment_next[0]), newton_schulz_orthogonal(adapter_moment_next[1])])
    adapter_up_updated = adapter_up_weight - ORTHO_STEP_SIZE * orthogonal_update
    clipped = scale_factor * head_gradient
    head_moment_next = BETA_ONE * head_first_moment + (1.0 - BETA_ONE) * clipped
    head_square_next = BETA_TWO * head_second_moment + (1.0 - BETA_TWO) * clipped * clipped
    first_hat = head_moment_next / (1.0 - BETA_ONE ** STEP)
    second_hat = head_square_next / (1.0 - BETA_TWO ** STEP)
    head_updated = head - ADAM_RATE * (first_hat / (jnp.sqrt(second_hat) + ADAM_EPS) + DECAY * head)
    return (squared_error_sum, item_gradient_sum, global_gradient_norm, adapter_moment_next, adapter_up_updated, adapter_up_updated.astype(jnp.bfloat16), head_moment_next, head_square_next, head_updated, head_updated.astype(jnp.bfloat16))
```

```python
import functools
import math

import jax
import jax.numpy as jnp
from jax import lax
from jax.experimental import pallas as pl
from jax.experimental.pallas import tpu as pltpu
from jax.sharding import PartitionSpec as P

HEAD_DIM = 64
STEP = 10
LN_EPS = 1e-05
CLIP_NORM = 0.5
ORTHO_MOMENTUM = 0.5
ORTHO_STEP_SIZE = 1.0
NS_A = 3.4445
NS_B = -4.775
NS_C = 2.0315
BETA_ONE = 0.9
BETA_TWO = 0.999
ADAM_RATE = 0.05
ADAM_EPS = 1e-08
DECAY = 0.01
TOP_PRECISION = lax.Precision.HIGHEST

F32 = jnp.float32
BF16 = jnp.bfloat16
LANES = 128
GROUP = 256
BLOCK = 128
NN = (((1,), (0,)), ((), ()))
NT = (((1,), (1,)), ((), ()))
TN = (((0,), (0,)), ((), ()))
INV_SQRT2 = 1.0 / math.sqrt(2.0)
INV_SQRT_2PI = 1.0 / math.sqrt(2.0 * math.pi)


def mm(left, right, dims=NN):
    return lax.dot_general(left, right, dims, preferred_element_type=F32)


def row_mean(rows):
    return jnp.mean(rows, axis=-1, keepdims=True)


def layer_kernel(
    x_ref,
    seg_ref,
    label_ref,
    pos_ref,
    gain_ref,
    shift_ref,
    bias_ref,
    down_ref,
    up_ref,
    head_ref,
    ffb_ref,
    acc_in_ref,
    wqkv_hbm,
    wo_hbm,
    win_hbm,
    wout_hbm,
    acc_ref,
    wqkv,
    wo,
    win,
    wout,
    xb,
    normed0,
    q,
    k,
    v,
    red,
    vr,
    pr,
    probs,
    mixed,
    xh1,
    stat1,
    acc,
    slope,
    act,
    sems,
):
    rows, width = normed0.shape
    parts = x_ref.shape[0]
    hidden_part = win.shape[2]
    groups = width // GROUP
    per_group = GROUP // HEAD_DIM
    blocks = rows // BLOCK
    tiles = rows // GROUP
    span = 3 * BLOCK
    chunk = 256 if hidden_part % 256 == 0 else hidden_part
    step_rows = 64
    row_steps = rows // step_rows

    copies = [
        pltpu.make_async_copy(wqkv_hbm, wqkv, sems.at[0]),
        pltpu.make_async_copy(wo_hbm, wo, sems.at[1]),
        pltpu.make_async_copy(win_hbm, win, sems.at[2]),
        pltpu.make_async_copy(wout_hbm, wout, sems.at[3]),
    ]
    for copy in copies:
        copy.start()

    seg_row = seg_ref[...].astype(F32)
    lane = lax.broadcasted_iota(jnp.int32, (rows, rows), 1)
    sub = lax.broadcasted_iota(jnp.int32, (rows, rows), 0)
    seg_col = jnp.sum(jnp.where(lane == sub, seg_row, 0.0), axis=1, keepdims=True)
    same = seg_col == seg_row
    place = jnp.sum(jnp.where(same & (lane < sub), 1.0, 0.0), axis=1, keepdims=True)
    one_hot = jnp.where(lane == place.astype(jnp.int32), 1.0, 0.0).astype(BF16)
    pieces = jnp.concatenate([x_ref[t] for t in range(parts)], axis=1).astype(F32)
    acc[...] = pieces + mm(one_hot, pos_ref[...])

    gain0, gain1, gain2 = gain_ref[0:1], gain_ref[1:2], gain_ref[2:3]
    shift0, shift1, shift2 = shift_ref[0:1], shift_ref[1:2], shift_ref[2:3]

    def at(i):
        return pl.ds(pl.multiple_of(i * step_rows, step_rows), step_rows)

    def norm0(i, carry):
        x = acc[at(i), :]
        off = x - row_mean(x)
        y = off * lax.rsqrt(row_mean(off * off) + LN_EPS) * gain0 + shift0
        normed0[at(i), :] = y
        xb[at(i), :] = y.astype(BF16)
        return carry

    lax.fori_loop(0, row_steps, norm0, 0)

    red[...] = mm(xb[...], down_ref[...]).astype(BF16)
    copies[0].wait()
    q[...] = (
        (mm(xb[...], wqkv[0]) + bias_ref[0:1] + mm(red[...], up_ref[0])).astype(BF16)
        * BF16(HEAD_DIM**-0.5)
    )
    k[...] = (mm(xb[...], wqkv[1]) + bias_ref[1:2]).astype(BF16)
    v[...] = (mm(xb[...], wqkv[2]) + bias_ref[2:3] + mm(red[...], up_ref[1])).astype(BF16)

    head_of = lax.broadcasted_iota(jnp.int32, (1, GROUP), 1) // HEAD_DIM
    in_head = [head_of == h for h in range(per_group)]
    keep = [jnp.where(m, 1.0, 0.0).astype(BF16) for m in in_head]

    def mask_block(b, c):
        hit = seg_col[b * BLOCK : (b + 1) * BLOCK] == seg_row[:, c * BLOCK : (c + 1) * BLOCK]
        return jnp.where(hit, 0.0, -1e9)

    away = {
        (b, c): mask_block(b, c)
        for b in range(blocks)
        for c in range(max(b - 1, 0), min(b + 2, blocks))
    }

    def tile_rows(t):
        lo = min(max(2 * t - 1, 0) * BLOCK, rows - min(span, rows))
        hi = min((2 * t + 3) * BLOCK, rows)
        return lo, hi

    def block_pieces(b):
        first, last = max(b - 1, 0), min(b + 1, blocks - 1)
        found = []
        for t in range(tiles):
            lo, hi = max(first, 2 * t), min(last, 2 * t + 1)
            if lo <= hi:
                found.append((t, lo, hi))
        return found

    zero_block = jnp.zeros((BLOCK, BLOCK), BF16)

    def spread(values, t, lo, hi):
        parts_ = [values] if lo == 2 * t else [zero_block, values]
        if hi == 2 * t:
            parts_.append(zero_block)
        return parts_[0] if len(parts_) == 1 else jnp.concatenate(parts_, axis=1)

    def attention(g, carry):
        lanes = pl.ds(pl.multiple_of(g * GROUP, GROUP), GROUP)
        qg, kg, vg = q[:, lanes], k[:, lanes], v[:, lanes]
        scores = []
        for t in range(tiles):
            lo, hi = tile_rows(t)
            stack = jnp.concatenate([qg[lo:hi] * keep[h] for h in range(per_group)], axis=0)
            scores.append(mm(stack, kg[t * GROUP : (t + 1) * GROUP], NT))
        out = jnp.zeros((rows, GROUP), F32)
        low = jnp.zeros((rows, GROUP), F32)
        for h in range(per_group):
            vrh = vg * keep[h] + red[...] * (1 - keep[h])
            prob_tiles = [[] for _ in range(tiles)]
            for b in range(blocks):
                found = []
                for t, lo, hi in block_pieces(b):
                    first, last = tile_rows(t)
                    top = h * (last - first) + b * BLOCK - first
                    s = scores[t][top : top + BLOCK, (lo - 2 * t) * BLOCK : (hi + 1 - 2 * t) * BLOCK]
                    far = jnp.concatenate([away[b, c] for c in range(lo, hi + 1)], axis=1)
                    found.append(s + far)
                peak = functools.reduce(
                    jnp.maximum, [jnp.max(s, axis=1, keepdims=True) for s in found]
                )
                found = [jnp.exp(s - peak) for s in found]
                total = functools.reduce(
                    jnp.add, [jnp.sum(s, axis=1, keepdims=True) for s in found]
                )
                inv = 1.0 / total
                for (t, lo, hi), s in zip(block_pieces(b), found):
                    prob_tiles[t].append(spread((s * inv).astype(BF16), t, lo, hi))
            res = [None] * blocks
            for t in range(tiles):
                first, last = tile_rows(t)
                pt = jnp.concatenate(prob_tiles[t], axis=0)
                probs[g * per_group + h, t, 0 : last - first, :] = pt
                part = mm(pt, vrh[t * GROUP : (t + 1) * GROUP])
                for i in range((last - first) // BLOCK):
                    b = first // BLOCK + i
                    piece = part[i * BLOCK : (i + 1) * BLOCK]
                    res[b] = piece if res[b] is None else res[b] + piece
            res = jnp.concatenate(res, axis=0)
            out = jnp.where(in_head[h], res, out)
            low = jnp.where(in_head[(h + 1) % per_group], res, low)
        mixed[:, lanes] = out.astype(BF16)
        pr[:, lanes] = low.astype(BF16)
        return carry

    lax.fori_loop(0, groups, attention, 0)

    copies[1].wait()
    acc[...] = mm(mixed[...], wo[...]) + bias_ref[3:4]

    def norm1(i, carry):
        x = normed0[at(i), :] + acc[at(i), :]
        off = x - row_mean(x)
        inv = lax.rsqrt(row_mean(off * off) + LN_EPS)
        xh = off * inv
        xh1[at(i), :] = xh
        stat1[at(i), :] = inv
        xb[at(i), :] = (xh * gain1 + shift1).astype(BF16)
        return carry

    lax.fori_loop(0, row_steps, norm1, 0)

    copies[2].wait()
    for t in range(parts):
        for c in range(0, hidden_part, chunk):
            at_hidden = slice(t * hidden_part + c, t * hidden_part + c + chunk)
            pre = mm(xb[...], win[t, :, c : c + chunk]) + ffb_ref[:, at_hidden]
            phi = 0.5 + 0.5 * lax.erf(pre * INV_SQRT2)
            act[:, at_hidden] = (pre * phi).astype(BF16)
            slope[:, at_hidden] = phi + pre * jnp.exp(-0.5 * pre * pre) * INV_SQRT_2PI
    copies[3].wait()
    for n in range(0, width, GROUP):
        acc[:, n : n + GROUP] = mm(act[...], wout[:, n : n + GROUP])

    head = head_ref[0:1, 0:width]
    head_bias = head_ref[0:1, width : width + 1]
    hg = head * gain2
    hg_mean = row_mean(hg)
    bias4 = bias_ref[4:5]
    base = jnp.sum(shift2 * head, axis=1, keepdims=True)

    inv_cols = []
    dot_cols = []
    for i in range(row_steps):
        part = slice(i * step_rows, (i + 1) * step_rows)
        x = xh1[part, :] * gain1 + shift1 + (acc[part, :] + bias4)
        off = x - row_mean(x)
        inv = lax.rsqrt(row_mean(off * off) + LN_EPS)
        xh = off * inv
        acc[part, :] = xh
        inv_cols.append(inv)
        dot_cols.append(jnp.sum(xh * hg, axis=1, keepdims=True))
    inv2 = jnp.concatenate(inv_cols, axis=0)
    dots = jnp.concatenate(dot_cols, axis=0)

    slots = label_ref.shape[1]
    slot = lax.broadcasted_iota(jnp.int32, (rows, slots), 1).astype(F32)
    member = jnp.where(seg_col == slot, 1.0, 0.0)
    counts = jnp.sum(member, axis=0, keepdims=True)
    sums = jnp.sum(member * (dots + base), axis=0, keepdims=True)
    most = jnp.maximum(counts, 1.0)
    error = jnp.where(counts > 0, sums / most + head_bias - label_ref[...], 0.0)
    grad_pred = 2.0 * error
    weight = jnp.sum(member * (grad_pred / most), axis=1, keepdims=True)
    loss = jnp.sum(error * error, axis=1, keepdims=True)
    weight_sum = jnp.sum(grad_pred, axis=1, keepdims=True)
    items = jnp.max(seg_row, axis=1, keepdims=True) + 1.0

    head_grad = jnp.zeros((8, width), F32)
    for i in range(row_steps):
        part = slice(i * step_rows, (i + 1) * step_rows)
        xh = acc[part, :]
        w = weight[part]
        weighted = xh * w
        for j in range(step_rows // 8):
            head_grad = head_grad + weighted[j * 8 : (j + 1) * 8]
        grad = (inv2[part] * w) * (hg - hg_mean - xh * (dots[part] * (1.0 / width)))
        acc[part, :] = grad
        xb[part, :] = grad.astype(BF16)
    head_grad = jnp.sum(head_grad, axis=0, keepdims=True) * gain2 + weight_sum * shift2

    for t in range(parts):
        for c in range(0, hidden_part, chunk):
            at_hidden = slice(t * hidden_part + c, t * hidden_part + c + chunk)
            back = mm(xb[...], wout[at_hidden, :], NT)
            act[:, at_hidden] = (back * slope[:, at_hidden]).astype(BF16)
    for n in range(0, width, GROUP):
        total = acc[:, n : n + GROUP]
        for t in range(parts):
            total = total + mm(
                act[:, t * hidden_part : (t + 1) * hidden_part], win[t, n : n + GROUP, :], NT
            )
        acc[:, n : n + GROUP] = total

    def back1(i, carry):
        g = acc[at(i), :] * gain1
        xh = xh1[at(i), :]
        grad = stat1[at(i), :] * (g - row_mean(g) - xh * row_mean(g * xh))
        xb[at(i), :] = grad.astype(BF16)
        return carry

    lax.fori_loop(0, row_steps, back1, 0)

    mixed[...] = mm(xb[...], wo[...], NT).astype(BF16)

    def attention_back(g, carry):
        lanes = pl.ds(pl.multiple_of(g * GROUP, GROUP), GROUP)
        gg, kg, vg = mixed[:, lanes], k[:, lanes], v[:, lanes]
        grads = []
        for t in range(tiles):
            lo, hi = tile_rows(t)
            stack = jnp.concatenate([gg[lo:hi] * keep[h] for h in range(per_group)], axis=0)
            grads.append(mm(stack, vg[t * GROUP : (t + 1) * GROUP], NT))
        out = jnp.zeros((rows, GROUP), F32)
        for h in range(per_group):
            score_tiles = [[] for _ in range(tiles)]
            for b in range(blocks):
                found = []
                for t, lo, hi in block_pieces(b):
                    first, last = tile_rows(t)
                    top = b * BLOCK - first
                    lane_at = slice((lo - 2 * t) * BLOCK, (hi + 1 - 2 * t) * BLOCK)
                    dp = grads[t][h * (last - first) + top : h * (last - first) + top + BLOCK, lane_at]
                    p = probs[g * per_group + h, t, top : top + BLOCK, lane_at].astype(F32)
                    found.append((p, dp))
                shared = functools.reduce(
                    jnp.add, [jnp.sum(p * dp, axis=1, keepdims=True) for p, dp in found]
                )
                for (t, lo, hi), (p, dp) in zip(block_pieces(b), found):
                    score_tiles[t].append(spread((p * (dp - shared)).astype(BF16), t, lo, hi))
            res = [None] * blocks
            for t in range(tiles):
                first, last = tile_rows(t)
                part = mm(jnp.concatenate(score_tiles[t], axis=0), kg[t * GROUP : (t + 1) * GROUP])
                for i in range((last - first) // BLOCK):
                    b = first // BLOCK + i
                    piece = part[i * BLOCK : (i + 1) * BLOCK]
                    res[b] = piece if res[b] is None else res[b] + piece
            out = jnp.where(in_head[h], jnp.concatenate(res, axis=0), out)
        query_part = mm(red[...], out.astype(BF16), TN)[0:8] * (2.0 * HEAD_DIM**-0.5)
        acc_ref[0:8, lanes] = acc_in_ref[0:8, lanes] + query_part
        cross = mm(pr[:, lanes], gg, TN)
        value_part = jnp.zeros((8, GROUP), F32)
        for h in range(per_group):
            top = ((h + 1) % per_group) * HEAD_DIM + 8
            value_part = jnp.where(in_head[h], cross[top : top + 8], value_part)
        acc_ref[8:16, lanes] = acc_in_ref[8:16, lanes] + 2.0 * value_part
        return carry

    lax.fori_loop(0, groups, attention_back, 0)

    acc_ref[16:17, :] = acc_in_ref[16:17, :] + head_grad
    lane_row = lax.broadcasted_iota(jnp.int32, (1, width), 1)
    extras = jnp.where(
        lane_row == 0,
        loss,
        jnp.where(lane_row == 1, items, jnp.where(lane_row == 2, weight_sum, 0.0)),
    )
    acc_ref[17:18, :] = acc_in_ref[17:18, :] + extras
    acc_ref[18:24, :] = jnp.zeros((6, width), F32)


def layer_call(x, seg, label, small, weights, acc_in):
    pos, gain, shift, bias, down, up, head, ffb = small
    wqkv, wo, win, wout = weights
    parts, rows, _ = x.shape
    width = pos.shape[1]
    hidden = wout.shape[0]
    heads = width // HEAD_DIM
    tiles = rows // GROUP
    vmem = pl.BlockSpec(memory_space=pltpu.VMEM)
    hbm = pl.BlockSpec(memory_space=pl.ANY)
    scratch = [
        pltpu.VMEM(wqkv.shape, BF16),
        pltpu.VMEM(wo.shape, BF16),
        pltpu.VMEM(win.shape, BF16),
        pltpu.VMEM(wout.shape, BF16),
        pltpu.VMEM((rows, width), BF16),
        pltpu.VMEM((rows, width), F32),
        pltpu.VMEM((rows, width), BF16),
        pltpu.VMEM((rows, width), BF16),
        pltpu.VMEM((rows, width), BF16),
        pltpu.VMEM((rows, GROUP), BF16),
        pltpu.VMEM((8, 128), BF16),
        pltpu.VMEM((rows, width), BF16),
        pltpu.VMEM((heads, tiles, 3 * BLOCK, GROUP), BF16),
        pltpu.VMEM((rows, width), BF16),
        pltpu.VMEM((rows, width), F32),
        pltpu.VMEM((rows, 1), F32),
        pltpu.VMEM((rows, width), F32),
        pltpu.VMEM((rows, hidden), F32),
        pltpu.VMEM((rows, hidden), BF16),
        pltpu.SemaphoreType.DMA((4,)),
    ]
    flops = 2 * rows * (width * width * 5 + 4 * width * hidden + 4 * rows * width)
    return pl.pallas_call(
        layer_kernel,
        out_shape=jax.ShapeDtypeStruct(acc_in.shape, F32),
        in_specs=[vmem] * 12 + [hbm] * 4,
        out_specs=vmem,
        scratch_shapes=scratch,
        compiler_params=pltpu.CompilerParams(vmem_limit_bytes=58 * 1024 * 1024),
        cost_estimate=pl.CostEstimate(
            flops=flops, bytes_accessed=16 * 1024 * 1024, transcendentals=3 * rows * hidden
        ),
        name="layer",
    )(x, seg, label, pos, gain, shift, bias, down, up, head, ffb, acc_in, wqkv, wo, win, wout)


def newton_schulz_orthogonal(moment):
    basis = moment / (jnp.sqrt(jnp.sum(moment * moment)) + 1e-07)
    for sweep in range(5):
        gram = jnp.dot(basis, basis.T, precision=TOP_PRECISION)
        poly = NS_B * gram + NS_C * jnp.dot(gram, gram, precision=TOP_PRECISION)
        basis = NS_A * basis + jnp.dot(poly, basis, precision=TOP_PRECISION)
    return basis


def local(
    input_token_ids,
    segments,
    labels,
    embedding,
    position_embedding_table,
    norm_gain_rows,
    norm_shift_rows,
    query_key_value_weight,
    attention_output_weight,
    attention_bias_stack,
    feedforward_in_weight,
    feedforward_bias,
    feedforward_out_weight,
    adapter_down_weight,
    adapter_up_weight,
    adapter_momentum,
    head,
    head_first_moment,
    head_second_moment,
):
    length = input_token_ids.shape[-1]
    slots = labels.shape[-1]
    width = position_embedding_table.shape[1]
    rank = adapter_up_weight.shape[1]
    ids = input_token_ids.reshape(-1, length)
    segs = segments.reshape(-1, 1, length)
    labs = labels.reshape(-1, 1, slots)
    units = ids.shape[0]
    feats = embedding.shape[0]

    win = lax.all_gather(feedforward_in_weight, "tensor", axis=0)
    wout = lax.all_gather(feedforward_out_weight, "tensor", axis=0, tiled=True)
    ffb = lax.all_gather(feedforward_bias, "tensor", axis=0, tiled=True).astype(F32)[None, :]

    all_ids = lax.all_gather(ids, "tensor", axis=0)
    parts = all_ids.shape[0]
    picked = jnp.take(embedding, all_ids.reshape(-1), axis=1).T.reshape(parts, units, length, feats)

    down = jnp.concatenate(
        [adapter_down_weight[0], adapter_down_weight[1], jnp.zeros((width, HEAD_DIM - 2 * rank), BF16)], axis=1
    )
    down = jnp.concatenate([down] * (GROUP // HEAD_DIM), axis=1)
    twice = 2.0 * adapter_up_weight.astype(BF16)
    up = jnp.stack(
        [
            jnp.pad(twice[0], ((0, GROUP - rank), (0, 0))),
            jnp.pad(twice[1], ((rank, GROUP - 2 * rank), (0, 0))),
        ]
    )
    small = (
        position_embedding_table,
        norm_gain_rows,
        norm_shift_rows,
        attention_bias_stack,
        down,
        up,
        head[None, :],
        ffb,
    )
    weights = (query_key_value_weight, attention_output_weight, win, wout)
    acc = jnp.zeros((24, width), F32)
    for u in range(units):
        x = lax.all_to_all(picked[:, u], "tensor", split_axis=0, concat_axis=0, tiled=True)
        acc = layer_call(x, segs[u], labs[u], small, weights, acc)
    acc = lax.psum(acc, ("dp", "tensor"))

    loss_total = acc[17, 0]
    item_total = acc[17, 1]
    adapter_gradient_sum = acc[0:16].reshape(2, rank, width) / item_total
    head_gradient_sum = jnp.concatenate([acc[16], acc[17, 2:3]]) / item_total
    global_gradient_norm = jnp.sqrt(
        jnp.sum(adapter_gradient_sum * adapter_gradient_sum)
        + jnp.sum(head_gradient_sum * head_gradient_sum)
    )
    scale_factor = jnp.minimum(1.0, CLIP_NORM / (global_gradient_norm + 1e-06))
    adapter_moment_next = ORTHO_MOMENTUM * adapter_momentum + scale_factor * adapter_gradient_sum
    orthogonal_update = jnp.stack(
        [
            newton_schulz_orthogonal(adapter_moment_next[0]),
            newton_schulz_orthogonal(adapter_moment_next[1]),
        ]
    )
    adapter_up_updated = adapter_up_weight - ORTHO_STEP_SIZE * orthogonal_update
    clipped = scale_factor * head_gradient_sum
    head_moment_next = BETA_ONE * head_first_moment + (1.0 - BETA_ONE) * clipped
    head_square_next = BETA_TWO * head_second_moment + (1.0 - BETA_TWO) * clipped * clipped
    first_hat = head_moment_next / (1.0 - BETA_ONE**STEP)
    second_hat = head_square_next / (1.0 - BETA_TWO**STEP)
    head_updated = head - ADAM_RATE * (first_hat / (jnp.sqrt(second_hat) + ADAM_EPS) + DECAY * head)
    return (
        loss_total,
        item_total,
        global_gradient_norm,
        adapter_moment_next,
        adapter_up_updated,
        adapter_up_updated.astype(jnp.bfloat16),
        head_moment_next,
        head_square_next,
        head_updated,
        head_updated.astype(jnp.bfloat16),
    )


def solution(mesh):
    placed = (
        P(None, ("dp", "tensor"), None),
        P(None, ("dp", "tensor"), None),
        P(None, ("dp", "tensor"), None),
        P("tensor", None),
        P(),
        P(),
        P(),
        P(),
        P(),
        P(),
        P(None, "tensor"),
        P("tensor"),
        P("tensor", None),
        P(),
        P(),
        P(),
        P(),
        P(),
        P(),
    )
    return jax.shard_map(
        local,
        mesh=mesh,
        in_specs=placed,
        out_specs=(P(), P(), P(), P(), P(), P(), P(), P(), P(), P()),
        check_vma=False,
    )
```

```python
import functools
import math

import jax
import jax.numpy as jnp
from jax import lax
from jax.experimental import pallas as pl
from jax.experimental.pallas import tpu as pltpu
from jax.sharding import PartitionSpec as P

HEAD_DIM = 64
STEP = 10
LN_EPS = 1e-05
CLIP_NORM = 0.5
ORTHO_MOMENTUM = 0.5
ORTHO_STEP_SIZE = 1.0
NS_A = 3.4445
NS_B = -4.775
NS_C = 2.0315
BETA_ONE = 0.9
BETA_TWO = 0.999
ADAM_RATE = 0.05
ADAM_EPS = 1e-08
DECAY = 0.01

F32 = jnp.float32
BF16 = jnp.bfloat16
LANES = 128
GROUP = 256
PER_GROUP = GROUP // HEAD_DIM
BLOCK = 128
SPAN = 3 * BLOCK
STEP_ROWS = 64
VOCAB_BLOCK = 2048
STREAMS = 2
UNROLL = 64
ACC_ROWS = 24
MIB = 1024 * 1024
NN = (((1,), (0,)), ((), ()))
NT = (((1,), (1,)), ((), ()))
TN = (((0,), (0,)), ((), ()))
INV_SQRT2 = 1.0 / math.sqrt(2.0)
INV_SQRT_2PI = 1.0 / math.sqrt(2.0 * math.pi)

VMEM = pl.BlockSpec(memory_space=pltpu.VMEM)
SMEM = pl.BlockSpec(memory_space=pltpu.SMEM)
ANY = pl.BlockSpec(memory_space=pl.ANY)


def mm(left, right, dims=NN):
    return lax.dot_general(left, right, dims, preferred_element_type=F32)


def row_mean(rows):
    return jnp.mean(rows, axis=-1, keepdims=True)


def add_all(terms):
    return functools.reduce(jnp.add, terms)


def at(i):
    return pl.ds(pl.multiple_of(i * STEP_ROWS, STEP_ROWS), STEP_ROWS)


def embed_kernel(*refs, parts, units, blocks):
    ids = refs[:parts]
    tables = refs[parts : parts + STREAMS]
    outs = refs[parts + STREAMS : parts + STREAMS + parts * units]
    scratch = refs[parts + STREAMS + parts * units :]
    feats, cols = tables[0].shape
    lanes = [(lo, min(lo + LANES, feats)) for lo in range(0, feats, LANES)]
    turned = scratch[: len(lanes)]
    picked = scratch[len(lanes) : 2 * len(lanes)]
    stage, sems = scratch[2 * len(lanes) :]
    step = pl.program_id(0)

    for s, table in enumerate(tables):
        base = jnp.minimum(step * STREAMS + s, blocks - 1) * cols
        for c in range(0, cols, GROUP):
            rows_at = pl.ds(pl.multiple_of(base + c, GROUP), GROUP)
            for (lo, hi), turn in zip(lanes, turned):
                turn[rows_at, :] = table[lo:hi, c : c + GROUP].T.astype(F32)

    @pl.when(step == pl.num_programs(0) - 1)
    def _():
        length = stage.shape[1]
        copies = []
        for p, out in enumerate(outs):
            u, r = p // parts, p % parts
            slot = p % 2

            def rows(i, carry, u=u, r=r):
                top = pl.multiple_of(i * UNROLL, UNROLL)
                for j in range(UNROLL):
                    token = ids[r][u, top + j]
                    for turn, pick in zip(turned, picked):
                        pick[pl.ds(top + j, 1), :] = turn[pl.ds(token, 1), :]
                return carry

            lax.fori_loop(0, length // UNROLL, rows, 0)
            if p >= 2:
                copies[p - 2].wait()
            for (lo, hi), pick in zip(lanes, picked):
                stage[slot, :, lo:hi] = pick[...].astype(BF16)
            copies.append(pltpu.make_async_copy(stage.at[slot], out, sems.at[slot]))
            copies[p].start()
        for copy in copies[-2:]:
            copy.wait()


def embed_call(ids, table):
    parts = len(ids)
    units, length = ids[0].shape
    feats, vocab = table.shape
    blocks = pl.cdiv(vocab, VOCAB_BLOCK)
    widths = [min(LANES, feats - lo) for lo in range(0, feats, LANES)]
    scratch = [pltpu.VMEM((blocks * VOCAB_BLOCK, w), F32) for w in widths]
    scratch += [pltpu.VMEM((length, w), F32) for w in widths]
    scratch += [pltpu.VMEM((2, length, feats), BF16), pltpu.SemaphoreType.DMA((2,))]
    streams = [
        pl.BlockSpec(
            (feats, VOCAB_BLOCK),
            functools.partial(lambda s, i: (0, jnp.minimum(i * STREAMS + s, blocks - 1)), s),
        )
        for s in range(STREAMS)
    ]
    return pl.pallas_call(
        functools.partial(embed_kernel, parts=parts, units=units, blocks=blocks),
        grid=(pl.cdiv(blocks, STREAMS),),
        in_specs=[SMEM] * parts + streams,
        out_specs=[ANY] * (parts * units),
        out_shape=[jax.ShapeDtypeStruct((length, feats), BF16)] * (parts * units),
        scratch_shapes=scratch,
        compiler_params=pltpu.CompilerParams(vmem_limit_bytes=62 * MIB),
        name="embed",
    )(*ids, *[table] * STREAMS)


def tile_rows(t, rows):
    lo = min(max(2 * t - 1, 0) * BLOCK, rows - min(SPAN, rows))
    return lo, min((2 * t + 3) * BLOCK, rows)


def block_pieces(b, blocks):
    first, last = max(b - 1, 0), min(b + 1, blocks - 1)
    found = []
    for t in range(blocks * BLOCK // GROUP):
        lo, hi = max(first, 2 * t), min(last, 2 * t + 1)
        if lo <= hi:
            found.append((t, lo, hi))
    return found


def spread(values, t, lo, hi):
    zero_block = jnp.zeros((BLOCK, BLOCK), BF16)
    parts = [values] if lo == 2 * t else [zero_block, values]
    if hi == 2 * t:
        parts.append(zero_block)
    return parts[0] if len(parts) == 1 else jnp.concatenate(parts, axis=1)


def head_masks():
    head_of = lax.broadcasted_iota(jnp.int32, (1, GROUP), 1) // HEAD_DIM
    in_head = [head_of == h for h in range(PER_GROUP)]
    return in_head, [jnp.where(m, 1.0, 0.0).astype(BF16) for m in in_head]


def segment_columns(seg_row):
    rows = seg_row.shape[1]
    lane = lax.broadcasted_iota(jnp.int32, (rows, rows), 1)
    sub = lax.broadcasted_iota(jnp.int32, (rows, rows), 0)
    return lane, sub, jnp.sum(jnp.where(lane == sub, seg_row, 0.0), axis=1, keepdims=True)


def tile_product(tiles, right):
    rows = right.shape[0]
    res = [None] * (rows // BLOCK)
    for t, left in enumerate(tiles):
        part = mm(left, right[t * GROUP : (t + 1) * GROUP])
        first = tile_rows(t, rows)[0] // BLOCK
        for i in range(left.shape[0] // BLOCK):
            piece = part[i * BLOCK : (i + 1) * BLOCK]
            res[first + i] = piece if res[first + i] is None else res[first + i] + piece
    return jnp.concatenate(res, axis=0)


def stacked_scores(left, right, keep):
    rows = left.shape[0]
    found = []
    for t in range(rows // GROUP):
        lo, hi = tile_rows(t, rows)
        stack = jnp.concatenate([left[lo:hi] * keep[h] for h in range(PER_GROUP)], axis=0)
        found.append(mm(stack, right[t * GROUP : (t + 1) * GROUP], NT))
    return found


def attend_kernel(*refs, parts, unit, fresh):
    pieces = refs[:parts]
    seg_ref, pos_ref, gain_ref, shift_ref, bias_ref, down_ref, up_ref, wqkv_hbm, wo_hbm = refs[
        parts : parts + 9
    ]
    refs = refs[parts + 9 + (0 if fresh else 6) :]
    outs, (x4, wqkv, wo, start, xb, normed0, q, k, v, red, pr, probs, mixed, sems) = refs[:6], refs[6:]
    rows, width = normed0.shape
    groups = width // GROUP
    blocks = rows // BLOCK
    tiles = rows // GROUP
    row_steps = rows // STEP_ROWS
    me = lax.axis_index("tensor")

    in_copies = [
        pltpu.make_async_copy(piece, x4.at[jnp.bitwise_xor(me, r)], sems.at[r])
        for r, piece in enumerate(pieces)
    ]
    w_copies = [
        pltpu.make_async_copy(wqkv_hbm, wqkv, sems.at[parts]),
        pltpu.make_async_copy(wo_hbm, wo, sems.at[parts + 1]),
    ]
    out_copies = [
        pltpu.make_async_copy(ref, out.at[unit], sems.at[parts + 2 + i])
        for i, (ref, out) in enumerate(zip((start, k, v, red, pr, probs), outs))
    ]
    for copy in in_copies + w_copies:
        copy.start()

    seg_row = seg_ref[...].astype(F32)
    lane, sub, seg_col = segment_columns(seg_row)
    same = seg_col == seg_row
    place = jnp.sum(jnp.where(same & (lane < sub), 1.0, 0.0), axis=1, keepdims=True)
    one_hot = jnp.where(lane == place.astype(jnp.int32), 1.0, 0.0).astype(BF16)
    start[...] = mm(one_hot, pos_ref[...])
    for copy in in_copies:
        copy.wait()
    start[...] += jnp.concatenate([x4[t] for t in range(parts)], axis=1).astype(F32)

    gain0, shift0 = gain_ref[0:1], shift_ref[0:1]

    def norm0(i, carry):
        x = start[at(i), :]
        off = x - row_mean(x)
        y = off * lax.rsqrt(row_mean(off * off) + LN_EPS) * gain0 + shift0
        normed0[at(i), :] = y
        xb[at(i), :] = y.astype(BF16)
        return carry

    lax.fori_loop(0, row_steps, norm0, 0)

    red[...] = mm(xb[...], down_ref[...]).astype(BF16)
    out_copies[3].start()
    w_copies[0].wait()
    q[...] = (mm(xb[...], wqkv[0]) + bias_ref[0:1] + mm(red[...], up_ref[0])).astype(BF16) * BF16(
        HEAD_DIM**-0.5
    )
    k[...] = (mm(xb[...], wqkv[1]) + bias_ref[1:2]).astype(BF16)
    out_copies[1].start()
    v[...] = (mm(xb[...], wqkv[2]) + bias_ref[2:3] + mm(red[...], up_ref[1])).astype(BF16)
    out_copies[2].start()

    in_head, keep = head_masks()

    def far(b, c):
        hit = seg_col[b * BLOCK : (b + 1) * BLOCK] == seg_row[:, c * BLOCK : (c + 1) * BLOCK]
        return jnp.where(hit, 0.0, -1e9)

    away = {
        (b, c): far(b, c) for b in range(blocks) for c in range(max(b - 1, 0), min(b + 2, blocks))
    }

    def attention(g, carry):
        lanes = pl.ds(pl.multiple_of(g * GROUP, GROUP), GROUP)
        vg = v[:, lanes]
        scores = stacked_scores(q[:, lanes], k[:, lanes], keep)
        out = jnp.zeros((rows, GROUP), F32)
        low = jnp.zeros((rows, GROUP), F32)
        for h in range(PER_GROUP):
            vrh = vg * keep[h] + red[...] * (1 - keep[h])
            prob_tiles = [[] for _ in range(tiles)]
            for b in range(blocks):
                found = []
                for t, lo, hi in block_pieces(b, blocks):
                    first, last = tile_rows(t, rows)
                    top = h * (last - first) + b * BLOCK - first
                    s = scores[t][top : top + BLOCK, (lo - 2 * t) * BLOCK : (hi + 1 - 2 * t) * BLOCK]
                    found.append(
                        s + jnp.concatenate([away[b, c] for c in range(lo, hi + 1)], axis=1)
                    )
                peak = functools.reduce(
                    jnp.maximum, [jnp.max(s, axis=1, keepdims=True) for s in found]
                )
                found = [jnp.exp(s - peak) for s in found]
                inv = 1.0 / add_all([jnp.sum(s, axis=1, keepdims=True) for s in found])
                for (t, lo, hi), s in zip(block_pieces(b, blocks), found):
                    prob_tiles[t].append(spread((s * inv).astype(BF16), t, lo, hi))
            prob_tiles = [jnp.concatenate(tile, axis=0) for tile in prob_tiles]
            for t, tile in enumerate(prob_tiles):
                probs[g * PER_GROUP + h, t, 0 : tile.shape[0], :] = tile
            res = tile_product(prob_tiles, vrh)
            out = jnp.where(in_head[h], res, out)
            low = jnp.where(in_head[(h + 1) % PER_GROUP], res, low)
        mixed[:, lanes] = out.astype(BF16)
        pr[:, lanes] = low.astype(BF16)
        return carry

    lax.fori_loop(0, groups, attention, 0)
    out_copies[4].start()
    out_copies[5].start()
    w_copies[1].wait()
    start[...] = normed0[...] + (mm(mixed[...], wo[...]) + bias_ref[3:4])
    out_copies[0].start()
    for copy in out_copies:
        copy.wait()


def attend_call(pieces, seg, small, wqkv, wo, kept, unit, units):
    pos, gain, shift, bias, down, up = small
    parts = len(pieces)
    rows, feats = pieces[0].shape
    width = pos.shape[1]
    heads = width // HEAD_DIM
    tiles = rows // GROUP
    forms = [
        ((rows, width), F32),
        ((rows, width), BF16),
        ((rows, width), BF16),
        ((rows, GROUP), BF16),
        ((rows, width), BF16),
        ((heads, tiles, SPAN, GROUP), BF16),
    ]
    fresh = kept is None
    scratch = [
        pltpu.VMEM((parts, rows, feats), BF16),
        pltpu.VMEM(wqkv.shape, BF16),
        pltpu.VMEM(wo.shape, BF16),
        pltpu.VMEM((rows, width), F32),
        pltpu.VMEM((rows, width), BF16),
        pltpu.VMEM((rows, width), F32),
        pltpu.VMEM((rows, width), BF16),
        pltpu.VMEM((rows, width), BF16),
        pltpu.VMEM((rows, width), BF16),
        pltpu.VMEM((rows, GROUP), BF16),
        pltpu.VMEM((rows, width), BF16),
        pltpu.VMEM((heads, tiles, SPAN, GROUP), BF16),
        pltpu.VMEM((rows, width), BF16),
        pltpu.SemaphoreType.DMA((parts + 8,)),
    ]
    args = [*pieces, seg, pos, gain, shift, bias, down, up, wqkv, wo]
    aliases = {} if fresh else {len(args) + i: i for i in range(len(forms))}
    return pl.pallas_call(
        functools.partial(attend_kernel, parts=parts, unit=unit, fresh=fresh),
        out_shape=[jax.ShapeDtypeStruct((units, *shape), kind) for shape, kind in forms],
        in_specs=[ANY] * parts + [VMEM] * 7 + [ANY] * 2 + ([] if fresh else [ANY] * len(forms)),
        out_specs=[ANY] * len(forms),
        input_output_aliases=aliases,
        scratch_shapes=scratch,
        compiler_params=pltpu.CompilerParams(vmem_limit_bytes=58 * MIB),
        cost_estimate=pl.CostEstimate(
            flops=2 * rows * width * (4 * width + 2 * rows),
            bytes_accessed=16 * MIB,
            transcendentals=rows * rows * heads,
        ),
        name="attend",
    )(*args, *([] if fresh else kept))


def finish_kernel(*refs, places, parts):
    (seg_ref, label_ref, gain_ref, shift_ref, bias_ref, head_ref, ffb_ref, wo_hbm, *refs) = refs
    weight_pieces, refs = refs[: 2 * len(places)], refs[2 * len(places) :]
    kept, refs = refs[:6], refs[6:]
    acc_ref, refs = refs[0], refs[1:]
    bufs, refs = refs[:6], refs[6:]
    wo, win, wout, xb, mixed, xh1, stat1, acc, slope, act, sems, wsems = refs
    resid2buf, k2, v2, red2, pr2, probs2 = bufs
    units = kept[0].shape[0]
    rows, width = xh1.shape
    hidden_part = win.shape[2]
    chunk = GROUP if hidden_part % GROUP == 0 else hidden_part
    groups = width // GROUP
    blocks = rows // BLOCK
    tiles = rows // GROUP
    row_steps = rows // STEP_ROWS
    half = lax.rem(lax.axis_index("dp"), 2)

    def weight_copies():
        made = []
        for i, (ref, (r, mine)) in enumerate(zip(weight_pieces[: len(places)], places)):
            if mine is None:
                dst = win.at[r]
            else:
                n = width // 2
                top = pl.multiple_of((half if mine else 1 - half) * n, 16)
                dst = win.at[r, pl.ds(top, n), :]
            made.append(pltpu.make_async_copy(ref, dst, wsems.at[i]))
        for i, (ref, (r, mine)) in enumerate(zip(weight_pieces[len(places) :], places)):
            if mine is None:
                dst = wout.at[r]
            else:
                n = hidden_part // 2
                top = pl.multiple_of((half if mine else 1 - half) * n, 16)
                dst = wout.at[r, pl.ds(top, n), :]
            made.append(pltpu.make_async_copy(ref, dst, wsems.at[len(places) + i]))
        made.append(pltpu.make_async_copy(wo_hbm, wo, wsems.at[2 * len(places)]))
        return made

    def state_copies(u, slot):
        return [
            pltpu.make_async_copy(src.at[u], buf.at[slot], sems.at[slot, i])
            for i, (src, buf) in enumerate(zip(kept, bufs))
        ]

    for copy in state_copies(0, 0)[:1] + weight_copies() + state_copies(0, 0)[1:]:
        copy.start()

    gain1, gain2 = gain_ref[1:2], gain_ref[2:3]
    shift1, shift2 = shift_ref[1:2], shift_ref[2:3]
    head = head_ref[0:1, 0:width]
    head_bias = head_ref[0:1, width : width + 1]
    hg = head * gain2
    hg_mean = row_mean(hg)
    bias4 = bias_ref[4:5]
    base = jnp.sum(shift2 * head, axis=1, keepdims=True)
    in_head, keep = head_masks()
    acc_ref[...] = jnp.zeros(acc_ref.shape, F32)

    def unit(u, carry):
        slot = lax.rem(u, 2)
        now = state_copies(u, slot)

        @pl.when(u + 1 < units)
        def _():
            for copy in state_copies(u + 1, 1 - slot):
                copy.start()

        now[0].wait()

        def norm1(i, c):
            x = resid2buf[slot, at(i), :]
            off = x - row_mean(x)
            inv = lax.rsqrt(row_mean(off * off) + LN_EPS)
            xh = off * inv
            xh1[at(i), :] = xh
            stat1[at(i), :] = inv
            xb[at(i), :] = (xh * gain1 + shift1).astype(BF16)
            return c

        lax.fori_loop(0, row_steps, norm1, 0)

        @pl.when(u == 0)
        def _():
            for copy in weight_copies():
                copy.wait()

        for r in range(parts):
            for c in range(0, hidden_part, chunk):
                hid = slice(r * hidden_part + c, r * hidden_part + c + chunk)
                pre = mm(xb[...], win[r, :, c : c + chunk]) + ffb_ref[:, hid]
                phi = 0.5 + 0.5 * lax.erf(pre * INV_SQRT2)
                act[:, hid] = (pre * phi).astype(BF16)
                slope[:, hid] = phi + pre * jnp.exp(-0.5 * pre * pre) * INV_SQRT_2PI
        for n in range(0, width, GROUP):
            acc[:, n : n + GROUP] = add_all(
                [
                    mm(act[:, r * hidden_part : (r + 1) * hidden_part], wout[r, :, n : n + GROUP])
                    for r in range(parts)
                ]
            )

        inv_cols = []
        dot_cols = []
        for i in range(row_steps):
            part = slice(i * STEP_ROWS, (i + 1) * STEP_ROWS)
            x = xh1[part, :] * gain1 + shift1 + (acc[part, :] + bias4)
            off = x - row_mean(x)
            inv = lax.rsqrt(row_mean(off * off) + LN_EPS)
            xh = off * inv
            acc[part, :] = xh
            inv_cols.append(inv)
            dot_cols.append(jnp.sum(xh * hg, axis=1, keepdims=True))
        inv2 = jnp.concatenate(inv_cols, axis=0)
        dots = jnp.concatenate(dot_cols, axis=0)

        seg_row = seg_ref[u].astype(F32)
        seg_col = segment_columns(seg_row)[2]
        label = label_ref[u]
        slots = label.shape[1]
        slot_no = lax.broadcasted_iota(jnp.int32, (rows, slots), 1).astype(F32)
        member = jnp.where(seg_col == slot_no, 1.0, 0.0)
        counts = jnp.sum(member, axis=0, keepdims=True)
        sums = jnp.sum(member * (dots + base), axis=0, keepdims=True)
        most = jnp.maximum(counts, 1.0)
        error = jnp.where(counts > 0, sums / most + head_bias - label, 0.0)
        grad_pred = 2.0 * error
        weight = jnp.sum(member * (grad_pred / most), axis=1, keepdims=True)
        loss = jnp.sum(error * error, axis=1, keepdims=True)
        weight_sum = jnp.sum(grad_pred, axis=1, keepdims=True)
        items = jnp.max(seg_row, axis=1, keepdims=True) + 1.0

        head_grad = jnp.zeros((8, width), F32)
        for i in range(row_steps):
            part = slice(i * STEP_ROWS, (i + 1) * STEP_ROWS)
            xh = acc[part, :]
            w = weight[part]
            weighted = xh * w
            for j in range(STEP_ROWS // 8):
                head_grad = head_grad + weighted[j * 8 : (j + 1) * 8]
            grad = (inv2[part] * w) * (hg - hg_mean - xh * (dots[part] * (1.0 / width)))
            acc[part, :] = grad
            xb[part, :] = grad.astype(BF16)
        head_grad = jnp.sum(head_grad, axis=0, keepdims=True) * gain2 + weight_sum * shift2
        acc_ref[16:17, :] += head_grad
        lane_row = lax.broadcasted_iota(jnp.int32, (1, width), 1)
        acc_ref[17:18, :] += jnp.where(
            lane_row == 0,
            loss,
            jnp.where(lane_row == 1, items, jnp.where(lane_row == 2, weight_sum, 0.0)),
        )

        for r in range(parts):
            for c in range(0, hidden_part, chunk):
                hid = slice(r * hidden_part + c, r * hidden_part + c + chunk)
                back = mm(xb[...], wout[r, c : c + chunk, :], NT)
                act[:, hid] = (back * slope[:, hid]).astype(BF16)
        for n in range(0, width, GROUP):
            acc[:, n : n + GROUP] = add_all(
                [acc[:, n : n + GROUP]]
                + [
                    mm(
                        act[:, r * hidden_part : (r + 1) * hidden_part],
                        win[r, n : n + GROUP, :],
                        NT,
                    )
                    for r in range(parts)
                ]
            )

        def back1(i, c):
            g = acc[at(i), :] * gain1
            xh = xh1[at(i), :]
            grad = stat1[at(i), :] * (g - row_mean(g) - xh * row_mean(g * xh))
            xb[at(i), :] = grad.astype(BF16)
            return c

        lax.fori_loop(0, row_steps, back1, 0)

        mixed[...] = mm(xb[...], wo[...], NT).astype(BF16)
        for copy in now[1:]:
            copy.wait()

        def attention_back(g, c):
            lanes = pl.ds(pl.multiple_of(g * GROUP, GROUP), GROUP)
            gg, kg = mixed[:, lanes], k2[slot, :, lanes]
            grads = stacked_scores(gg, v2[slot, :, lanes], keep)
            out = jnp.zeros((rows, GROUP), F32)
            for h in range(PER_GROUP):
                score_tiles = [[] for _ in range(tiles)]
                for b in range(blocks):
                    found = []
                    for t, lo, hi in block_pieces(b, blocks):
                        first, last = tile_rows(t, rows)
                        top = b * BLOCK - first
                        lane_at = slice((lo - 2 * t) * BLOCK, (hi + 1 - 2 * t) * BLOCK)
                        here = h * (last - first) + top
                        dp = grads[t][here : here + BLOCK, lane_at]
                        p = probs2[slot, g * PER_GROUP + h, t, top : top + BLOCK, lane_at]
                        found.append((p.astype(F32), dp))
                    shared = add_all([jnp.sum(p * dp, axis=1, keepdims=True) for p, dp in found])
                    for (t, lo, hi), (p, dp) in zip(block_pieces(b, blocks), found):
                        score_tiles[t].append(
                            spread((p * (dp - shared)).astype(BF16), t, lo, hi)
                        )
                res = tile_product([jnp.concatenate(tile, axis=0) for tile in score_tiles], kg)
                out = jnp.where(in_head[h], res, out)
            query_part = mm(red2[slot], out.astype(BF16), TN)[0:8]
            acc_ref[0:8, lanes] += query_part * (2.0 * HEAD_DIM**-0.5)
            cross = mm(pr2[slot, :, lanes], gg, TN)
            value_part = jnp.zeros((8, GROUP), F32)
            for h in range(PER_GROUP):
                top = ((h + 1) % PER_GROUP) * HEAD_DIM + 8
                value_part = jnp.where(in_head[h], cross[top : top + 8], value_part)
            acc_ref[8:16, lanes] += 2.0 * value_part
            return c

        lax.fori_loop(0, groups, attention_back, 0)
        return carry

    lax.fori_loop(0, units, unit, 0)


def finish_call(segs, labels, small, wo, weight_in, weight_out, places, kept, parts):
    gain, shift, bias, head, ffb = small
    units, rows, width = kept[0].shape
    hidden_part = weight_in[0].shape[1]
    hidden = hidden_part * parts
    scratch = [pltpu.VMEM((2, *a.shape[1:]), a.dtype) for a in kept]
    scratch += [
        pltpu.VMEM(wo.shape, BF16),
        pltpu.VMEM((parts, width, hidden_part), BF16),
        pltpu.VMEM((parts, hidden_part, width), BF16),
        pltpu.VMEM((rows, width), BF16),
        pltpu.VMEM((rows, width), BF16),
        pltpu.VMEM((rows, width), F32),
        pltpu.VMEM((rows, 1), F32),
        pltpu.VMEM((rows, width), F32),
        pltpu.VMEM((rows, hidden), F32),
        pltpu.VMEM((rows, hidden), BF16),
        pltpu.SemaphoreType.DMA((2, len(kept))),
        pltpu.SemaphoreType.DMA((2 * len(places) + 1,)),
    ]
    return pl.pallas_call(
        functools.partial(finish_kernel, places=places, parts=parts),
        out_shape=jax.ShapeDtypeStruct((ACC_ROWS, width), F32),
        in_specs=[VMEM] * 7 + [ANY] * (1 + 2 * len(places) + len(kept)),
        out_specs=VMEM,
        scratch_shapes=scratch,
        compiler_params=pltpu.CompilerParams(vmem_limit_bytes=62 * MIB),
        cost_estimate=pl.CostEstimate(
            flops=units * 2 * rows * width * (4 * hidden + width + 2 * rows),
            bytes_accessed=48 * MIB,
            transcendentals=2 * units * rows * hidden,
        ),
        name="finish",
    )(segs, labels, gain, shift, bias, head, ffb, wo, *weight_in, *weight_out, *kept)


def update_kernel(
    acc_ref,
    other_ref,
    up_ref,
    momentum_ref,
    head_ref,
    first_ref,
    second_ref,
    loss_ref,
    items_ref,
    norm_ref,
    moment_out,
    up_out,
    low_out,
    first_out,
    second_out,
    head_out,
    head_low_out,
):
    total = acc_ref[...] + other_ref[...]
    width = total.shape[1]
    rank = up_ref.shape[0] // 2
    items = total[17:18, 1:2]
    loss_ref[...] = total[17:18, 0:1]
    items_ref[...] = items
    adapter = total[0:16] / items
    head_grad = jnp.concatenate([total[16:17], total[17:18, 2:3]], axis=1) / items
    norm = jnp.sqrt(jnp.sum(adapter * adapter) + jnp.sum(head_grad * head_grad))
    norm_ref[...] = jnp.full((1, 1), norm, F32)
    factor = jnp.minimum(1.0, CLIP_NORM / (norm_ref[...] + 1e-06))
    moment = ORTHO_MOMENTUM * momentum_ref[...] + factor * adapter
    moment_out[...] = moment

    def dot(left, right, dims=NN):
        return lax.dot_general(
            left, right, dims, preferred_element_type=F32, precision=lax.Precision.HIGHEST
        )

    basis = []
    for i in range(2):
        part = moment[i * rank : (i + 1) * rank]
        size = jnp.sqrt(jnp.sum(jnp.sum(part * part, axis=1, keepdims=True), axis=0, keepdims=True))
        basis.append(part / (size + 1e-07))
    for sweep in range(5):
        gram = [dot(x, x, NT) for x in basis]
        poly = [NS_B * g + NS_C * dot(g, g) for g in gram]
        basis = [NS_A * x + dot(p, x) for x, p in zip(basis, poly)]
    up = up_ref[...] - ORTHO_STEP_SIZE * jnp.concatenate(basis, axis=0)
    up_out[...] = up
    low_out[...] = up.astype(BF16)

    clipped = factor * head_grad
    first = BETA_ONE * first_ref[...] + (1.0 - BETA_ONE) * clipped
    second = BETA_TWO * second_ref[...] + (1.0 - BETA_TWO) * clipped * clipped
    first_hat = first / (1.0 - BETA_ONE**STEP)
    second_hat = second / (1.0 - BETA_TWO**STEP)
    head = head_ref[...]
    new_head = head - ADAM_RATE * (first_hat / (jnp.sqrt(second_hat) + ADAM_EPS) + DECAY * head)
    first_out[...] = first
    second_out[...] = second
    head_out[...] = new_head
    head_low_out[...] = new_head.astype(BF16)


def update_call(acc, other, up, momentum, head, first, second):
    one = jax.ShapeDtypeStruct((1, 1), F32)
    flat = jax.ShapeDtypeStruct(up.shape, F32)
    row = jax.ShapeDtypeStruct(head.shape, F32)
    return pl.pallas_call(
        update_kernel,
        out_shape=[
            one,
            one,
            one,
            flat,
            flat,
            jax.ShapeDtypeStruct(up.shape, BF16),
            row,
            row,
            row,
            jax.ShapeDtypeStruct(head.shape, BF16),
        ],
        in_specs=[VMEM] * 7,
        out_specs=[VMEM] * 10,
        name="update",
    )(acc, other, up, momentum, head, first, second)


def swap(value, axis, bit):
    size = lax.axis_size(axis)
    return lax.ppermute(value, axis, [(i, i ^ bit) for i in range(size)])


def gather_weights(own_in, own_out):
    parts = lax.axis_size("tensor")
    half = lax.rem(lax.axis_index("dp"), 2)

    def cut(w):
        n = w.shape[0] // 2
        return lax.dynamic_slice_in_dim(w, half * n, n, 0)

    found = {}
    for name, own in (("in", own_in), ("out", own_out)):
        mine = {0: cut(own)}
        bit = parts // 2
        while bit > 1:
            for r in list(mine):
                mine[r ^ bit] = swap(mine[r], "tensor", bit)
            bit //= 2
        del mine[0]
        full = [(own, 0, None), (swap(own, "tensor", 1), 1, None)]
        other = {r: swap(a, "dp", 1) for r, a in mine.items()}
        for r in mine:
            full += [(mine[r], r, True), (other[r], r, False)]
            full += [(swap(mine[r], "tensor", 1), r ^ 1, True)]
            full += [(swap(other[r], "tensor", 1), r ^ 1, False)]
        found[name] = full
    places = tuple((r, mine) for _, r, mine in found["in"])
    return [a for a, _, _ in found["in"]], [a for a, _, _ in found["out"]], places


def local(
    input_token_ids,
    segments,
    labels,
    embedding,
    position_embedding_table,
    norm_gain_rows,
    norm_shift_rows,
    query_key_value_weight,
    attention_output_weight,
    attention_bias_stack,
    feedforward_in_weight,
    feedforward_bias,
    feedforward_out_weight,
    adapter_down_weight,
    adapter_up_weight,
    adapter_momentum,
    head,
    head_first_moment,
    head_second_moment,
):
    length = input_token_ids.shape[-1]
    slots = labels.shape[-1]
    width = position_embedding_table.shape[1]
    rank = adapter_up_weight.shape[1]
    parts = lax.axis_size("tensor")
    ids = input_token_ids.reshape(-1, length)
    segs = segments.reshape(-1, 1, length)
    labs = labels.reshape(-1, 1, slots)
    units = ids.shape[0]

    all_ids = [ids] + [swap(ids, "tensor", r) for r in range(1, parts)]
    ffb = feedforward_bias[None, :].astype(F32)
    ffb = jnp.concatenate([ffb] + [swap(ffb, "tensor", r) for r in range(1, parts)], axis=1)
    weight_in, weight_out, places = gather_weights(feedforward_in_weight, feedforward_out_weight)

    down = jnp.concatenate(
        [
            adapter_down_weight[0],
            adapter_down_weight[1],
            jnp.zeros((width, HEAD_DIM - 2 * rank), BF16),
        ],
        axis=1,
    )
    down = jnp.concatenate([down] * PER_GROUP, axis=1)
    twice = 2.0 * adapter_up_weight.astype(BF16)
    up = jnp.stack(
        [
            jnp.pad(twice[0], ((0, GROUP - rank), (0, 0))),
            jnp.pad(twice[1], ((rank, GROUP - 2 * rank), (0, 0))),
        ]
    )
    picked = embed_call(all_ids, embedding)
    picked = [picked[u * parts : (u + 1) * parts] for u in range(units)]

    small = (
        position_embedding_table,
        norm_gain_rows,
        norm_shift_rows,
        attention_bias_stack,
        down,
        up,
    )
    kept = None
    moved = None
    for u in range(units):
        sends = picked[u][1:]
        if moved is not None:
            sends = lax.optimization_barrier((sends, moved))[0]
        moved = [swap(a, "tensor", r + 1) for r, a in enumerate(sends)]
        kept = attend_call(
            [picked[u][0], *moved],
            segs[u],
            small,
            query_key_value_weight,
            attention_output_weight,
            kept,
            u,
            units,
        )

    acc = finish_call(
        segs,
        labs,
        (norm_gain_rows, norm_shift_rows, attention_bias_stack, head[None, :], ffb),
        attention_output_weight,
        weight_in,
        weight_out,
        places,
        kept,
        parts,
    )
    steps = []
    for axis in ("tensor", "dp"):
        bit = 1
        while bit < lax.axis_size(axis):
            steps.append((axis, bit))
            bit *= 2
    for axis, bit in steps[:-1]:
        acc = acc + swap(acc, axis, bit)
    other = swap(acc, *steps[-1])

    flat = (2 * rank, width)
    outs = update_call(
        acc,
        other,
        adapter_up_weight.reshape(flat),
        adapter_momentum.reshape(flat),
        head[None, :],
        head_first_moment[None, :],
        head_second_moment[None, :],
    )
    loss, items, norm, moment, new_up, low, first, second, new_head, head_low = outs
    shape = adapter_up_weight.shape
    return (
        loss[0, 0],
        items[0, 0],
        norm[0, 0],
        moment.reshape(shape),
        new_up.reshape(shape),
        low.reshape(shape),
        first[0],
        second[0],
        new_head[0],
        head_low[0],
    )


def solution(mesh):
    rows = P(None, ("dp", "tensor"), None)
    placed = (
        (rows, rows, rows, P("tensor", None))
        + (P(),) * 6
        + (P(None, "tensor"), P("tensor"), P("tensor", None))
        + (P(),) * 6
    )
    return jax.shard_map(
        local, mesh=mesh, in_specs=placed, out_specs=(P(),) * 10, check_vma=False
    )
```

```python
import functools
import math

import jax
import jax.numpy as jnp
from jax import lax
from jax.experimental import pallas as pl
from jax.experimental.pallas import tpu as pltpu
from jax.sharding import PartitionSpec as P

HEAD_DIM = 64
STEP = 10
LN_EPS = 1e-05
CLIP_NORM = 0.5
ORTHO_MOMENTUM = 0.5
ORTHO_STEP_SIZE = 1.0
NS_A = 3.4445
NS_B = -4.775
NS_C = 2.0315
BETA_ONE = 0.9
BETA_TWO = 0.999
ADAM_RATE = 0.05
ADAM_EPS = 1e-08
DECAY = 0.01

F32 = jnp.float32
BF16 = jnp.bfloat16
LANES = 128
GROUP = 256
PER_GROUP = GROUP // HEAD_DIM
BLOCK = 128
SPAN = 3 * BLOCK
STEP_ROWS = 64
VOCAB_BLOCK = 2048
STREAMS = 2
UNROLL = 64
ACC_ROWS = 24
MIB = 1024 * 1024
NN = (((1,), (0,)), ((), ()))
NT = (((1,), (1,)), ((), ()))
TN = (((0,), (0,)), ((), ()))
INV_SQRT2 = 1.0 / math.sqrt(2.0)
INV_SQRT_2PI = 1.0 / math.sqrt(2.0 * math.pi)

VMEM = pl.BlockSpec(memory_space=pltpu.VMEM)
SMEM = pl.BlockSpec(memory_space=pltpu.SMEM)
ANY = pl.BlockSpec(memory_space=pl.ANY)


def mm(left, right, dims=NN):
    return lax.dot_general(left, right, dims, preferred_element_type=F32)


def row_mean(rows):
    return jnp.mean(rows, axis=-1, keepdims=True)


def add_all(terms):
    return functools.reduce(jnp.add, terms)


def at(i):
    return pl.ds(pl.multiple_of(i * STEP_ROWS, STEP_ROWS), STEP_ROWS)


def embed_kernel(*refs, parts, units, blocks):
    ids = refs[:parts]
    tables = refs[parts : parts + STREAMS]
    outs = refs[parts + STREAMS : parts + STREAMS + parts * units]
    scratch = refs[parts + STREAMS + parts * units :]
    feats, cols = tables[0].shape
    lanes = [(lo, min(lo + LANES, feats)) for lo in range(0, feats, LANES)]
    turned = scratch[: len(lanes)]
    picked = scratch[len(lanes) : 2 * len(lanes)]
    stage, sems = scratch[2 * len(lanes) :]
    step = pl.program_id(0)

    for s, table in enumerate(tables):
        base = jnp.minimum(step * STREAMS + s, blocks - 1) * cols
        for c in range(0, cols, GROUP):
            rows_at = pl.ds(pl.multiple_of(base + c, GROUP), GROUP)
            for (lo, hi), turn in zip(lanes, turned):
                turn[rows_at, :] = table[lo:hi, c : c + GROUP].T.astype(F32)

    @pl.when(step == pl.num_programs(0) - 1)
    def _():
        length = stage.shape[1]
        copies = []
        for p, out in enumerate(outs):
            u, r = p // parts, p % parts
            slot = p % 2

            def rows(i, carry, u=u, r=r):
                top = pl.multiple_of(i * UNROLL, UNROLL)
                for j in range(UNROLL):
                    token = ids[r][u, top + j]
                    for turn, pick in zip(turned, picked):
                        pick[pl.ds(top + j, 1), :] = turn[pl.ds(token, 1), :]
                return carry

            lax.fori_loop(0, length // UNROLL, rows, 0)
            if p >= 2:
                copies[p - 2].wait()
            for (lo, hi), pick in zip(lanes, picked):
                stage[slot, :, lo:hi] = pick[...].astype(BF16)
            copies.append(pltpu.make_async_copy(stage.at[slot], out, sems.at[slot]))
            copies[p].start()
        for copy in copies[-2:]:
            copy.wait()


def embed_call(ids, table):
    parts = len(ids)
    units, length = ids[0].shape
    feats, vocab = table.shape
    blocks = pl.cdiv(vocab, VOCAB_BLOCK)
    widths = [min(LANES, feats - lo) for lo in range(0, feats, LANES)]
    scratch = [pltpu.VMEM((blocks * VOCAB_BLOCK, w), F32) for w in widths]
    scratch += [pltpu.VMEM((length, w), F32) for w in widths]
    scratch += [pltpu.VMEM((2, length, feats), BF16), pltpu.SemaphoreType.DMA((2,))]
    streams = [
        pl.BlockSpec(
            (feats, VOCAB_BLOCK),
            functools.partial(lambda s, i: (0, jnp.minimum(i * STREAMS + s, blocks - 1)), s),
        )
        for s in range(STREAMS)
    ]
    return pl.pallas_call(
        functools.partial(embed_kernel, parts=parts, units=units, blocks=blocks),
        grid=(pl.cdiv(blocks, STREAMS),),
        in_specs=[SMEM] * parts + streams,
        out_specs=[ANY] * (parts * units),
        out_shape=[jax.ShapeDtypeStruct((length, feats), BF16)] * (parts * units),
        scratch_shapes=scratch,
        compiler_params=pltpu.CompilerParams(vmem_limit_bytes=62 * MIB),
        name="embed",
    )(*ids, *[table] * STREAMS)


def tile_rows(t, rows):
    lo = min(max(2 * t - 1, 0) * BLOCK, rows - min(SPAN, rows))
    return lo, min((2 * t + 3) * BLOCK, rows)


def block_pieces(b, blocks):
    first, last = max(b - 1, 0), min(b + 1, blocks - 1)
    found = []
    for t in range(blocks * BLOCK // GROUP):
        lo, hi = max(first, 2 * t), min(last, 2 * t + 1)
        if lo <= hi:
            found.append((t, lo, hi))
    return found


def spread(values, t, lo, hi):
    zero_block = jnp.zeros((BLOCK, BLOCK), BF16)
    parts = [values] if lo == 2 * t else [zero_block, values]
    if hi == 2 * t:
        parts.append(zero_block)
    return parts[0] if len(parts) == 1 else jnp.concatenate(parts, axis=1)


def head_masks():
    head_of = lax.broadcasted_iota(jnp.int32, (1, GROUP), 1) // HEAD_DIM
    in_head = [head_of == h for h in range(PER_GROUP)]
    return in_head, [jnp.where(m, 1.0, 0.0).astype(BF16) for m in in_head]


def segment_columns(seg_row):
    rows = seg_row.shape[1]
    lane = lax.broadcasted_iota(jnp.int32, (rows, rows), 1)
    sub = lax.broadcasted_iota(jnp.int32, (rows, rows), 0)
    return lane, sub, jnp.sum(jnp.where(lane == sub, seg_row, 0.0), axis=1, keepdims=True)


def tile_product(tiles, right):
    rows = right.shape[0]
    res = [None] * (rows // BLOCK)
    for t, left in enumerate(tiles):
        part = mm(left, right[t * GROUP : (t + 1) * GROUP])
        first = tile_rows(t, rows)[0] // BLOCK
        for i in range(left.shape[0] // BLOCK):
            piece = part[i * BLOCK : (i + 1) * BLOCK]
            res[first + i] = piece if res[first + i] is None else res[first + i] + piece
    return jnp.concatenate(res, axis=0)


def stacked_scores(left, right, keep):
    rows = left.shape[0]
    found = []
    for t in range(rows // GROUP):
        lo, hi = tile_rows(t, rows)
        stack = jnp.concatenate([left[lo:hi] * keep[h] for h in range(PER_GROUP)], axis=0)
        found.append(mm(stack, right[t * GROUP : (t + 1) * GROUP], NT))
    return found


def attend_kernel(*refs, parts, unit, fresh):
    pieces = refs[:parts]
    seg_ref, pos_ref, gain_ref, shift_ref, bias_ref, down_ref, up_ref, wqkv_hbm, wo_hbm = refs[
        parts : parts + 9
    ]
    refs = refs[parts + 9 + (0 if fresh else 6) :]
    outs, (x4, wqkv, wo, start, xb, normed0, q, k, v, red, pr, probs, mixed, sems) = refs[:6], refs[6:]
    rows, width = normed0.shape
    groups = width // GROUP
    blocks = rows // BLOCK
    tiles = rows // GROUP
    row_steps = rows // STEP_ROWS
    me = lax.axis_index("tensor")

    in_copies = [
        pltpu.make_async_copy(piece, x4.at[jnp.bitwise_xor(me, r)], sems.at[r])
        for r, piece in enumerate(pieces)
    ]
    w_copies = [
        pltpu.make_async_copy(wqkv_hbm, wqkv, sems.at[parts]),
        pltpu.make_async_copy(wo_hbm, wo, sems.at[parts + 1]),
    ]
    out_copies = [
        pltpu.make_async_copy(ref, out.at[unit], sems.at[parts + 2 + i])
        for i, (ref, out) in enumerate(zip((start, k, v, red, pr, probs), outs))
    ]
    for copy in in_copies + w_copies:
        copy.start()

    seg_row = seg_ref[...].astype(F32)
    lane, sub, seg_col = segment_columns(seg_row)
    same = seg_col == seg_row
    place = jnp.sum(jnp.where(same & (lane < sub), 1.0, 0.0), axis=1, keepdims=True)
    one_hot = jnp.where(lane == place.astype(jnp.int32), 1.0, 0.0).astype(BF16)
    start[...] = mm(one_hot, pos_ref[...])
    for copy in in_copies:
        copy.wait()
    start[...] += jnp.concatenate([x4[t] for t in range(parts)], axis=1).astype(F32)

    gain0, shift0 = gain_ref[0:1], shift_ref[0:1]

    def norm0(i, carry):
        x = start[at(i), :]
        off = x - row_mean(x)
        y = off * lax.rsqrt(row_mean(off * off) + LN_EPS) * gain0 + shift0
        normed0[at(i), :] = y
        xb[at(i), :] = y.astype(BF16)
        return carry

    lax.fori_loop(0, row_steps, norm0, 0)

    red[...] = mm(xb[...], down_ref[...]).astype(BF16)
    out_copies[3].start()
    w_copies[0].wait()
    q[...] = (mm(xb[...], wqkv[0]) + bias_ref[0:1] + mm(red[...], up_ref[0])).astype(BF16) * BF16(
        HEAD_DIM**-0.5
    )
    k[...] = (mm(xb[...], wqkv[1]) + bias_ref[1:2]).astype(BF16)
    out_copies[1].start()
    v[...] = (mm(xb[...], wqkv[2]) + bias_ref[2:3] + mm(red[...], up_ref[1])).astype(BF16)
    out_copies[2].start()

    in_head, keep = head_masks()

    def far(b, c):
        hit = seg_col[b * BLOCK : (b + 1) * BLOCK] == seg_row[:, c * BLOCK : (c + 1) * BLOCK]
        return jnp.where(hit, 0.0, -1e9)

    away = {
        (b, c): far(b, c) for b in range(blocks) for c in range(max(b - 1, 0), min(b + 2, blocks))
    }

    def attention(g, carry):
        lanes = pl.ds(pl.multiple_of(g * GROUP, GROUP), GROUP)
        vg = v[:, lanes]
        scores = stacked_scores(q[:, lanes], k[:, lanes], keep)
        out = jnp.zeros((rows, GROUP), F32)
        low = jnp.zeros((rows, GROUP), F32)
        for h in range(PER_GROUP):
            vrh = vg * keep[h] + red[...] * (1 - keep[h])
            prob_tiles = [[] for _ in range(tiles)]
            for b in range(blocks):
                found = []
                for t, lo, hi in block_pieces(b, blocks):
                    first, last = tile_rows(t, rows)
                    top = h * (last - first) + b * BLOCK - first
                    s = scores[t][top : top + BLOCK, (lo - 2 * t) * BLOCK : (hi + 1 - 2 * t) * BLOCK]
                    found.append(
                        s + jnp.concatenate([away[b, c] for c in range(lo, hi + 1)], axis=1)
                    )
                peak = functools.reduce(
                    jnp.maximum, [jnp.max(s, axis=1, keepdims=True) for s in found]
                )
                found = [jnp.exp(s - peak) for s in found]
                inv = 1.0 / add_all([jnp.sum(s, axis=1, keepdims=True) for s in found])
                for (t, lo, hi), s in zip(block_pieces(b, blocks), found):
                    prob_tiles[t].append(spread((s * inv).astype(BF16), t, lo, hi))
            prob_tiles = [jnp.concatenate(tile, axis=0) for tile in prob_tiles]
            for t, tile in enumerate(prob_tiles):
                probs[g * PER_GROUP + h, t, 0 : tile.shape[0], :] = tile
            res = tile_product(prob_tiles, vrh)
            out = jnp.where(in_head[h], res, out)
            low = jnp.where(in_head[(h + 1) % PER_GROUP], res, low)
        mixed[:, lanes] = out.astype(BF16)
        pr[:, lanes] = low.astype(BF16)
        return carry

    lax.fori_loop(0, groups, attention, 0)
    out_copies[4].start()
    out_copies[5].start()
    w_copies[1].wait()
    start[...] = normed0[...] + (mm(mixed[...], wo[...]) + bias_ref[3:4])
    out_copies[0].start()
    for copy in out_copies:
        copy.wait()


def attend_call(pieces, seg, small, wqkv, wo, kept, unit, units):
    pos, gain, shift, bias, down, up = small
    parts = len(pieces)
    rows, feats = pieces[0].shape
    width = pos.shape[1]
    heads = width // HEAD_DIM
    tiles = rows // GROUP
    forms = [
        ((rows, width), F32),
        ((rows, width), BF16),
        ((rows, width), BF16),
        ((rows, GROUP), BF16),
        ((rows, width), BF16),
        ((heads, tiles, SPAN, GROUP), BF16),
    ]
    fresh = kept is None
    scratch = [
        pltpu.VMEM((parts, rows, feats), BF16),
        pltpu.VMEM(wqkv.shape, BF16),
        pltpu.VMEM(wo.shape, BF16),
        pltpu.VMEM((rows, width), F32),
        pltpu.VMEM((rows, width), BF16),
        pltpu.VMEM((rows, width), F32),
        pltpu.VMEM((rows, width), BF16),
        pltpu.VMEM((rows, width), BF16),
        pltpu.VMEM((rows, width), BF16),
        pltpu.VMEM((rows, GROUP), BF16),
        pltpu.VMEM((rows, width), BF16),
        pltpu.VMEM((heads, tiles, SPAN, GROUP), BF16),
        pltpu.VMEM((rows, width), BF16),
        pltpu.SemaphoreType.DMA((parts + 8,)),
    ]
    args = [*pieces, seg, pos, gain, shift, bias, down, up, wqkv, wo]
    aliases = {} if fresh else {len(args) + i: i for i in range(len(forms))}
    return pl.pallas_call(
        functools.partial(attend_kernel, parts=parts, unit=unit, fresh=fresh),
        out_shape=[jax.ShapeDtypeStruct((units, *shape), kind) for shape, kind in forms],
        in_specs=[ANY] * parts + [VMEM] * 7 + [ANY] * 2 + ([] if fresh else [ANY] * len(forms)),
        out_specs=[ANY] * len(forms),
        input_output_aliases=aliases,
        scratch_shapes=scratch,
        compiler_params=pltpu.CompilerParams(vmem_limit_bytes=58 * MIB),
        cost_estimate=pl.CostEstimate(
            flops=rows * width * width,
            bytes_accessed=4 * MIB,
            transcendentals=0,
        ),
        name="attend",
    )(*args, *([] if fresh else kept))


def finish_kernel(*refs, places, parts):
    (seg_ref, label_ref, gain_ref, shift_ref, bias_ref, head_ref, ffb_ref, wo_hbm, *refs) = refs
    weight_pieces, refs = refs[: 2 * len(places)], refs[2 * len(places) :]
    kept, refs = refs[:6], refs[6:]
    acc_ref, refs = refs[0], refs[1:]
    bufs, refs = refs[:6], refs[6:]
    wo, win, wout, xb, mixed, xh1, stat1, acc, slope, act, sems, wsems = refs
    resid2buf, k2, v2, red2, pr2, probs2 = bufs
    units = kept[0].shape[0]
    rows, width = xh1.shape
    hidden_part = win.shape[2]
    chunk = GROUP if hidden_part % GROUP == 0 else hidden_part
    groups = width // GROUP
    blocks = rows // BLOCK
    tiles = rows // GROUP
    row_steps = rows // STEP_ROWS
    half = lax.rem(lax.axis_index("dp"), 2)

    def weight_copies():
        made = []
        for i, (ref, (r, mine)) in enumerate(zip(weight_pieces[: len(places)], places)):
            if mine is None:
                dst = win.at[r]
            else:
                n = width // 2
                top = pl.multiple_of((half if mine else 1 - half) * n, 16)
                dst = win.at[r, pl.ds(top, n), :]
            made.append(pltpu.make_async_copy(ref, dst, wsems.at[i]))
        for i, (ref, (r, mine)) in enumerate(zip(weight_pieces[len(places) :], places)):
            if mine is None:
                dst = wout.at[r]
            else:
                n = hidden_part // 2
                top = pl.multiple_of((half if mine else 1 - half) * n, 16)
                dst = wout.at[r, pl.ds(top, n), :]
            made.append(pltpu.make_async_copy(ref, dst, wsems.at[len(places) + i]))
        made.append(pltpu.make_async_copy(wo_hbm, wo, wsems.at[2 * len(places)]))
        return made

    def state_copies(u, slot):
        return [
            pltpu.make_async_copy(src.at[u], buf.at[slot], sems.at[slot, i])
            for i, (src, buf) in enumerate(zip(kept, bufs))
        ]

    for copy in state_copies(0, 0)[:1] + weight_copies() + state_copies(0, 0)[1:]:
        copy.start()

    gain1, gain2 = gain_ref[1:2], gain_ref[2:3]
    shift1, shift2 = shift_ref[1:2], shift_ref[2:3]
    head = head_ref[0:1, 0:width]
    head_bias = head_ref[0:1, width : width + 1]
    hg = head * gain2
    hg_mean = row_mean(hg)
    bias4 = bias_ref[4:5]
    base = jnp.sum(shift2 * head, axis=1, keepdims=True)
    in_head, keep = head_masks()
    acc_ref[...] = jnp.zeros(acc_ref.shape, F32)

    def unit(u, carry):
        slot = lax.rem(u, 2)
        now = state_copies(u, slot)

        @pl.when(u + 1 < units)
        def _():
            for copy in state_copies(u + 1, 1 - slot):
                copy.start()

        now[0].wait()

        def norm1(i, c):
            x = resid2buf[slot, at(i), :]
            off = x - row_mean(x)
            inv = lax.rsqrt(row_mean(off * off) + LN_EPS)
            xh = off * inv
            xh1[at(i), :] = xh
            stat1[at(i), :] = inv
            xb[at(i), :] = (xh * gain1 + shift1).astype(BF16)
            return c

        lax.fori_loop(0, row_steps, norm1, 0)

        @pl.when(u == 0)
        def _():
            for copy in weight_copies():
                copy.wait()

        for r in range(parts):
            for c in range(0, hidden_part, chunk):
                hid = slice(r * hidden_part + c, r * hidden_part + c + chunk)
                pre = mm(xb[...], win[r, :, c : c + chunk]) + ffb_ref[:, hid]
                phi = 0.5 + 0.5 * lax.erf(pre * INV_SQRT2)
                act[:, hid] = (pre * phi).astype(BF16)
                slope[:, hid] = phi + pre * jnp.exp(-0.5 * pre * pre) * INV_SQRT_2PI
        for n in range(0, width, GROUP):
            acc[:, n : n + GROUP] = add_all(
                [
                    mm(act[:, r * hidden_part : (r + 1) * hidden_part], wout[r, :, n : n + GROUP])
                    for r in range(parts)
                ]
            )

        inv_cols = []
        dot_cols = []
        for i in range(row_steps):
            part = slice(i * STEP_ROWS, (i + 1) * STEP_ROWS)
            x = xh1[part, :] * gain1 + shift1 + (acc[part, :] + bias4)
            off = x - row_mean(x)
            inv = lax.rsqrt(row_mean(off * off) + LN_EPS)
            xh = off * inv
            acc[part, :] = xh
            inv_cols.append(inv)
            dot_cols.append(jnp.sum(xh * hg, axis=1, keepdims=True))
        inv2 = jnp.concatenate(inv_cols, axis=0)
        dots = jnp.concatenate(dot_cols, axis=0)

        seg_row = seg_ref[u].astype(F32)
        seg_col = segment_columns(seg_row)[2]
        label = label_ref[u]
        slots = label.shape[1]
        slot_no = lax.broadcasted_iota(jnp.int32, (rows, slots), 1).astype(F32)
        member = jnp.where(seg_col == slot_no, 1.0, 0.0)
        counts = jnp.sum(member, axis=0, keepdims=True)
        sums = jnp.sum(member * (dots + base), axis=0, keepdims=True)
        most = jnp.maximum(counts, 1.0)
        error = jnp.where(counts > 0, sums / most + head_bias - label, 0.0)
        grad_pred = 2.0 * error
        weight = jnp.sum(member * (grad_pred / most), axis=1, keepdims=True)
        loss = jnp.sum(error * error, axis=1, keepdims=True)
        weight_sum = jnp.sum(grad_pred, axis=1, keepdims=True)
        items = jnp.max(seg_row, axis=1, keepdims=True) + 1.0

        head_grad = jnp.zeros((8, width), F32)
        for i in range(row_steps):
            part = slice(i * STEP_ROWS, (i + 1) * STEP_ROWS)
            xh = acc[part, :]
            w = weight[part]
            weighted = xh * w
            for j in range(STEP_ROWS // 8):
                head_grad = head_grad + weighted[j * 8 : (j + 1) * 8]
            grad = (inv2[part] * w) * (hg - hg_mean - xh * (dots[part] * (1.0 / width)))
            acc[part, :] = grad
            xb[part, :] = grad.astype(BF16)
        head_grad = jnp.sum(head_grad, axis=0, keepdims=True) * gain2 + weight_sum * shift2
        acc_ref[16:17, :] += head_grad
        lane_row = lax.broadcasted_iota(jnp.int32, (1, width), 1)
        acc_ref[17:18, :] += jnp.where(
            lane_row == 0,
            loss,
            jnp.where(lane_row == 1, items, jnp.where(lane_row == 2, weight_sum, 0.0)),
        )

        for r in range(parts):
            for c in range(0, hidden_part, chunk):
                hid = slice(r * hidden_part + c, r * hidden_part + c + chunk)
                back = mm(xb[...], wout[r, c : c + chunk, :], NT)
                act[:, hid] = (back * slope[:, hid]).astype(BF16)
        for n in range(0, width, GROUP):
            acc[:, n : n + GROUP] = add_all(
                [acc[:, n : n + GROUP]]
                + [
                    mm(
                        act[:, r * hidden_part : (r + 1) * hidden_part],
                        win[r, n : n + GROUP, :],
                        NT,
                    )
                    for r in range(parts)
                ]
            )

        def back1(i, c):
            g = acc[at(i), :] * gain1
            xh = xh1[at(i), :]
            grad = stat1[at(i), :] * (g - row_mean(g) - xh * row_mean(g * xh))
            xb[at(i), :] = grad.astype(BF16)
            return c

        lax.fori_loop(0, row_steps, back1, 0)

        mixed[...] = mm(xb[...], wo[...], NT).astype(BF16)
        for copy in now[1:]:
            copy.wait()

        def attention_back(g, c):
            lanes = pl.ds(pl.multiple_of(g * GROUP, GROUP), GROUP)
            gg, kg = mixed[:, lanes], k2[slot, :, lanes]
            grads = stacked_scores(gg, v2[slot, :, lanes], keep)
            out = jnp.zeros((rows, GROUP), F32)
            for h in range(PER_GROUP):
                score_tiles = [[] for _ in range(tiles)]
                for b in range(blocks):
                    found = []
                    for t, lo, hi in block_pieces(b, blocks):
                        first, last = tile_rows(t, rows)
                        top = b * BLOCK - first
                        lane_at = slice((lo - 2 * t) * BLOCK, (hi + 1 - 2 * t) * BLOCK)
                        here = h * (last - first) + top
                        dp = grads[t][here : here + BLOCK, lane_at]
                        p = probs2[slot, g * PER_GROUP + h, t, top : top + BLOCK, lane_at]
                        found.append((p.astype(F32), dp))
                    shared = add_all([jnp.sum(p * dp, axis=1, keepdims=True) for p, dp in found])
                    for (t, lo, hi), (p, dp) in zip(block_pieces(b, blocks), found):
                        score_tiles[t].append(
                            spread((p * (dp - shared)).astype(BF16), t, lo, hi)
                        )
                res = tile_product([jnp.concatenate(tile, axis=0) for tile in score_tiles], kg)
                out = jnp.where(in_head[h], res, out)
            query_part = mm(red2[slot], out.astype(BF16), TN)[0:8]
            acc_ref[0:8, lanes] += query_part * (2.0 * HEAD_DIM**-0.5)
            cross = mm(pr2[slot, :, lanes], gg, TN)
            value_part = jnp.zeros((8, GROUP), F32)
            for h in range(PER_GROUP):
                top = ((h + 1) % PER_GROUP) * HEAD_DIM + 8
                value_part = jnp.where(in_head[h], cross[top : top + 8], value_part)
            acc_ref[8:16, lanes] += 2.0 * value_part
            return c

        lax.fori_loop(0, groups, attention_back, 0)
        return carry

    lax.fori_loop(0, units, unit, 0)


def finish_call(segs, labels, small, wo, weight_in, weight_out, places, kept, parts):
    gain, shift, bias, head, ffb = small
    units, rows, width = kept[0].shape
    hidden_part = weight_in[0].shape[1]
    hidden = hidden_part * parts
    scratch = [pltpu.VMEM((2, *a.shape[1:]), a.dtype) for a in kept]
    scratch += [
        pltpu.VMEM(wo.shape, BF16),
        pltpu.VMEM((parts, width, hidden_part), BF16),
        pltpu.VMEM((parts, hidden_part, width), BF16),
        pltpu.VMEM((rows, width), BF16),
        pltpu.VMEM((rows, width), BF16),
        pltpu.VMEM((rows, width), F32),
        pltpu.VMEM((rows, 1), F32),
        pltpu.VMEM((rows, width), F32),
        pltpu.VMEM((rows, hidden), F32),
        pltpu.VMEM((rows, hidden), BF16),
        pltpu.SemaphoreType.DMA((2, len(kept))),
        pltpu.SemaphoreType.DMA((2 * len(places) + 1,)),
    ]
    return pl.pallas_call(
        functools.partial(finish_kernel, places=places, parts=parts),
        out_shape=jax.ShapeDtypeStruct((ACC_ROWS, width), F32),
        in_specs=[VMEM] * 7 + [ANY] * (1 + 2 * len(places) + len(kept)),
        out_specs=VMEM,
        scratch_shapes=scratch,
        compiler_params=pltpu.CompilerParams(vmem_limit_bytes=62 * MIB),
        cost_estimate=pl.CostEstimate(
            flops=units * 2 * rows * width * (4 * hidden + width + 2 * rows),
            bytes_accessed=48 * MIB,
            transcendentals=2 * units * rows * hidden,
        ),
        name="finish",
    )(segs, labels, gain, shift, bias, head, ffb, wo, *weight_in, *weight_out, *kept)


def update_kernel(
    acc_ref,
    other_ref,
    up_ref,
    momentum_ref,
    head_ref,
    first_ref,
    second_ref,
    loss_ref,
    items_ref,
    norm_ref,
    moment_out,
    up_out,
    low_out,
    first_out,
    second_out,
    head_out,
    head_low_out,
):
    total = acc_ref[...] + other_ref[...]
    width = total.shape[1]
    rank = up_ref.shape[0] // 2
    items = total[17:18, 1:2]
    loss_ref[...] = total[17:18, 0:1]
    items_ref[...] = items
    adapter = total[0:16] / items
    head_grad = jnp.concatenate([total[16:17], total[17:18, 2:3]], axis=1) / items
    norm = jnp.sqrt(jnp.sum(adapter * adapter) + jnp.sum(head_grad * head_grad))
    norm_ref[...] = jnp.full((1, 1), norm, F32)
    factor = jnp.minimum(1.0, CLIP_NORM / (norm_ref[...] + 1e-06))
    moment = ORTHO_MOMENTUM * momentum_ref[...] + factor * adapter
    moment_out[...] = moment

    def dot(left, right, dims=NN):
        return lax.dot_general(
            left, right, dims, preferred_element_type=F32, precision=lax.Precision.HIGHEST
        )

    basis = []
    for i in range(2):
        part = moment[i * rank : (i + 1) * rank]
        size = jnp.sqrt(jnp.sum(jnp.sum(part * part, axis=1, keepdims=True), axis=0, keepdims=True))
        basis.append(part / (size + 1e-07))
    for sweep in range(5):
        gram = [dot(x, x, NT) for x in basis]
        poly = [NS_B * g + NS_C * dot(g, g) for g in gram]
        basis = [NS_A * x + dot(p, x) for x, p in zip(basis, poly)]
    up = up_ref[...] - ORTHO_STEP_SIZE * jnp.concatenate(basis, axis=0)
    up_out[...] = up
    low_out[...] = up.astype(BF16)

    clipped = factor * head_grad
    first = BETA_ONE * first_ref[...] + (1.0 - BETA_ONE) * clipped
    second = BETA_TWO * second_ref[...] + (1.0 - BETA_TWO) * clipped * clipped
    first_hat = first / (1.0 - BETA_ONE**STEP)
    second_hat = second / (1.0 - BETA_TWO**STEP)
    head = head_ref[...]
    new_head = head - ADAM_RATE * (first_hat / (jnp.sqrt(second_hat) + ADAM_EPS) + DECAY * head)
    first_out[...] = first[0]
    second_out[...] = second[0]
    head_out[...] = new_head[0]
    head_low_out[...] = new_head[0].astype(BF16)


def update_call(acc, other, up, momentum, head, first, second):
    one = jax.ShapeDtypeStruct((1, 1), F32)
    flat = jax.ShapeDtypeStruct(up.shape, F32)
    row = jax.ShapeDtypeStruct(head.shape[1:], F32)
    return pl.pallas_call(
        update_kernel,
        out_shape=[
            one,
            one,
            one,
            flat,
            flat,
            jax.ShapeDtypeStruct(up.shape, BF16),
            row,
            row,
            row,
            jax.ShapeDtypeStruct(head.shape[1:], BF16),
        ],
        in_specs=[VMEM] * 7,
        out_specs=[VMEM] * 10,
        name="update",
    )(acc, other, up, momentum, head, first, second)


def swap(value, axis, bit):
    size = lax.axis_size(axis)
    return lax.ppermute(value, axis, [(i, i ^ bit) for i in range(size)])


def gather_weights(own_in, own_out):
    parts = lax.axis_size("tensor")
    half = lax.rem(lax.axis_index("dp"), 2)

    def cut(w):
        n = w.shape[0] // 2
        return lax.dynamic_slice_in_dim(w, half * n, n, 0)

    found = {}
    for name, own in (("in", own_in), ("out", own_out)):
        mine = {0: cut(own)}
        bit = parts // 2
        while bit > 1:
            for r in list(mine):
                mine[r ^ bit] = swap(mine[r], "tensor", bit)
            bit //= 2
        del mine[0]
        full = [(own, 0, None), (swap(own, "tensor", 1), 1, None)]
        other = {r: swap(a, "dp", 1) for r, a in mine.items()}
        for r in mine:
            full += [(mine[r], r, True), (other[r], r, False)]
            full += [(swap(mine[r], "tensor", 1), r ^ 1, True)]
            full += [(swap(other[r], "tensor", 1), r ^ 1, False)]
        found[name] = full
    places = tuple((r, mine) for _, r, mine in found["in"])
    return [a for a, _, _ in found["in"]], [a for a, _, _ in found["out"]], places


def local(
    input_token_ids,
    segments,
    labels,
    embedding,
    position_embedding_table,
    norm_gain_rows,
    norm_shift_rows,
    query_key_value_weight,
    attention_output_weight,
    attention_bias_stack,
    feedforward_in_weight,
    feedforward_bias,
    feedforward_out_weight,
    adapter_down_weight,
    adapter_up_weight,
    adapter_momentum,
    head,
    head_first_moment,
    head_second_moment,
):
    length = input_token_ids.shape[-1]
    slots = labels.shape[-1]
    width = position_embedding_table.shape[1]
    rank = adapter_up_weight.shape[1]
    parts = lax.axis_size("tensor")
    ids = input_token_ids.reshape(-1, length)
    segs = segments.reshape(-1, 1, length)
    labs = labels.reshape(-1, 1, slots)
    units = ids.shape[0]

    all_ids = [ids] + [swap(ids, "tensor", r) for r in range(1, parts)]
    ffb = feedforward_bias[None, :].astype(F32)
    ffb = jnp.concatenate([ffb] + [swap(ffb, "tensor", r) for r in range(1, parts)], axis=1)
    weight_in, weight_out, places = gather_weights(feedforward_in_weight, feedforward_out_weight)

    down = jnp.concatenate(
        [
            adapter_down_weight[0],
            adapter_down_weight[1],
            jnp.zeros((width, HEAD_DIM - 2 * rank), BF16),
        ],
        axis=1,
    )
    down = jnp.concatenate([down] * PER_GROUP, axis=1)
    twice = 2.0 * adapter_up_weight.astype(BF16)
    up = jnp.stack(
        [
            jnp.pad(twice[0], ((0, GROUP - rank), (0, 0))),
            jnp.pad(twice[1], ((rank, GROUP - 2 * rank), (0, 0))),
        ]
    )
    head_rows = [head[None, :], head_first_moment[None, :], head_second_moment[None, :]]
    all_ids, down, up, head_rows = lax.optimization_barrier((all_ids, down, up, head_rows))
    picked = embed_call(all_ids, embedding)
    picked = [picked[u * parts : (u + 1) * parts] for u in range(units)]

    small = (
        position_embedding_table,
        norm_gain_rows,
        norm_shift_rows,
        attention_bias_stack,
        down,
        up,
    )
    kept = None
    moved = []
    for u in range(units):
        while len(moved) < min(u + 2, units):
            sends = picked[len(moved)][1:]
            if moved:
                sends = lax.optimization_barrier((sends, moved[-1], kept))[0]
            moved.append([swap(a, "tensor", r + 1) for r, a in enumerate(sends)])
        kept = attend_call(
            [picked[u][0], *moved[u]],
            segs[u],
            small,
            query_key_value_weight,
            attention_output_weight,
            kept,
            u,
            units,
        )

    acc = finish_call(
        segs,
        labs,
        (norm_gain_rows, norm_shift_rows, attention_bias_stack, head_rows[0], ffb),
        attention_output_weight,
        weight_in,
        weight_out,
        places,
        kept,
        parts,
    )
    steps = []
    for axis in ("tensor", "dp"):
        bit = 1
        while bit < lax.axis_size(axis):
            steps.append((axis, bit))
            bit *= 2
    for axis, bit in steps[:-1]:
        acc = acc + swap(acc, axis, bit)
    other = swap(acc, *steps[-1])

    flat = (2 * rank, width)
    outs = update_call(
        acc,
        other,
        adapter_up_weight.reshape(flat),
        adapter_momentum.reshape(flat),
        *head_rows,
    )
    loss, items, norm, moment, new_up, low, first, second, new_head, head_low = outs
    shape = adapter_up_weight.shape
    return (
        loss[0, 0],
        items[0, 0],
        norm[0, 0],
        moment.reshape(shape),
        new_up.reshape(shape),
        low.reshape(shape),
        first,
        second,
        new_head,
        head_low,
    )


def solution(mesh):
    rows = P(None, ("dp", "tensor"), None)
    placed = (
        (rows, rows, rows, P("tensor", None))
        + (P(),) * 6
        + (P(None, "tensor"), P("tensor"), P("tensor", None))
        + (P(),) * 6
    )
    return jax.shard_map(
        local, mesh=mesh, in_specs=placed, out_specs=(P(),) * 10, check_vma=False
    )
```

```python
import functools
import math

import jax
import jax.numpy as jnp
from jax import lax
from jax.experimental import pallas as pl
from jax.experimental.pallas import tpu as pltpu
from jax.sharding import PartitionSpec as P

HEAD_DIM = 64
STEP = 10
LN_EPS = 1e-05
CLIP_NORM = 0.5
ORTHO_MOMENTUM = 0.5
ORTHO_STEP_SIZE = 1.0
NS_A = 3.4445
NS_B = -4.775
NS_C = 2.0315
BETA_ONE = 0.9
BETA_TWO = 0.999
ADAM_RATE = 0.05
ADAM_EPS = 1e-08
DECAY = 0.01

F32 = jnp.float32
BF16 = jnp.bfloat16
LANES = 128
GROUP = 256
PER_GROUP = GROUP // HEAD_DIM
BLOCK = 128
SPAN = 3 * BLOCK
STEP_ROWS = 64
VOCAB_BLOCK = 2048
STREAMS = 2
UNROLL = 64
ACC_ROWS = 24
MIB = 1024 * 1024
NN = (((1,), (0,)), ((), ()))
NT = (((1,), (1,)), ((), ()))
TN = (((0,), (0,)), ((), ()))
INV_SQRT2 = 1.0 / math.sqrt(2.0)
INV_SQRT_2PI = 1.0 / math.sqrt(2.0 * math.pi)

VMEM = pl.BlockSpec(memory_space=pltpu.VMEM)
SMEM = pl.BlockSpec(memory_space=pltpu.SMEM)
ANY = pl.BlockSpec(memory_space=pl.ANY)


def mm(left, right, dims=NN):
    return lax.dot_general(left, right, dims, preferred_element_type=F32)


def row_mean(rows):
    return jnp.mean(rows, axis=-1, keepdims=True)


def add_all(terms):
    return functools.reduce(jnp.add, terms)


def at(i):
    return pl.ds(pl.multiple_of(i * STEP_ROWS, STEP_ROWS), STEP_ROWS)


def embed_kernel(*refs, parts, units, blocks):
    ids = refs[:parts]
    tables = refs[parts : parts + STREAMS]
    outs = refs[parts + STREAMS : parts + STREAMS + parts * units]
    scratch = refs[parts + STREAMS + parts * units :]
    feats, cols = tables[0].shape
    lanes = [(lo, min(lo + LANES, feats)) for lo in range(0, feats, LANES)]
    turned = scratch[: len(lanes)]
    picked = scratch[len(lanes) : 2 * len(lanes)]
    stage, sems = scratch[2 * len(lanes) :]
    step = pl.program_id(0)

    for s, table in enumerate(tables):
        base = jnp.minimum(step * STREAMS + s, blocks - 1) * cols
        for c in range(0, cols, GROUP):
            rows_at = pl.ds(pl.multiple_of(base + c, GROUP), GROUP)
            for (lo, hi), turn in zip(lanes, turned):
                turn[rows_at, :] = table[lo:hi, c : c + GROUP].T.astype(F32)

    @pl.when(step == pl.num_programs(0) - 1)
    def _():
        length = stage.shape[1]
        copies = []
        for p, out in enumerate(outs):
            u, r = p // parts, p % parts
            slot = p % 2

            def rows(i, carry, u=u, r=r):
                top = pl.multiple_of(i * UNROLL, UNROLL)
                for j in range(UNROLL):
                    token = ids[r][u, top + j]
                    for turn, pick in zip(turned, picked):
                        pick[pl.ds(top + j, 1), :] = turn[pl.ds(token, 1), :]
                return carry

            lax.fori_loop(0, length // UNROLL, rows, 0)
            if p >= 2:
                copies[p - 2].wait()
            for (lo, hi), pick in zip(lanes, picked):
                stage[slot, :, lo:hi] = pick[...].astype(BF16)
            copies.append(pltpu.make_async_copy(stage.at[slot], out, sems.at[slot]))
            copies[p].start()
        for copy in copies[-2:]:
            copy.wait()


def embed_call(ids, table):
    parts = len(ids)
    units, length = ids[0].shape
    feats, vocab = table.shape
    blocks = pl.cdiv(vocab, VOCAB_BLOCK)
    widths = [min(LANES, feats - lo) for lo in range(0, feats, LANES)]
    scratch = [pltpu.VMEM((blocks * VOCAB_BLOCK, w), F32) for w in widths]
    scratch += [pltpu.VMEM((length, w), F32) for w in widths]
    scratch += [pltpu.VMEM((2, length, feats), BF16), pltpu.SemaphoreType.DMA((2,))]
    streams = [
        pl.BlockSpec(
            (feats, VOCAB_BLOCK),
            functools.partial(lambda s, i: (0, jnp.minimum(i * STREAMS + s, blocks - 1)), s),
        )
        for s in range(STREAMS)
    ]
    return pl.pallas_call(
        functools.partial(embed_kernel, parts=parts, units=units, blocks=blocks),
        grid=(pl.cdiv(blocks, STREAMS),),
        in_specs=[SMEM] * parts + streams,
        out_specs=[ANY] * (parts * units),
        out_shape=[jax.ShapeDtypeStruct((length, feats), BF16)] * (parts * units),
        scratch_shapes=scratch,
        compiler_params=pltpu.CompilerParams(vmem_limit_bytes=62 * MIB),
        cost_estimate=pl.CostEstimate(
            flops=length * feats, bytes_accessed=MIB // 4, transcendentals=0
        ),
        name="embed",
    )(*ids, *[table] * STREAMS)


def tile_rows(t, rows):
    lo = min(max(2 * t - 1, 0) * BLOCK, rows - min(SPAN, rows))
    return lo, min((2 * t + 3) * BLOCK, rows)


def block_pieces(b, blocks):
    first, last = max(b - 1, 0), min(b + 1, blocks - 1)
    found = []
    for t in range(blocks * BLOCK // GROUP):
        lo, hi = max(first, 2 * t), min(last, 2 * t + 1)
        if lo <= hi:
            found.append((t, lo, hi))
    return found


def spread(values, t, lo, hi):
    zero_block = jnp.zeros((BLOCK, BLOCK), BF16)
    parts = [values] if lo == 2 * t else [zero_block, values]
    if hi == 2 * t:
        parts.append(zero_block)
    return parts[0] if len(parts) == 1 else jnp.concatenate(parts, axis=1)


def head_masks():
    head_of = lax.broadcasted_iota(jnp.int32, (1, GROUP), 1) // HEAD_DIM
    in_head = [head_of == h for h in range(PER_GROUP)]
    return in_head, [jnp.where(m, 1.0, 0.0).astype(BF16) for m in in_head]


def segment_columns(seg_row):
    rows = seg_row.shape[1]
    lane = lax.broadcasted_iota(jnp.int32, (rows, rows), 1)
    sub = lax.broadcasted_iota(jnp.int32, (rows, rows), 0)
    return lane, sub, jnp.sum(jnp.where(lane == sub, seg_row, 0.0), axis=1, keepdims=True)


def tile_product(tiles, right):
    rows = right.shape[0]
    res = [None] * (rows // BLOCK)
    for t, left in enumerate(tiles):
        part = mm(left, right[t * GROUP : (t + 1) * GROUP])
        first = tile_rows(t, rows)[0] // BLOCK
        for i in range(left.shape[0] // BLOCK):
            piece = part[i * BLOCK : (i + 1) * BLOCK]
            res[first + i] = piece if res[first + i] is None else res[first + i] + piece
    return jnp.concatenate(res, axis=0)


def stacked_scores(left, right, keep):
    rows = left.shape[0]
    found = []
    for t in range(rows // GROUP):
        lo, hi = tile_rows(t, rows)
        stack = jnp.concatenate([left[lo:hi] * keep[h] for h in range(PER_GROUP)], axis=0)
        found.append(mm(stack, right[t * GROUP : (t + 1) * GROUP], NT))
    return found


def attend_kernel(*refs, parts, unit, fresh):
    pieces = refs[:parts]
    seg_ref, pos_ref, gain_ref, shift_ref, bias_ref, down_ref, up_ref, wqkv_hbm, wo_hbm = refs[
        parts : parts + 9
    ]
    refs = refs[parts + 9 + (0 if fresh else 6) :]
    outs, (x4, wqkv, wo, start, xb, normed0, q, k, v, red, pr, probs, mixed, sems) = refs[:6], refs[6:]
    rows, width = normed0.shape
    groups = width // GROUP
    blocks = rows // BLOCK
    tiles = rows // GROUP
    row_steps = rows // STEP_ROWS
    me = lax.axis_index("tensor")

    in_copies = [
        pltpu.make_async_copy(piece, x4.at[jnp.bitwise_xor(me, r)], sems.at[r])
        for r, piece in enumerate(pieces)
    ]
    w_copies = [
        pltpu.make_async_copy(wqkv_hbm, wqkv, sems.at[parts]),
        pltpu.make_async_copy(wo_hbm, wo, sems.at[parts + 1]),
    ]
    out_copies = [
        pltpu.make_async_copy(ref, out.at[unit], sems.at[parts + 2 + i])
        for i, (ref, out) in enumerate(zip((start, k, v, red, pr, probs), outs))
    ]
    for copy in in_copies + w_copies:
        copy.start()

    seg_row = seg_ref[...].astype(F32)
    lane, sub, seg_col = segment_columns(seg_row)
    same = seg_col == seg_row
    place = jnp.sum(jnp.where(same & (lane < sub), 1.0, 0.0), axis=1, keepdims=True)
    one_hot = jnp.where(lane == place.astype(jnp.int32), 1.0, 0.0).astype(BF16)
    start[...] = mm(one_hot, pos_ref[...])
    for copy in in_copies:
        copy.wait()
    start[...] += jnp.concatenate([x4[t] for t in range(parts)], axis=1).astype(F32)

    gain0, shift0 = gain_ref[0:1], shift_ref[0:1]

    def norm0(i, carry):
        x = start[at(i), :]
        off = x - row_mean(x)
        y = off * lax.rsqrt(row_mean(off * off) + LN_EPS) * gain0 + shift0
        normed0[at(i), :] = y
        xb[at(i), :] = y.astype(BF16)
        return carry

    lax.fori_loop(0, row_steps, norm0, 0)

    red[...] = mm(xb[...], down_ref[...]).astype(BF16)
    out_copies[3].start()
    w_copies[0].wait()
    q[...] = (mm(xb[...], wqkv[0]) + bias_ref[0:1] + mm(red[...], up_ref[0])).astype(BF16) * BF16(
        HEAD_DIM**-0.5
    )
    k[...] = (mm(xb[...], wqkv[1]) + bias_ref[1:2]).astype(BF16)
    out_copies[1].start()
    v[...] = (mm(xb[...], wqkv[2]) + bias_ref[2:3] + mm(red[...], up_ref[1])).astype(BF16)
    out_copies[2].start()

    in_head, keep = head_masks()

    def far(b, c):
        hit = seg_col[b * BLOCK : (b + 1) * BLOCK] == seg_row[:, c * BLOCK : (c + 1) * BLOCK]
        return jnp.where(hit, 0.0, -1e9)

    away = {
        (b, c): far(b, c) for b in range(blocks) for c in range(max(b - 1, 0), min(b + 2, blocks))
    }

    def attention(g, carry):
        lanes = pl.ds(pl.multiple_of(g * GROUP, GROUP), GROUP)
        vg = v[:, lanes]
        scores = stacked_scores(q[:, lanes], k[:, lanes], keep)
        out = jnp.zeros((rows, GROUP), F32)
        low = jnp.zeros((rows, GROUP), F32)
        for h in range(PER_GROUP):
            vrh = vg * keep[h] + red[...] * (1 - keep[h])
            prob_tiles = [[] for _ in range(tiles)]
            for b in range(blocks):
                found = []
                for t, lo, hi in block_pieces(b, blocks):
                    first, last = tile_rows(t, rows)
                    top = h * (last - first) + b * BLOCK - first
                    s = scores[t][top : top + BLOCK, (lo - 2 * t) * BLOCK : (hi + 1 - 2 * t) * BLOCK]
                    found.append(
                        s + jnp.concatenate([away[b, c] for c in range(lo, hi + 1)], axis=1)
                    )
                peak = functools.reduce(
                    jnp.maximum, [jnp.max(s, axis=1, keepdims=True) for s in found]
                )
                found = [jnp.exp(s - peak) for s in found]
                inv = 1.0 / add_all([jnp.sum(s, axis=1, keepdims=True) for s in found])
                for (t, lo, hi), s in zip(block_pieces(b, blocks), found):
                    prob_tiles[t].append(spread((s * inv).astype(BF16), t, lo, hi))
            prob_tiles = [jnp.concatenate(tile, axis=0) for tile in prob_tiles]
            for t, tile in enumerate(prob_tiles):
                probs[g * PER_GROUP + h, t, 0 : tile.shape[0], :] = tile
            res = tile_product(prob_tiles, vrh)
            out = jnp.where(in_head[h], res, out)
            low = jnp.where(in_head[(h + 1) % PER_GROUP], res, low)
        mixed[:, lanes] = out.astype(BF16)
        pr[:, lanes] = low.astype(BF16)
        return carry

    lax.fori_loop(0, groups, attention, 0)
    out_copies[4].start()
    out_copies[5].start()
    w_copies[1].wait()
    start[...] = normed0[...] + (mm(mixed[...], wo[...]) + bias_ref[3:4])
    out_copies[0].start()
    for copy in out_copies:
        copy.wait()


def attend_call(pieces, seg, small, wqkv, wo, kept, unit, units):
    pos, gain, shift, bias, down, up = small
    parts = len(pieces)
    rows, feats = pieces[0].shape
    width = pos.shape[1]
    heads = width // HEAD_DIM
    tiles = rows // GROUP
    forms = [
        ((rows, width), F32),
        ((rows, width), BF16),
        ((rows, width), BF16),
        ((rows, GROUP), BF16),
        ((rows, width), BF16),
        ((heads, tiles, SPAN, GROUP), BF16),
    ]
    fresh = kept is None
    scratch = [
        pltpu.VMEM((parts, rows, feats), BF16),
        pltpu.VMEM(wqkv.shape, BF16),
        pltpu.VMEM(wo.shape, BF16),
        pltpu.VMEM((rows, width), F32),
        pltpu.VMEM((rows, width), BF16),
        pltpu.VMEM((rows, width), F32),
        pltpu.VMEM((rows, width), BF16),
        pltpu.VMEM((rows, width), BF16),
        pltpu.VMEM((rows, width), BF16),
        pltpu.VMEM((rows, GROUP), BF16),
        pltpu.VMEM((rows, width), BF16),
        pltpu.VMEM((heads, tiles, SPAN, GROUP), BF16),
        pltpu.VMEM((rows, width), BF16),
        pltpu.SemaphoreType.DMA((parts + 8,)),
    ]
    args = [*pieces, seg, pos, gain, shift, bias, down, up, wqkv, wo]
    aliases = {} if fresh else {len(args) + i: i for i in range(len(forms))}
    return pl.pallas_call(
        functools.partial(attend_kernel, parts=parts, unit=unit, fresh=fresh),
        out_shape=[jax.ShapeDtypeStruct((units, *shape), kind) for shape, kind in forms],
        in_specs=[ANY] * parts + [VMEM] * 7 + [ANY] * 2 + ([] if fresh else [ANY] * len(forms)),
        out_specs=[ANY] * len(forms),
        input_output_aliases=aliases,
        scratch_shapes=scratch,
        compiler_params=pltpu.CompilerParams(vmem_limit_bytes=58 * MIB),
        cost_estimate=pl.CostEstimate(
            flops=rows * width,
            bytes_accessed=MIB // 4,
            transcendentals=0,
        ),
        name="attend",
    )(*args, *([] if fresh else kept))


def finish_kernel(*refs, plan, arrays, parts):
    seg_ref, label_ref, gain_ref, shift_ref, bias_ref, head_ref, *refs = refs
    ffb_refs, wo_hbm, refs = refs[:parts], refs[parts], refs[parts + 1 :]
    weight_refs, refs = refs[:arrays], refs[arrays:]
    kept, refs = refs[:6], refs[6:]
    acc_ref, refs = refs[0], refs[1:]
    bufs, refs = refs[:6], refs[6:]
    wo, win, wout, xb, mixed, xh1, stat1, acc, slope, act, sems, wsems = refs
    resid2buf, k2, v2, red2, pr2, probs2 = bufs
    units = kept[0].shape[0]
    rows, width = xh1.shape
    hidden_part = win.shape[2]
    chunk = GROUP if hidden_part % GROUP == 0 else hidden_part
    groups = width // GROUP
    blocks = rows // BLOCK
    tiles = rows // GROUP
    row_steps = rows // STEP_ROWS
    half = lax.rem(lax.axis_index("dp"), 2)

    def weight_copies():
        made = []
        for i, (array, piece, matrix, r, mine) in enumerate(plan):
            src = weight_refs[array] if piece is None else weight_refs[array].at[piece]
            dst = (win, wout)[matrix].at[r]
            if mine is not None:
                n = dst.shape[0] // 2
                top = pl.multiple_of((half if mine else 1 - half) * n, 16)
                dst = (win, wout)[matrix].at[r, pl.ds(top, n), :]
            made.append(pltpu.make_async_copy(src, dst, wsems.at[i]))
        made.append(pltpu.make_async_copy(wo_hbm, wo, wsems.at[len(plan)]))
        return made

    def state_copies(u, slot):
        return [
            pltpu.make_async_copy(src.at[u], buf.at[slot], sems.at[slot, i])
            for i, (src, buf) in enumerate(zip(kept, bufs))
        ]

    for copy in state_copies(0, 0)[:1] + weight_copies() + state_copies(0, 0)[1:]:
        copy.start()

    gain1, gain2 = gain_ref[1:2], gain_ref[2:3]
    shift1, shift2 = shift_ref[1:2], shift_ref[2:3]
    head = head_ref[0:1, 0:width]
    head_bias = head_ref[0:1, width : width + 1]
    hg = head * gain2
    hg_mean = row_mean(hg)
    bias4 = bias_ref[4:5]
    base = jnp.sum(shift2 * head, axis=1, keepdims=True)
    in_head, keep = head_masks()
    acc_ref[...] = jnp.zeros(acc_ref.shape, F32)

    def unit(u, carry):
        slot = lax.rem(u, 2)
        now = state_copies(u, slot)

        @pl.when(u + 1 < units)
        def _():
            for copy in state_copies(u + 1, 1 - slot):
                copy.start()

        now[0].wait()

        def norm1(i, c):
            x = resid2buf[slot, at(i), :]
            off = x - row_mean(x)
            inv = lax.rsqrt(row_mean(off * off) + LN_EPS)
            xh = off * inv
            xh1[at(i), :] = xh
            stat1[at(i), :] = inv
            xb[at(i), :] = (xh * gain1 + shift1).astype(BF16)
            return c

        lax.fori_loop(0, row_steps, norm1, 0)

        @pl.when(u == 0)
        def _():
            for copy in weight_copies():
                copy.wait()

        for r in range(parts):
            for c in range(0, hidden_part, chunk):
                hid = slice(r * hidden_part + c, r * hidden_part + c + chunk)
                line, lane = units + c // rows, c % rows
                line_bias = ffb_refs[r][line : line + 1, lane : lane + chunk]
                pre = mm(xb[...], win[r, :, c : c + chunk]) + line_bias
                phi = 0.5 + 0.5 * lax.erf(pre * INV_SQRT2)
                act[:, hid] = (pre * phi).astype(BF16)
                slope[:, hid] = phi + pre * jnp.exp(-0.5 * pre * pre) * INV_SQRT_2PI
        for n in range(0, width, GROUP):
            acc[:, n : n + GROUP] = add_all(
                [
                    mm(act[:, r * hidden_part : (r + 1) * hidden_part], wout[r, :, n : n + GROUP])
                    for r in range(parts)
                ]
            )

        inv_cols = []
        dot_cols = []
        for i in range(row_steps):
            part = slice(i * STEP_ROWS, (i + 1) * STEP_ROWS)
            x = xh1[part, :] * gain1 + shift1 + (acc[part, :] + bias4)
            off = x - row_mean(x)
            inv = lax.rsqrt(row_mean(off * off) + LN_EPS)
            xh = off * inv
            acc[part, :] = xh
            inv_cols.append(inv)
            dot_cols.append(jnp.sum(xh * hg, axis=1, keepdims=True))
        inv2 = jnp.concatenate(inv_cols, axis=0)
        dots = jnp.concatenate(dot_cols, axis=0)

        seg_row = seg_ref[u].astype(F32)
        seg_col = segment_columns(seg_row)[2]
        label = label_ref[u]
        slots = label.shape[1]
        slot_no = lax.broadcasted_iota(jnp.int32, (rows, slots), 1).astype(F32)
        member = jnp.where(seg_col == slot_no, 1.0, 0.0)
        counts = jnp.sum(member, axis=0, keepdims=True)
        sums = jnp.sum(member * (dots + base), axis=0, keepdims=True)
        most = jnp.maximum(counts, 1.0)
        error = jnp.where(counts > 0, sums / most + head_bias - label, 0.0)
        grad_pred = 2.0 * error
        weight = jnp.sum(member * (grad_pred / most), axis=1, keepdims=True)
        loss = jnp.sum(error * error, axis=1, keepdims=True)
        weight_sum = jnp.sum(grad_pred, axis=1, keepdims=True)
        items = jnp.max(seg_row, axis=1, keepdims=True) + 1.0

        head_grad = jnp.zeros((8, width), F32)
        for i in range(row_steps):
            part = slice(i * STEP_ROWS, (i + 1) * STEP_ROWS)
            xh = acc[part, :]
            w = weight[part]
            weighted = xh * w
            for j in range(STEP_ROWS // 8):
                head_grad = head_grad + weighted[j * 8 : (j + 1) * 8]
            grad = (inv2[part] * w) * (hg - hg_mean - xh * (dots[part] * (1.0 / width)))
            acc[part, :] = grad
            xb[part, :] = grad.astype(BF16)
        head_grad = jnp.sum(head_grad, axis=0, keepdims=True) * gain2 + weight_sum * shift2
        acc_ref[16:17, :] += head_grad
        lane_row = lax.broadcasted_iota(jnp.int32, (1, width), 1)
        acc_ref[17:18, :] += jnp.where(
            lane_row == 0,
            loss,
            jnp.where(lane_row == 1, items, jnp.where(lane_row == 2, weight_sum, 0.0)),
        )

        for r in range(parts):
            for c in range(0, hidden_part, chunk):
                hid = slice(r * hidden_part + c, r * hidden_part + c + chunk)
                back = mm(xb[...], wout[r, c : c + chunk, :], NT)
                act[:, hid] = (back * slope[:, hid]).astype(BF16)
        for n in range(0, width, GROUP):
            acc[:, n : n + GROUP] = add_all(
                [acc[:, n : n + GROUP]]
                + [
                    mm(
                        act[:, r * hidden_part : (r + 1) * hidden_part],
                        win[r, n : n + GROUP, :],
                        NT,
                    )
                    for r in range(parts)
                ]
            )

        def back1(i, c):
            g = acc[at(i), :] * gain1
            xh = xh1[at(i), :]
            grad = stat1[at(i), :] * (g - row_mean(g) - xh * row_mean(g * xh))
            xb[at(i), :] = grad.astype(BF16)
            return c

        lax.fori_loop(0, row_steps, back1, 0)

        mixed[...] = mm(xb[...], wo[...], NT).astype(BF16)
        for copy in now[1:]:
            copy.wait()

        def attention_back(g, c):
            lanes = pl.ds(pl.multiple_of(g * GROUP, GROUP), GROUP)
            gg, kg = mixed[:, lanes], k2[slot, :, lanes]
            grads = stacked_scores(gg, v2[slot, :, lanes], keep)
            out = jnp.zeros((rows, GROUP), F32)
            for h in range(PER_GROUP):
                score_tiles = [[] for _ in range(tiles)]
                for b in range(blocks):
                    found = []
                    for t, lo, hi in block_pieces(b, blocks):
                        first, last = tile_rows(t, rows)
                        top = b * BLOCK - first
                        lane_at = slice((lo - 2 * t) * BLOCK, (hi + 1 - 2 * t) * BLOCK)
                        here = h * (last - first) + top
                        dp = grads[t][here : here + BLOCK, lane_at]
                        p = probs2[slot, g * PER_GROUP + h, t, top : top + BLOCK, lane_at]
                        found.append((p.astype(F32), dp))
                    shared = add_all([jnp.sum(p * dp, axis=1, keepdims=True) for p, dp in found])
                    for (t, lo, hi), (p, dp) in zip(block_pieces(b, blocks), found):
                        score_tiles[t].append(
                            spread((p * (dp - shared)).astype(BF16), t, lo, hi)
                        )
                res = tile_product([jnp.concatenate(tile, axis=0) for tile in score_tiles], kg)
                out = jnp.where(in_head[h], res, out)
            query_part = mm(red2[slot], out.astype(BF16), TN)[0:8]
            acc_ref[0:8, lanes] += query_part * (2.0 * HEAD_DIM**-0.5)
            cross = mm(pr2[slot, :, lanes], gg, TN)
            value_part = jnp.zeros((8, GROUP), F32)
            for h in range(PER_GROUP):
                top = ((h + 1) % PER_GROUP) * HEAD_DIM + 8
                value_part = jnp.where(in_head[h], cross[top : top + 8], value_part)
            acc_ref[8:16, lanes] += 2.0 * value_part
            return c

        lax.fori_loop(0, groups, attention_back, 0)
        return carry

    lax.fori_loop(0, units, unit, 0)


def finish_call(segs, labels, small, ffb, wo, arrays, plan, kept):
    gain, shift, bias, head = small
    parts = len(ffb)
    units, rows, width = kept[0].shape
    hidden_part = arrays[0].shape[1]
    hidden = hidden_part * parts
    scratch = [pltpu.VMEM((2, *a.shape[1:]), a.dtype) for a in kept]
    scratch += [
        pltpu.VMEM(wo.shape, BF16),
        pltpu.VMEM((parts, width, hidden_part), BF16),
        pltpu.VMEM((parts, hidden_part, width), BF16),
        pltpu.VMEM((rows, width), BF16),
        pltpu.VMEM((rows, width), BF16),
        pltpu.VMEM((rows, width), F32),
        pltpu.VMEM((rows, 1), F32),
        pltpu.VMEM((rows, width), F32),
        pltpu.VMEM((rows, hidden), F32),
        pltpu.VMEM((rows, hidden), BF16),
        pltpu.SemaphoreType.DMA((2, len(kept))),
        pltpu.SemaphoreType.DMA((len(plan) + 1,)),
    ]
    return pl.pallas_call(
        functools.partial(finish_kernel, plan=plan, arrays=len(arrays), parts=parts),
        out_shape=jax.ShapeDtypeStruct((ACC_ROWS, width), F32),
        in_specs=[VMEM] * (6 + parts) + [ANY] * (1 + len(arrays) + len(kept)),
        out_specs=VMEM,
        scratch_shapes=scratch,
        compiler_params=pltpu.CompilerParams(vmem_limit_bytes=62 * MIB),
        cost_estimate=pl.CostEstimate(
            flops=rows * width,
            bytes_accessed=MIB // 4,
            transcendentals=0,
        ),
        name="finish",
    )(segs, labels, gain, shift, bias, head, *ffb, wo, *arrays, *kept)


def update_kernel(
    acc_ref,
    other_ref,
    up_ref,
    momentum_ref,
    head_ref,
    first_ref,
    second_ref,
    loss_ref,
    items_ref,
    norm_ref,
    moment_out,
    up_out,
    low_out,
    first_out,
    second_out,
    head_out,
    head_low_out,
):
    total = acc_ref[...] + other_ref[...]
    width = total.shape[1]
    rank = up_ref.shape[0] // 2
    items = total[17:18, 1:2]
    loss_ref[...] = total[17:18, 0:1]
    items_ref[...] = items
    adapter = total[0:16] / items
    head_grad = jnp.concatenate([total[16:17], total[17:18, 2:3]], axis=1) / items
    norm = jnp.sqrt(jnp.sum(adapter * adapter) + jnp.sum(head_grad * head_grad))
    norm_ref[...] = jnp.full((1, 1), norm, F32)
    factor = jnp.minimum(1.0, CLIP_NORM / (norm_ref[...] + 1e-06))
    moment = ORTHO_MOMENTUM * momentum_ref[...] + factor * adapter
    moment_out[...] = moment

    def dot(left, right, dims=NN):
        return lax.dot_general(
            left, right, dims, preferred_element_type=F32, precision=lax.Precision.HIGHEST
        )

    basis = []
    for i in range(2):
        part = moment[i * rank : (i + 1) * rank]
        size = jnp.sqrt(jnp.sum(jnp.sum(part * part, axis=1, keepdims=True), axis=0, keepdims=True))
        basis.append(part / (size + 1e-07))
    for sweep in range(5):
        gram = [dot(x, x, NT) for x in basis]
        poly = [NS_B * g + NS_C * dot(g, g) for g in gram]
        basis = [NS_A * x + dot(p, x) for x, p in zip(basis, poly)]
    up = up_ref[...] - ORTHO_STEP_SIZE * jnp.concatenate(basis, axis=0)
    up_out[...] = up
    low_out[...] = up.astype(BF16)

    clipped = factor * head_grad
    first = BETA_ONE * first_ref[...] + (1.0 - BETA_ONE) * clipped
    second = BETA_TWO * second_ref[...] + (1.0 - BETA_TWO) * clipped * clipped
    first_hat = first / (1.0 - BETA_ONE**STEP)
    second_hat = second / (1.0 - BETA_TWO**STEP)
    head = head_ref[...]
    new_head = head - ADAM_RATE * (first_hat / (jnp.sqrt(second_hat) + ADAM_EPS) + DECAY * head)
    first_out[...] = first[0]
    second_out[...] = second[0]
    head_out[...] = new_head[0]
    head_low_out[...] = new_head[0].astype(BF16)


def update_call(acc, other, up, momentum, head, first, second):
    one = jax.ShapeDtypeStruct((1, 1), F32)
    flat = jax.ShapeDtypeStruct(up.shape, F32)
    row = jax.ShapeDtypeStruct(head.shape[1:], F32)
    return pl.pallas_call(
        update_kernel,
        out_shape=[
            one,
            one,
            one,
            flat,
            flat,
            jax.ShapeDtypeStruct(up.shape, BF16),
            row,
            row,
            row,
            jax.ShapeDtypeStruct(head.shape[1:], BF16),
        ],
        in_specs=[VMEM] * 7,
        out_specs=[VMEM] * 10,
        name="update",
    )(acc, other, up, momentum, head, first, second)


def swap(value, axis, bit):
    size = lax.axis_size(axis)
    return lax.ppermute(value, axis, [(i, i ^ bit) for i in range(size)])


class Weights:
    def __init__(self, owns):
        parts = lax.axis_size("tensor")
        half = lax.rem(lax.axis_index("dp"), 2)
        self.owns = owns
        cuts = []
        for own in owns:
            n = own.shape[0] // 2
            cuts.append(lax.dynamic_slice_in_dim(own, half * n, n, 0))
        self.one = cuts[0].shape == cuts[1].shape
        mine = {0: [jnp.stack(cuts)] if self.one else cuts}
        bit = parts // 2
        while bit > 1:
            mine.update({r ^ bit: [swap(a, "tensor", bit) for a in mine[r]] for r in list(mine)})
            bit //= 2
        del mine[0]
        self.mine = mine

    def core(self, pieces):
        return {r ^ 1: [swap(a, "tensor", 1) for a in arrays] for r, arrays in pieces.items()}

    def across(self, pieces):
        return {r: [swap(a, "dp", 1) for a in arrays] for r, arrays in pieces.items()}

    def operands(self):
        arrays, plan = list(self.owns) + list(self.core_own), []
        for i in range(2):
            plan += [(i, None, i, 0, None), (2 + i, None, i, 1, None)]
        for pieces, is_mine in (
            (self.mine, True),
            (self.core_mine, True),
            (self.other, False),
            (self.core_other, False),
        ):
            for r, found in pieces.items():
                for i in range(2):
                    if self.one:
                        plan.append((len(arrays), i, i, r, is_mine))
                    else:
                        plan.append((len(arrays) + i, None, i, r, is_mine))
                arrays += found
        plan.sort(key=lambda step: step[2])
        return arrays, tuple(plan)


def local(
    input_token_ids,
    segments,
    labels,
    embedding,
    position_embedding_table,
    norm_gain_rows,
    norm_shift_rows,
    query_key_value_weight,
    attention_output_weight,
    attention_bias_stack,
    feedforward_in_weight,
    feedforward_bias,
    feedforward_out_weight,
    adapter_down_weight,
    adapter_up_weight,
    adapter_momentum,
    head,
    head_first_moment,
    head_second_moment,
):
    length = input_token_ids.shape[-1]
    slots = labels.shape[-1]
    width = position_embedding_table.shape[1]
    rank = adapter_up_weight.shape[1]
    parts = lax.axis_size("tensor")
    ids = input_token_ids.reshape(-1, length)
    segs = segments.reshape(-1, 1, length)
    labs = labels.reshape(-1, 1, slots)
    units = ids.shape[0]

    hidden_part = feedforward_bias.shape[0]
    more = pl.cdiv(hidden_part, length)
    ffb = jnp.pad(feedforward_bias.astype(F32), (0, more * length - hidden_part))
    sent = jnp.concatenate([ids.astype(F32), ffb.reshape(more, length)], axis=0)
    sent = [sent] + [swap(sent, "tensor", r) for r in range(1, parts)]
    weights = Weights([feedforward_in_weight, feedforward_out_weight])

    down = jnp.concatenate(
        [
            adapter_down_weight[0],
            adapter_down_weight[1],
            jnp.zeros((width, HEAD_DIM - 2 * rank), BF16),
        ],
        axis=1,
    )
    down = jnp.concatenate([down] * PER_GROUP, axis=1)
    twice = 2.0 * adapter_up_weight.astype(BF16)
    up = jnp.stack(
        [
            jnp.pad(twice[0], ((0, GROUP - rank), (0, 0))),
            jnp.pad(twice[1], ((rank, GROUP - 2 * rank), (0, 0))),
        ]
    )
    head_rows = [head[None, :], head_first_moment[None, :], head_second_moment[None, :]]
    sent, owns, down, up, head_rows = lax.optimization_barrier(
        (sent, weights.owns, down, up, head_rows)
    )
    all_ids = [ids] + [a[:units].astype(jnp.int32) for a in sent[1:]]
    weights.core_own = [swap(own, "tensor", 1) for own in owns]
    picked = embed_call(all_ids, embedding)
    picked, weights.mine, weights.core_own = lax.optimization_barrier(
        (picked, weights.mine, weights.core_own)
    )
    weights.other = weights.across(weights.mine)
    weights.core_mine = weights.core(weights.mine)
    picked = [picked[u * parts : (u + 1) * parts] for u in range(units)]

    small = (
        position_embedding_table,
        norm_gain_rows,
        norm_shift_rows,
        attention_bias_stack,
        down,
        up,
    )
    kept = None
    moved = []
    for u in range(units):
        while len(moved) < min(u + 2, units):
            sends = picked[len(moved)][1:]
            if moved:
                sends = lax.optimization_barrier((sends, moved[-1], kept))[0]
            moved.append([swap(a, "tensor", r + 1) for r, a in enumerate(sends)])
        if u == 0:
            moved[0], weights.core_mine = lax.optimization_barrier((moved[0], weights.core_mine))
        kept = attend_call(
            [picked[u][0], *moved[u]],
            segs[u],
            small,
            query_key_value_weight,
            attention_output_weight,
            kept,
            u,
            units,
        )

    weights.core_other = weights.core(lax.optimization_barrier((weights.other, kept))[0])
    arrays, plan = weights.operands()
    acc = finish_call(
        segs,
        labs,
        (norm_gain_rows, norm_shift_rows, attention_bias_stack, head_rows[0]),
        sent,
        attention_output_weight,
        arrays,
        plan,
        kept,
    )
    steps = []
    for axis in ("tensor", "dp"):
        bit = 1
        while bit < lax.axis_size(axis):
            steps.append((axis, bit))
            bit *= 2
    for axis, bit in steps[:-1]:
        acc = acc + swap(acc, axis, bit)
    other = swap(acc, *steps[-1])

    flat = (2 * rank, width)
    outs = update_call(
        acc,
        other,
        adapter_up_weight.reshape(flat),
        adapter_momentum.reshape(flat),
        *head_rows,
    )
    loss, items, norm, moment, new_up, low, first, second, new_head, head_low = outs
    shape = adapter_up_weight.shape
    return (
        loss[0, 0],
        items[0, 0],
        norm[0, 0],
        moment.reshape(shape),
        new_up.reshape(shape),
        low.reshape(shape),
        first,
        second,
        new_head,
        head_low,
    )


def solution(mesh):
    rows = P(None, ("dp", "tensor"), None)
    placed = (
        (rows, rows, rows, P("tensor", None))
        + (P(),) * 6
        + (P(None, "tensor"), P("tensor"), P("tensor", None))
        + (P(),) * 6
    )
    return jax.shard_map(
        local, mesh=mesh, in_specs=placed, out_specs=(P(),) * 10, check_vma=False
    )
```

```python
import functools
import math

import jax
import jax.numpy as jnp
from jax import lax
from jax.experimental import pallas as pl
from jax.experimental.pallas import tpu as pltpu
from jax.sharding import PartitionSpec as P

HEAD_DIM = 64
STEP = 10
LN_EPS = 1e-05
CLIP_NORM = 0.5
ORTHO_MOMENTUM = 0.5
ORTHO_STEP_SIZE = 1.0
NS_A = 3.4445
NS_B = -4.775
NS_C = 2.0315
BETA_ONE = 0.9
BETA_TWO = 0.999
ADAM_RATE = 0.05
ADAM_EPS = 1e-08
DECAY = 0.01

F32 = jnp.float32
BF16 = jnp.bfloat16
LANES = 128
GROUP = 256
PER_GROUP = GROUP // HEAD_DIM
BLOCK = 128
SPAN = 3 * BLOCK
STEP_ROWS = 64
VOCAB_BLOCK = 2048
RING = 6
UNROLL = 64
ACC_ROWS = 24
BIAS_ROWS = 16
MIB = 1024 * 1024
NN = (((1,), (0,)), ((), ()))
NT = (((1,), (1,)), ((), ()))
TN = (((0,), (0,)), ((), ()))
INV_SQRT2 = 1.0 / math.sqrt(2.0)
INV_SQRT_2PI = 1.0 / math.sqrt(2.0 * math.pi)

VMEM = pl.BlockSpec(memory_space=pltpu.VMEM)
SMEM = pl.BlockSpec(memory_space=pltpu.SMEM)
ANY = pl.BlockSpec(memory_space=pl.ANY)


def mm(left, right, dims=NN):
    return lax.dot_general(left, right, dims, preferred_element_type=F32)


def row_mean(rows):
    return jnp.mean(rows, axis=-1, keepdims=True)


def add_all(terms):
    return functools.reduce(jnp.add, terms)


def at(i):
    return pl.ds(pl.multiple_of(i * STEP_ROWS, STEP_ROWS), STEP_ROWS)


def embed_kernel(*refs, parts, units):
    ids = refs[:parts]
    table, tail = refs[parts : parts + 2]
    outs = refs[parts + 2 : parts + 2 + parts * units]
    scratch = refs[parts + 2 + parts * units :]
    feats = table.shape[0]
    full = table.shape[1] // VOCAB_BLOCK
    lanes = [(lo, min(lo + LANES, feats)) for lo in range(0, feats, LANES)]
    turned = scratch[: len(lanes)]
    picked = scratch[len(lanes) : 2 * len(lanes)]
    ring, stage, ring_sems, sems = scratch[2 * len(lanes) :]

    def fetch(i):
        cols = pl.ds(pl.multiple_of(i * VOCAB_BLOCK, VOCAB_BLOCK), VOCAB_BLOCK)
        slot = lax.rem(i, RING)
        return pltpu.make_async_copy(table.at[:, cols], ring.at[slot], ring_sems.at[slot])

    def turn_block(base, block):
        for c in range(0, VOCAB_BLOCK, GROUP):
            rows_at = pl.ds(pl.multiple_of(base + c, GROUP), GROUP)
            for (lo, hi), turn in zip(lanes, turned):
                turn[rows_at, :] = block[lo:hi, c : c + GROUP].T.astype(F32)

    for i in range(min(RING, full)):
        fetch(i).start()
    turn_block(full * VOCAB_BLOCK, tail)

    def step(i, carry):
        fetch(i).wait()
        turn_block(i * VOCAB_BLOCK, ring.at[lax.rem(i, RING)])

        @pl.when(i + RING < full)
        def _():
            fetch(i + RING).start()

        return carry

    lax.fori_loop(0, full, step, 0)

    length = stage.shape[1]
    copies = []
    for p, out in enumerate(outs):
        u, r = p // parts, p % parts
        slot = p % 2

        def rows(i, carry, u=u, r=r):
            top = pl.multiple_of(i * UNROLL, UNROLL)
            for j in range(UNROLL):
                token = ids[r][u, 0, top + j]
                for turn, pick in zip(turned, picked):
                    pick[pl.ds(top + j, 1), :] = turn[pl.ds(token, 1), :]
            return carry

        lax.fori_loop(0, length // UNROLL, rows, 0)
        if p >= 2:
            copies[p - 2].wait()
        for (lo, hi), pick in zip(lanes, picked):
            stage[slot, :, lo:hi] = pick[...].astype(BF16)
        copies.append(pltpu.make_async_copy(stage.at[slot], out, sems.at[slot]))
        copies[p].start()
    for copy in copies[-2:]:
        copy.wait()


def embed_call(ids, table):
    parts = len(ids)
    units, _, length = ids[0].shape
    feats, vocab = table.shape
    full = vocab // VOCAB_BLOCK
    widths = [min(LANES, feats - lo) for lo in range(0, feats, LANES)]
    scratch = [pltpu.VMEM(((full + 1) * VOCAB_BLOCK, w), F32) for w in widths]
    scratch += [pltpu.VMEM((length, w), F32) for w in widths]
    scratch += [
        pltpu.VMEM((RING, feats, VOCAB_BLOCK), BF16),
        pltpu.VMEM((2, length, feats), BF16),
        pltpu.SemaphoreType.DMA((RING,)),
        pltpu.SemaphoreType.DMA((2,)),
    ]
    last = pl.cdiv(vocab, VOCAB_BLOCK) - 1
    tail = pl.BlockSpec((feats, VOCAB_BLOCK), lambda i: (0, last), pipeline_mode=pl.Buffered(1))
    return pl.pallas_call(
        functools.partial(embed_kernel, parts=parts, units=units),
        grid=(1,),
        in_specs=[SMEM] * parts + [ANY, tail],
        out_specs=[ANY] * (parts * units),
        out_shape=[jax.ShapeDtypeStruct((length, feats), BF16)] * (parts * units),
        scratch_shapes=scratch,
        compiler_params=pltpu.CompilerParams(vmem_limit_bytes=62 * MIB),
        name="embed",
    )(*ids, table, table)


def tile_rows(t, rows):
    lo = min(max(2 * t - 1, 0) * BLOCK, rows - min(SPAN, rows))
    return lo, min((2 * t + 3) * BLOCK, rows)


def block_pieces(b, blocks):
    first, last = max(b - 1, 0), min(b + 1, blocks - 1)
    found = []
    for t in range(blocks * BLOCK // GROUP):
        lo, hi = max(first, 2 * t), min(last, 2 * t + 1)
        if lo <= hi:
            found.append((t, lo, hi))
    return found


def spread(values, t, lo, hi):
    zero_block = jnp.zeros((BLOCK, BLOCK), BF16)
    parts = [values] if lo == 2 * t else [zero_block, values]
    if hi == 2 * t:
        parts.append(zero_block)
    return parts[0] if len(parts) == 1 else jnp.concatenate(parts, axis=1)


def head_masks():
    head_of = lax.broadcasted_iota(jnp.int32, (1, GROUP), 1) // HEAD_DIM
    in_head = [head_of == h for h in range(PER_GROUP)]
    return in_head, [jnp.where(m, 1.0, 0.0).astype(BF16) for m in in_head]


def column(row):
    return jnp.broadcast_to(row, (8, row.shape[1])).T[:, 0:1]


def tile_product(tiles, right):
    rows = right.shape[0]
    res = [None] * (rows // BLOCK)
    for t, left in enumerate(tiles):
        part = mm(left, right[t * GROUP : (t + 1) * GROUP])
        first = tile_rows(t, rows)[0] // BLOCK
        for i in range(left.shape[0] // BLOCK):
            piece = part[i * BLOCK : (i + 1) * BLOCK]
            res[first + i] = piece if res[first + i] is None else res[first + i] + piece
    return jnp.concatenate(res, axis=0)


def stacked_scores(left, right, keep):
    rows = left.shape[0]
    found = []
    for t in range(rows // GROUP):
        lo, hi = tile_rows(t, rows)
        stack = jnp.concatenate([left[lo:hi] * keep[h] for h in range(PER_GROUP)], axis=0)
        found.append(mm(stack, right[t * GROUP : (t + 1) * GROUP], NT))
    return found


def attend_kernel(*refs, parts, unit, fresh):
    pieces = refs[:parts]
    seg_ref, gain_ref, shift_ref, bias_ref, up_ref, pos_hbm, down_hbm, wqkv_hbm, wo_hbm = refs[
        parts : parts + 9
    ]
    refs = refs[parts + 9 + (0 if fresh else 6) :]
    outs, (x4, pos, down, wqkv, wo, start, xb, normed0, q, k, v, red, pr, probs, mixed, sems) = refs[:6], refs[6:]
    rows, width = normed0.shape
    groups = width // GROUP
    blocks = rows // BLOCK
    tiles = rows // GROUP
    row_steps = rows // STEP_ROWS
    me = lax.axis_index("tensor")

    in_copies = [
        pltpu.make_async_copy(piece, x4.at[jnp.bitwise_xor(me, r)], sems.at[r])
        for r, piece in enumerate(pieces)
    ]
    w_copies = [
        pltpu.make_async_copy(pos_hbm, pos, sems.at[parts]),
        pltpu.make_async_copy(down_hbm, down, sems.at[parts + 1]),
        pltpu.make_async_copy(wqkv_hbm, wqkv, sems.at[parts + 2]),
        pltpu.make_async_copy(wo_hbm, wo, sems.at[parts + 3]),
    ]
    out_copies = [
        pltpu.make_async_copy(ref, out.at[unit], sems.at[parts + 4 + i])
        for i, (ref, out) in enumerate(zip((start, k, v, red, pr), outs))
    ]

    def probs_copy(g):
        heads = pl.ds(g * PER_GROUP, PER_GROUP)
        return pltpu.make_async_copy(
            probs.at[heads], outs[5].at[unit, heads], sems.at[parts + 9 + g]
        )

    for copy in [w_copies[0], *in_copies, *w_copies[1:]]:
        copy.start()

    seg_row = seg_ref[...].astype(F32)
    seg_col = column(seg_row)
    lane = lax.broadcasted_iota(jnp.int32, (rows, rows), 1)
    sub = lax.broadcasted_iota(jnp.int32, (rows, rows), 0)
    before = (seg_col == seg_row) & (lane < sub)
    place = jnp.sum(jnp.where(before, 1.0, 0.0), axis=1, keepdims=True).astype(jnp.int32)
    one_hot = jnp.where(lane == place, 1.0, 0.0).astype(BF16)
    w_copies[0].wait()
    start[...] = mm(one_hot, pos[...])
    for copy in in_copies:
        copy.wait()
    start[...] += jnp.concatenate([x4[t] for t in range(parts)], axis=1).astype(F32)

    gain0, shift0 = gain_ref[0:1], shift_ref[0:1]

    def norm0(i, carry):
        x = start[at(i), :]
        off = x - row_mean(x)
        y = off * lax.rsqrt(row_mean(off * off) + LN_EPS) * gain0 + shift0
        normed0[at(i), :] = y
        xb[at(i), :] = y.astype(BF16)
        return carry

    lax.fori_loop(0, row_steps, norm0, 0, unroll=True)

    w_copies[1].wait()
    red[...] = mm(xb[...], down[...]).astype(BF16)
    out_copies[3].start()
    w_copies[2].wait()
    low_rows = red[:, 0 : up_ref.shape[1]]
    q[...] = (mm(xb[...], wqkv[0]) + bias_ref[0:1] + mm(low_rows, up_ref[0])).astype(BF16) * BF16(
        HEAD_DIM**-0.5
    )
    k[...] = (mm(xb[...], wqkv[1]) + bias_ref[1:2]).astype(BF16)
    out_copies[1].start()
    v[...] = (mm(xb[...], wqkv[2]) + bias_ref[2:3] + mm(low_rows, up_ref[1])).astype(BF16)
    out_copies[2].start()

    in_head, keep = head_masks()

    def far(b, c):
        hit = seg_col[b * BLOCK : (b + 1) * BLOCK] == seg_row[:, c * BLOCK : (c + 1) * BLOCK]
        return jnp.where(hit, 0.0, -1e9)

    away = {
        (b, c): far(b, c) for b in range(blocks) for c in range(max(b - 1, 0), min(b + 2, blocks))
    }

    def attention(g, carry):
        lanes = pl.ds(pl.multiple_of(g * GROUP, GROUP), GROUP)
        vg = v[:, lanes]
        scores = stacked_scores(q[:, lanes], k[:, lanes], keep)
        out = jnp.zeros((rows, GROUP), F32)
        low = jnp.zeros((rows, GROUP), F32)
        for h in range(PER_GROUP):
            vrh = vg * keep[h] + red[...] * (1 - keep[h])
            prob_tiles = [[] for _ in range(tiles)]
            for b in range(blocks):
                found = []
                for t, lo, hi in block_pieces(b, blocks):
                    first, last = tile_rows(t, rows)
                    top = h * (last - first) + b * BLOCK - first
                    s = scores[t][top : top + BLOCK, (lo - 2 * t) * BLOCK : (hi + 1 - 2 * t) * BLOCK]
                    found.append(
                        s + jnp.concatenate([away[b, c] for c in range(lo, hi + 1)], axis=1)
                    )
                peak = functools.reduce(
                    jnp.maximum, [jnp.max(s, axis=1, keepdims=True) for s in found]
                )
                found = [jnp.exp(s - peak) for s in found]
                inv = 1.0 / add_all([jnp.sum(s, axis=1, keepdims=True) for s in found])
                for (t, lo, hi), s in zip(block_pieces(b, blocks), found):
                    prob_tiles[t].append(spread((s * inv).astype(BF16), t, lo, hi))
            prob_tiles = [jnp.concatenate(tile, axis=0) for tile in prob_tiles]
            for t, tile in enumerate(prob_tiles):
                probs[g * PER_GROUP + h, t, 0 : tile.shape[0], :] = tile
            res = tile_product(prob_tiles, vrh)
            out = jnp.where(in_head[h], res, out)
            low = jnp.where(in_head[(h + 1) % PER_GROUP], res, low)
        mixed[:, lanes] = out.astype(BF16)
        pr[:, lanes] = low.astype(BF16)
        probs_copy(g).start()
        return carry

    lax.fori_loop(0, groups, attention, 0, unroll=True)
    out_copies[4].start()
    w_copies[3].wait()
    start[...] = normed0[...] + (mm(mixed[...], wo[...]) + bias_ref[3:4])
    out_copies[0].start()
    for copy in out_copies + [probs_copy(g) for g in range(groups)]:
        copy.wait()


def attend_call(pieces, seg, small, wqkv, wo, kept, unit, units):
    pos, gain, shift, bias, down, up = small
    parts = len(pieces)
    rows, feats = pieces[0].shape
    width = pos.shape[1]
    heads = width // HEAD_DIM
    tiles = rows // GROUP
    forms = [
        ((rows, width), F32),
        ((rows, width), BF16),
        ((rows, width), BF16),
        ((rows, GROUP), BF16),
        ((rows, width), BF16),
        ((heads, tiles, SPAN, GROUP), BF16),
    ]
    fresh = kept is None
    scratch = [
        pltpu.VMEM((parts, rows, feats), BF16),
        pltpu.VMEM(pos.shape, BF16),
        pltpu.VMEM(down.shape, BF16),
        pltpu.VMEM(wqkv.shape, BF16),
        pltpu.VMEM(wo.shape, BF16),
        pltpu.VMEM((rows, width), F32),
        pltpu.VMEM((rows, width), BF16),
        pltpu.VMEM((rows, width), F32),
        pltpu.VMEM((rows, width), BF16),
        pltpu.VMEM((rows, width), BF16),
        pltpu.VMEM((rows, width), BF16),
        pltpu.VMEM((rows, GROUP), BF16),
        pltpu.VMEM((rows, width), BF16),
        pltpu.VMEM((heads, tiles, SPAN, GROUP), BF16),
        pltpu.VMEM((rows, width), BF16),
        pltpu.SemaphoreType.DMA((parts + 9 + width // GROUP,)),
    ]
    args = [*pieces, seg, gain, shift, bias, up, pos, down, wqkv, wo]
    aliases = {} if fresh else {len(args) + i: i for i in range(len(forms))}
    return pl.pallas_call(
        functools.partial(attend_kernel, parts=parts, unit=unit, fresh=fresh),
        out_shape=[jax.ShapeDtypeStruct((units, *shape), kind) for shape, kind in forms],
        in_specs=[ANY] * parts + [VMEM] * 5 + [ANY] * 4 + ([] if fresh else [ANY] * len(forms)),
        out_specs=[ANY] * len(forms),
        input_output_aliases=aliases,
        scratch_shapes=scratch,
        compiler_params=pltpu.CompilerParams(vmem_limit_bytes=58 * MIB),
        cost_estimate=pl.CostEstimate(
            flops=rows * width,
            bytes_accessed=MIB // 4,
            transcendentals=0,
        ),
        name="attend",
    )(*args, *([] if fresh else kept))


def finish_kernel(*refs, plan, arrays, parts):
    seg_ref, label_ref, gain_ref, shift_ref, bias_ref, head_ref, *refs = refs
    wo_hbm, refs = refs[0], refs[1:]
    weight_refs, refs = refs[:arrays], refs[arrays:]
    kept, refs = refs[:6], refs[6:]
    acc_ref, refs = refs[0], refs[1:]
    bufs, refs = refs[:6], refs[6:]
    wo, win, wout, ffb, xb, mixed, xh1, stat1, acc, slope, act, sems, wsems = refs
    resid2buf, k2, v2, red2, pr2, probs2 = bufs
    units = kept[0].shape[0]
    rows, width = xh1.shape
    hidden_part = win.shape[2]
    chunk = GROUP if hidden_part % GROUP == 0 else hidden_part
    groups = width // GROUP
    blocks = rows // BLOCK
    tiles = rows // GROUP
    row_steps = rows // STEP_ROWS
    half = lax.rem(lax.axis_index("dp"), 2)

    def weight_copies():
        made = []
        for i, (matrix, array, first, n, r, mine) in enumerate(plan):
            src = weight_refs[array].at[pl.ds(first, n), :]
            dst = (win, wout, ffb)[matrix].at[r]
            if mine is not None:
                top = pl.multiple_of((half if mine else 1 - half) * n, 16)
                dst = (win, wout, ffb)[matrix].at[r, pl.ds(top, n), :]
            made.append(pltpu.make_async_copy(src, dst, wsems.at[i]))
        made.append(pltpu.make_async_copy(wo_hbm, wo, wsems.at[len(plan)]))
        return made

    def state_copies(u, slot):
        return [
            pltpu.make_async_copy(src.at[u], buf.at[slot], sems.at[slot, i])
            for i, (src, buf) in enumerate(zip(kept, bufs))
        ]

    for copy in state_copies(0, 0)[:1] + weight_copies() + state_copies(0, 0)[1:]:
        copy.start()

    gain1, gain2 = gain_ref[1:2], gain_ref[2:3]
    shift1, shift2 = shift_ref[1:2], shift_ref[2:3]
    head = head_ref[0:1, 0:width]
    head_bias = head_ref[0:1, width : width + 1]
    hg = head * gain2
    hg_mean = row_mean(hg)
    bias4 = bias_ref[4:5]
    base = jnp.sum(shift2 * head, axis=1, keepdims=True)
    in_head, keep = head_masks()
    acc_ref[...] = jnp.zeros(acc_ref.shape, F32)

    def unit(u, carry):
        slot = lax.rem(u, 2)
        now = state_copies(u, slot)

        @pl.when(u + 1 < units)
        def _():
            for copy in state_copies(u + 1, 1 - slot):
                copy.start()

        now[0].wait()

        def norm1(i, c):
            x = resid2buf[slot, at(i), :]
            off = x - row_mean(x)
            inv = lax.rsqrt(row_mean(off * off) + LN_EPS)
            xh = off * inv
            xh1[at(i), :] = xh
            stat1[at(i), :] = inv
            xb[at(i), :] = (xh * gain1 + shift1).astype(BF16)
            return c

        lax.fori_loop(0, row_steps, norm1, 0, unroll=True)

        @pl.when(u == 0)
        def _():
            for copy in weight_copies():
                copy.wait()

        for r in range(parts):
            for c in range(0, hidden_part, chunk):
                hid = slice(r * hidden_part + c, r * hidden_part + c + chunk)
                line = ffb[r, 0:1, c : c + chunk].astype(F32)
                pre = mm(xb[...], win[r, :, c : c + chunk]) + line
                phi = 0.5 + 0.5 * lax.erf(pre * INV_SQRT2)
                act[:, hid] = (pre * phi).astype(BF16)
                slope[:, hid] = phi + pre * jnp.exp(-0.5 * pre * pre) * INV_SQRT_2PI
        for n in range(0, width, GROUP):
            acc[:, n : n + GROUP] = add_all(
                [
                    mm(act[:, r * hidden_part : (r + 1) * hidden_part], wout[r, :, n : n + GROUP])
                    for r in range(parts)
                ]
            )

        inv_cols = []
        dot_cols = []
        for i in range(row_steps):
            part = slice(i * STEP_ROWS, (i + 1) * STEP_ROWS)
            x = xh1[part, :] * gain1 + shift1 + (acc[part, :] + bias4)
            off = x - row_mean(x)
            inv = lax.rsqrt(row_mean(off * off) + LN_EPS)
            xh = off * inv
            acc[part, :] = xh
            inv_cols.append(inv)
            dot_cols.append(jnp.sum(xh * hg, axis=1, keepdims=True))
        inv2 = jnp.concatenate(inv_cols, axis=0)
        dots = jnp.concatenate(dot_cols, axis=0)

        seg_row = seg_ref[u].astype(F32)
        seg_col = column(seg_row)
        label = label_ref[u]
        slots = label.shape[1]
        slot_no = lax.broadcasted_iota(jnp.int32, (rows, slots), 1).astype(F32)
        member = jnp.where(seg_col == slot_no, 1.0, 0.0)
        counts = jnp.sum(member, axis=0, keepdims=True)
        sums = jnp.sum(member * (dots + base), axis=0, keepdims=True)
        most = jnp.maximum(counts, 1.0)
        error = jnp.where(counts > 0, sums / most + head_bias - label, 0.0)
        grad_pred = 2.0 * error
        weight = jnp.sum(member * (grad_pred / most), axis=1, keepdims=True)
        loss = jnp.sum(error * error, axis=1, keepdims=True)
        weight_sum = jnp.sum(grad_pred, axis=1, keepdims=True)
        items = jnp.max(seg_row, axis=1, keepdims=True) + 1.0

        head_grad = jnp.zeros((8, width), F32)
        for i in range(row_steps):
            part = slice(i * STEP_ROWS, (i + 1) * STEP_ROWS)
            xh = acc[part, :]
            w = weight[part]
            weighted = xh * w
            for j in range(STEP_ROWS // 8):
                head_grad = head_grad + weighted[j * 8 : (j + 1) * 8]
            grad = (inv2[part] * w) * (hg - hg_mean - xh * (dots[part] * (1.0 / width)))
            acc[part, :] = grad
            xb[part, :] = grad.astype(BF16)
        head_grad = jnp.sum(head_grad, axis=0, keepdims=True) * gain2 + weight_sum * shift2
        acc_ref[16:17, :] += head_grad
        lane_row = lax.broadcasted_iota(jnp.int32, (1, width), 1)
        acc_ref[17:18, :] += jnp.where(
            lane_row == 0,
            loss,
            jnp.where(lane_row == 1, items, jnp.where(lane_row == 2, weight_sum, 0.0)),
        )

        for r in range(parts):
            for c in range(0, hidden_part, chunk):
                hid = slice(r * hidden_part + c, r * hidden_part + c + chunk)
                back = mm(xb[...], wout[r, c : c + chunk, :], NT)
                act[:, hid] = (back * slope[:, hid]).astype(BF16)
        for n in range(0, width, GROUP):
            acc[:, n : n + GROUP] = add_all(
                [acc[:, n : n + GROUP]]
                + [
                    mm(
                        act[:, r * hidden_part : (r + 1) * hidden_part],
                        win[r, n : n + GROUP, :],
                        NT,
                    )
                    for r in range(parts)
                ]
            )

        def back1(i, c):
            g = acc[at(i), :] * gain1
            xh = xh1[at(i), :]
            grad = stat1[at(i), :] * (g - row_mean(g) - xh * row_mean(g * xh))
            xb[at(i), :] = grad.astype(BF16)
            return c

        lax.fori_loop(0, row_steps, back1, 0, unroll=True)

        mixed[...] = mm(xb[...], wo[...], NT).astype(BF16)
        for copy in now[1:]:
            copy.wait()

        def attention_back(g, c):
            lanes = pl.ds(pl.multiple_of(g * GROUP, GROUP), GROUP)
            gg, kg = mixed[:, lanes], k2[slot, :, lanes]
            grads = stacked_scores(gg, v2[slot, :, lanes], keep)
            out = jnp.zeros((rows, GROUP), F32)
            for h in range(PER_GROUP):
                score_tiles = [[] for _ in range(tiles)]
                for b in range(blocks):
                    found = []
                    for t, lo, hi in block_pieces(b, blocks):
                        first, last = tile_rows(t, rows)
                        top = b * BLOCK - first
                        lane_at = slice((lo - 2 * t) * BLOCK, (hi + 1 - 2 * t) * BLOCK)
                        here = h * (last - first) + top
                        dp = grads[t][here : here + BLOCK, lane_at]
                        p = probs2[slot, g * PER_GROUP + h, t, top : top + BLOCK, lane_at]
                        found.append((p.astype(F32), dp))
                    shared = add_all([jnp.sum(p * dp, axis=1, keepdims=True) for p, dp in found])
                    for (t, lo, hi), (p, dp) in zip(block_pieces(b, blocks), found):
                        score_tiles[t].append(
                            spread((p * (dp - shared)).astype(BF16), t, lo, hi)
                        )
                res = tile_product([jnp.concatenate(tile, axis=0) for tile in score_tiles], kg)
                out = jnp.where(in_head[h], res, out)
            query_part = mm(red2[slot], out.astype(BF16), TN)[0:8]
            acc_ref[0:8, lanes] += query_part * (2.0 * HEAD_DIM**-0.5)
            cross = mm(pr2[slot, :, lanes], gg, TN)
            value_part = jnp.zeros((8, GROUP), F32)
            for h in range(PER_GROUP):
                top = ((h + 1) % PER_GROUP) * HEAD_DIM + 8
                value_part = jnp.where(in_head[h], cross[top : top + 8], value_part)
            acc_ref[8:16, lanes] += 2.0 * value_part
            return c

        lax.fori_loop(0, groups, attention_back, 0, unroll=True)
        return carry

    lax.fori_loop(0, units, unit, 0)


def finish_call(segs, labels, small, wo, arrays, plan, kept, parts):
    gain, shift, bias, head = small
    units, rows, width = kept[0].shape
    hidden_part = arrays[0].shape[1]
    hidden = hidden_part * parts
    scratch = [pltpu.VMEM((2, *a.shape[1:]), a.dtype) for a in kept]
    scratch += [
        pltpu.VMEM(wo.shape, BF16),
        pltpu.VMEM((parts, width, hidden_part), BF16),
        pltpu.VMEM((parts, hidden_part, width), BF16),
        pltpu.VMEM((parts, BIAS_ROWS, hidden_part), BF16),
        pltpu.VMEM((rows, width), BF16),
        pltpu.VMEM((rows, width), BF16),
        pltpu.VMEM((rows, width), F32),
        pltpu.VMEM((rows, 1), F32),
        pltpu.VMEM((rows, width), F32),
        pltpu.VMEM((rows, hidden), F32),
        pltpu.VMEM((rows, hidden), BF16),
        pltpu.SemaphoreType.DMA((2, len(kept))),
        pltpu.SemaphoreType.DMA((len(plan) + 1,)),
    ]
    return pl.pallas_call(
        functools.partial(finish_kernel, plan=plan, arrays=len(arrays), parts=parts),
        out_shape=jax.ShapeDtypeStruct((ACC_ROWS, width), F32),
        in_specs=[VMEM] * 6 + [ANY] * (1 + len(arrays) + len(kept)),
        out_specs=VMEM,
        scratch_shapes=scratch,
        compiler_params=pltpu.CompilerParams(vmem_limit_bytes=62 * MIB),
        cost_estimate=pl.CostEstimate(
            flops=rows * width,
            bytes_accessed=MIB // 4,
            transcendentals=0,
        ),
        name="finish",
    )(segs, labels, gain, shift, bias, head, wo, *arrays, *kept)


def update_kernel(
    acc_ref,
    other_ref,
    up_ref,
    momentum_ref,
    head_ref,
    first_ref,
    second_ref,
    loss_ref,
    items_ref,
    norm_ref,
    moment_out,
    up_out,
    low_out,
    first_out,
    second_out,
    head_out,
    head_low_out,
):
    total = acc_ref[...] + other_ref[...]
    width = total.shape[1]
    rank = up_ref.shape[0] // 2
    items = total[17:18, 1:2]
    loss_ref[...] = total[17:18, 0:1]
    items_ref[...] = items
    adapter = total[0:16] / items
    head_grad = jnp.concatenate([total[16:17], total[17:18, 2:3]], axis=1) / items
    norm = jnp.sqrt(jnp.sum(adapter * adapter) + jnp.sum(head_grad * head_grad))
    norm_ref[...] = jnp.full((1, 1), norm, F32)
    factor = jnp.minimum(1.0, CLIP_NORM / (norm_ref[...] + 1e-06))
    moment = ORTHO_MOMENTUM * momentum_ref[...] + factor * adapter
    moment_out[...] = moment

    def dot(left, right, dims=NN):
        return lax.dot_general(
            left, right, dims, preferred_element_type=F32, precision=lax.Precision.HIGHEST
        )

    basis = []
    for i in range(2):
        part = moment[i * rank : (i + 1) * rank]
        size = jnp.sqrt(jnp.sum(jnp.sum(part * part, axis=1, keepdims=True), axis=0, keepdims=True))
        basis.append(part / (size + 1e-07))
    for sweep in range(5):
        gram = [dot(x, x, NT) for x in basis]
        poly = [NS_B * g + NS_C * dot(g, g) for g in gram]
        basis = [NS_A * x + dot(p, x) for x, p in zip(basis, poly)]
    up = up_ref[...] - ORTHO_STEP_SIZE * jnp.concatenate(basis, axis=0)
    up_out[...] = up
    low_out[...] = up.astype(BF16)

    clipped = factor * head_grad
    first = BETA_ONE * first_ref[...] + (1.0 - BETA_ONE) * clipped
    second = BETA_TWO * second_ref[...] + (1.0 - BETA_TWO) * clipped * clipped
    first_hat = first / (1.0 - BETA_ONE**STEP)
    second_hat = second / (1.0 - BETA_TWO**STEP)
    head = head_ref[...]
    new_head = head - ADAM_RATE * (first_hat / (jnp.sqrt(second_hat) + ADAM_EPS) + DECAY * head)
    first_out[...] = first[0]
    second_out[...] = second[0]
    head_out[...] = new_head[0]
    head_low_out[...] = new_head[0].astype(BF16)


def update_call(acc, other, up, momentum, head, first, second):
    one = jax.ShapeDtypeStruct((1, 1), F32)
    flat = jax.ShapeDtypeStruct(up.shape, F32)
    row = jax.ShapeDtypeStruct(head.shape[1:], F32)
    return pl.pallas_call(
        update_kernel,
        out_shape=[
            one,
            one,
            one,
            flat,
            flat,
            jax.ShapeDtypeStruct(up.shape, BF16),
            row,
            row,
            row,
            jax.ShapeDtypeStruct(head.shape[1:], BF16),
        ],
        in_specs=[VMEM] * 7,
        out_specs=[VMEM] * 10,
        name="update",
    )(acc, other, up, momentum, head, first, second)


def swap(value, axis, bit):
    size = lax.axis_size(axis)
    return lax.ppermute(value, axis, [(i, i ^ bit) for i in range(size)])


class Weights:
    def __init__(self, owns, bias):
        parts = lax.axis_size("tensor")
        half = lax.rem(lax.axis_index("dp"), 2)
        self.owns = owns
        self.sizes = [own.shape[0] // 2 for own in owns]
        self.bias = jnp.pad(bias[None, :], ((0, BIAS_ROWS - 1), (0, 0)))
        cuts = [
            lax.dynamic_slice_in_dim(own, half * n, n, 0) for own, n in zip(owns, self.sizes)
        ]
        if cuts[0].shape[1] == cuts[1].shape[1]:
            cuts = [jnp.concatenate([*cuts, self.bias], axis=0)]
        else:
            cuts.append(self.bias)
        self.one = len(cuts) == 1
        mine = {0: cuts}
        bit = parts // 2
        while bit > 1:
            mine.update({r ^ bit: [swap(a, "tensor", bit) for a in mine[r]] for r in list(mine)})
            bit //= 2
        del mine[0]
        self.mine = mine

    def core(self, pieces):
        return {r ^ 1: [swap(a, "tensor", 1) for a in arrays] for r, arrays in pieces.items()}

    def across(self, pieces):
        return {r: [swap(a, "dp", 1) for a in arrays] for r, arrays in pieces.items()}

    def operands(self):
        arrays = [*self.owns, *self.core_own, self.bias, self.core_bias]
        plan = [(2, 4, 0, BIAS_ROWS, 0, None), (2, 5, 0, BIAS_ROWS, 1, None)]
        for i in range(2):
            n = 2 * self.sizes[i]
            plan += [(i, i, 0, n, 0, None), (i, 2 + i, 0, n, 1, None)]
        for pieces, is_mine in (
            (self.mine, True),
            (self.core_mine, True),
            (self.other, False),
            (self.core_other, False),
        ):
            for r, found in pieces.items():
                first = 0
                for i, n in enumerate([*self.sizes, BIAS_ROWS]):
                    array = len(arrays) + (0 if self.one else i)
                    if i < 2:
                        plan.append((i, array, first, n, r, is_mine))
                    elif is_mine:
                        plan.append((i, array, first, n, r, None))
                    first += n if self.one else 0
                arrays += found
        return arrays, tuple(sorted(plan, key=lambda step: step[0]))


def local(
    input_token_ids,
    segments,
    labels,
    embedding,
    position_embedding_table,
    norm_gain_rows,
    norm_shift_rows,
    query_key_value_weight,
    attention_output_weight,
    attention_bias_stack,
    feedforward_in_weight,
    feedforward_bias,
    feedforward_out_weight,
    adapter_down_weight,
    adapter_up_weight,
    adapter_momentum,
    head,
    head_first_moment,
    head_second_moment,
):
    length = input_token_ids.shape[-1]
    slots = labels.shape[-1]
    width = position_embedding_table.shape[1]
    rank = adapter_up_weight.shape[1]
    parts = lax.axis_size("tensor")
    ids = input_token_ids.reshape(-1, 1, length)
    all_ids = [ids] + [swap(ids, "tensor", r) for r in range(1, parts)]
    segs = segments.reshape(-1, 1, length)
    labs = labels.reshape(-1, 1, slots)
    units = ids.shape[0]

    weights = Weights([feedforward_in_weight, feedforward_out_weight], feedforward_bias)

    all_ids, owns, bias = lax.optimization_barrier((all_ids, weights.owns, weights.bias))
    weights.core_own = [swap(own, "tensor", 1) for own in owns]
    weights.core_bias = swap(bias, "tensor", 1)
    picked = embed_call(all_ids, embedding)
    (
        picked,
        weights.mine,
        weights.core_own,
        weights.core_bias,
        adapter_down_weight,
        adapter_up_weight,
        head_rows,
    ) = lax.optimization_barrier(
        (
            picked,
            weights.mine,
            weights.core_own,
            weights.core_bias,
            adapter_down_weight,
            adapter_up_weight,
            (head, head_first_moment, head_second_moment),
        )
    )
    head_rows = [a[None, :] for a in head_rows]
    weights.other = weights.across(weights.mine)
    weights.core_mine = weights.core(weights.mine)
    down = jnp.concatenate(
        [
            adapter_down_weight[0],
            adapter_down_weight[1],
            jnp.zeros((width, HEAD_DIM - 2 * rank), BF16),
        ],
        axis=1,
    )
    down = jnp.concatenate([down] * PER_GROUP, axis=1)
    twice = 2.0 * adapter_up_weight.astype(BF16)
    up = jnp.stack(
        [jnp.pad(twice[0], ((0, rank), (0, 0))), jnp.pad(twice[1], ((rank, 0), (0, 0)))]
    )
    picked = [picked[u * parts : (u + 1) * parts] for u in range(units)]

    small = (
        position_embedding_table,
        norm_gain_rows,
        norm_shift_rows,
        attention_bias_stack,
        down,
        up,
    )
    kept = None
    moved = []
    for u in range(units):
        while len(moved) < min(u + 2, units):
            sends = picked[len(moved)][1:]
            if moved:
                sends = lax.optimization_barrier((sends, moved[-1], kept))[0]
            moved.append([swap(a, "tensor", r + 1) for r, a in enumerate(sends)])
        if u == 0:
            moved[0], weights.core_mine = lax.optimization_barrier((moved[0], weights.core_mine))
        kept = attend_call(
            [picked[u][0], *moved[u]],
            segs[u],
            small,
            query_key_value_weight,
            attention_output_weight,
            kept,
            u,
            units,
        )

    weights.core_other = weights.core(lax.optimization_barrier((weights.other, kept))[0])
    arrays, plan = weights.operands()
    acc = finish_call(
        segs,
        labs,
        (norm_gain_rows, norm_shift_rows, attention_bias_stack, head_rows[0]),
        attention_output_weight,
        arrays,
        plan,
        kept,
        parts,
    )
    steps = []
    for axis in ("tensor", "dp"):
        bit = 1
        while bit < lax.axis_size(axis):
            steps.append((axis, bit))
            bit *= 2
    for axis, bit in steps[:-1]:
        acc = acc + swap(acc, axis, bit)
    other = swap(acc, *steps[-1])

    flat = (2 * rank, width)
    outs = update_call(
        acc,
        other,
        adapter_up_weight.reshape(flat),
        adapter_momentum.reshape(flat),
        *head_rows,
    )
    loss, items, norm, moment, new_up, low, first, second, new_head, head_low = outs
    shape = adapter_up_weight.shape
    return (
        loss[0, 0],
        items[0, 0],
        norm[0, 0],
        moment.reshape(shape),
        new_up.reshape(shape),
        low.reshape(shape),
        first,
        second,
        new_head,
        head_low,
    )


def solution(mesh):
    rows = P(None, ("dp", "tensor"), None)
    placed = (
        (rows, rows, rows, P("tensor", None))
        + (P(),) * 6
        + (P(None, "tensor"), P("tensor"), P("tensor", None))
        + (P(),) * 6
    )
    return jax.shard_map(
        local, mesh=mesh, in_specs=placed, out_specs=(P(),) * 10, check_vma=False
    )
```

```python
import functools
import math

import jax
import jax.numpy as jnp
from jax import lax
from jax.experimental import pallas as pl
from jax.experimental.pallas import tpu as pltpu
from jax.sharding import PartitionSpec as P

HEAD_DIM = 64
STEP = 10
LN_EPS = 1e-05
CLIP_NORM = 0.5
ORTHO_MOMENTUM = 0.5
ORTHO_STEP_SIZE = 1.0
NS_A = 3.4445
NS_B = -4.775
NS_C = 2.0315
BETA_ONE = 0.9
BETA_TWO = 0.999
ADAM_RATE = 0.05
ADAM_EPS = 1e-08
DECAY = 0.01

F32 = jnp.float32
BF16 = jnp.bfloat16
LANES = 128
GROUP = 256
PER_GROUP = GROUP // HEAD_DIM
BLOCK = 128
SPAN = 3 * BLOCK
STEP_ROWS = 64
VOCAB_BLOCK = 2048
RING = 6
UNROLL = 64
ACC_ROWS = 24
BIAS_ROWS = 16
MIB = 1024 * 1024
NN = (((1,), (0,)), ((), ()))
NT = (((1,), (1,)), ((), ()))
TN = (((0,), (0,)), ((), ()))
INV_SQRT2 = 1.0 / math.sqrt(2.0)
INV_SQRT_2PI = 1.0 / math.sqrt(2.0 * math.pi)

VMEM = pl.BlockSpec(memory_space=pltpu.VMEM)
SMEM = pl.BlockSpec(memory_space=pltpu.SMEM)
ANY = pl.BlockSpec(memory_space=pl.ANY)


def mm(left, right, dims=NN):
    return lax.dot_general(left, right, dims, preferred_element_type=F32)


def row_mean(rows):
    return jnp.mean(rows, axis=-1, keepdims=True)


def add_all(terms):
    return functools.reduce(jnp.add, terms)


def at(i):
    return pl.ds(pl.multiple_of(i * STEP_ROWS, STEP_ROWS), STEP_ROWS)


def embed_kernel(*refs, parts, units):
    ids = refs[:parts]
    table, tail = refs[parts : parts + 2]
    outs = refs[parts + 2 : parts + 2 + parts * units]
    scratch = refs[parts + 2 + parts * units :]
    feats = table.shape[0]
    full = table.shape[1] // VOCAB_BLOCK
    lanes = [(lo, min(lo + LANES, feats)) for lo in range(0, feats, LANES)]
    turned = scratch[: len(lanes)]
    picked = scratch[len(lanes) : 2 * len(lanes)]
    ring, stage, ring_sems, sems = scratch[2 * len(lanes) :]

    def fetch(i):
        cols = pl.ds(pl.multiple_of(i * VOCAB_BLOCK, VOCAB_BLOCK), VOCAB_BLOCK)
        slot = lax.rem(i, RING)
        return pltpu.make_async_copy(table.at[:, cols], ring.at[slot], ring_sems.at[slot])

    def turn_block(base, block):
        for c in range(0, VOCAB_BLOCK, GROUP):
            rows_at = pl.ds(pl.multiple_of(base + c, GROUP), GROUP)
            for (lo, hi), turn in zip(lanes, turned):
                turn[rows_at, :] = block[lo:hi, c : c + GROUP].T.astype(F32)

    for i in range(min(RING, full)):
        fetch(i).start()
    turn_block(full * VOCAB_BLOCK, tail)

    def step(i, carry):
        fetch(i).wait()
        turn_block(i * VOCAB_BLOCK, ring.at[lax.rem(i, RING)])

        @pl.when(i + RING < full)
        def _():
            fetch(i + RING).start()

        return carry

    lax.fori_loop(0, full, step, 0)

    length = stage.shape[1]
    copies = []
    for p, out in enumerate(outs):
        u, r = p // parts, p % parts
        slot = p % 2

        def rows(i, carry, u=u, r=r):
            top = pl.multiple_of(i * UNROLL, UNROLL)
            for j in range(UNROLL):
                token = ids[r][u, 0, top + j]
                for turn, pick in zip(turned, picked):
                    pick[pl.ds(top + j, 1), :] = turn[pl.ds(token, 1), :]
            return carry

        lax.fori_loop(0, length // UNROLL, rows, 0)
        if p >= 2:
            copies[p - 2].wait()
        for (lo, hi), pick in zip(lanes, picked):
            stage[slot, :, lo:hi] = pick[...].astype(BF16)
        copies.append(pltpu.make_async_copy(stage.at[slot], out, sems.at[slot]))
        copies[p].start()
    for copy in copies[-2:]:
        copy.wait()


def embed_call(ids, table):
    parts = len(ids)
    units, _, length = ids[0].shape
    feats, vocab = table.shape
    full = vocab // VOCAB_BLOCK
    widths = [min(LANES, feats - lo) for lo in range(0, feats, LANES)]
    scratch = [pltpu.VMEM(((full + 1) * VOCAB_BLOCK, w), F32) for w in widths]
    scratch += [pltpu.VMEM((length, w), F32) for w in widths]
    scratch += [
        pltpu.VMEM((RING, feats, VOCAB_BLOCK), BF16),
        pltpu.VMEM((2, length, feats), BF16),
        pltpu.SemaphoreType.DMA((RING,)),
        pltpu.SemaphoreType.DMA((2,)),
    ]
    last = pl.cdiv(vocab, VOCAB_BLOCK) - 1
    tail = pl.BlockSpec((feats, VOCAB_BLOCK), lambda i: (0, last), pipeline_mode=pl.Buffered(1))
    return pl.pallas_call(
        functools.partial(embed_kernel, parts=parts, units=units),
        grid=(1,),
        in_specs=[SMEM] * parts + [ANY, tail],
        out_specs=[ANY] * (parts * units),
        out_shape=[jax.ShapeDtypeStruct((length, feats), BF16)] * (parts * units),
        scratch_shapes=scratch,
        compiler_params=pltpu.CompilerParams(vmem_limit_bytes=62 * MIB),
        name="embed",
    )(*ids, table, table)


def tile_rows(t, rows):
    lo = min(max(2 * t - 1, 0) * BLOCK, rows - min(SPAN, rows))
    return lo, min((2 * t + 3) * BLOCK, rows)


def block_pieces(b, blocks):
    first, last = max(b - 1, 0), min(b + 1, blocks - 1)
    found = []
    for t in range(blocks * BLOCK // GROUP):
        lo, hi = max(first, 2 * t), min(last, 2 * t + 1)
        if lo <= hi:
            found.append((t, lo, hi))
    return found


def spread(values, t, lo, hi):
    zero_block = jnp.zeros((BLOCK, BLOCK), BF16)
    parts = [values] if lo == 2 * t else [zero_block, values]
    if hi == 2 * t:
        parts.append(zero_block)
    return parts[0] if len(parts) == 1 else jnp.concatenate(parts, axis=1)


def head_masks():
    head_of = lax.broadcasted_iota(jnp.int32, (1, GROUP), 1) // HEAD_DIM
    in_head = [head_of == h for h in range(PER_GROUP)]
    return in_head, [jnp.where(m, 1.0, 0.0).astype(BF16) for m in in_head]


def column(row):
    return jnp.broadcast_to(row, (8, row.shape[1])).T[:, 0:1]


def tile_product(tiles, right):
    rows = right.shape[0]
    res = [None] * (rows // BLOCK)
    for t, left in enumerate(tiles):
        part = mm(left, right[t * GROUP : (t + 1) * GROUP])
        first = tile_rows(t, rows)[0] // BLOCK
        for i in range(left.shape[0] // BLOCK):
            piece = part[i * BLOCK : (i + 1) * BLOCK]
            res[first + i] = piece if res[first + i] is None else res[first + i] + piece
    return jnp.concatenate(res, axis=0)


def stacked_scores(left, right, keep):
    rows = left.shape[0]
    found = []
    for t in range(rows // GROUP):
        lo, hi = tile_rows(t, rows)
        stack = jnp.concatenate([left[lo:hi] * keep[h] for h in range(PER_GROUP)], axis=0)
        found.append(mm(stack, right[t * GROUP : (t + 1) * GROUP], NT))
    return found


def attend_kernel(*refs, parts, unit, fresh):
    pieces = refs[:parts]
    seg_ref, gain_ref, shift_ref, bias_ref, up_ref, pos_hbm, down_hbm, wqkv_hbm, wo_hbm = refs[
        parts : parts + 9
    ]
    refs = refs[parts + 9 + (0 if fresh else 6) :]
    outs, (x4, pos, down, wqkv, wo, start, xb, normed0, q, k, v, red, pr, probs, mixed, sems) = refs[:6], refs[6:]
    rows, width = normed0.shape
    groups = width // GROUP
    blocks = rows // BLOCK
    tiles = rows // GROUP
    row_steps = rows // STEP_ROWS
    me = lax.axis_index("tensor")

    in_copies = [
        pltpu.make_async_copy(piece, x4.at[jnp.bitwise_xor(me, r)], sems.at[r])
        for r, piece in enumerate(pieces)
    ]
    w_copies = [
        pltpu.make_async_copy(pos_hbm, pos, sems.at[parts]),
        pltpu.make_async_copy(down_hbm, down, sems.at[parts + 1]),
        pltpu.make_async_copy(wqkv_hbm, wqkv, sems.at[parts + 2]),
        pltpu.make_async_copy(wo_hbm, wo, sems.at[parts + 3]),
    ]
    out_copies = [
        pltpu.make_async_copy(ref, out.at[unit], sems.at[parts + 4 + i])
        for i, (ref, out) in enumerate(zip((start, k, v, red, pr), outs))
    ]

    def probs_copy(g):
        heads = pl.ds(g * PER_GROUP, PER_GROUP)
        return pltpu.make_async_copy(
            probs.at[heads], outs[5].at[unit, heads], sems.at[parts + 9 + g]
        )

    for copy in [w_copies[0], *in_copies, *w_copies[1:]]:
        copy.start()

    seg_row = seg_ref[...].astype(F32)
    seg_col = column(seg_row)
    lane = lax.broadcasted_iota(jnp.int32, (rows, rows), 1)
    sub = lax.broadcasted_iota(jnp.int32, (rows, rows), 0)
    before = (seg_col == seg_row) & (lane < sub)
    place = jnp.sum(jnp.where(before, 1.0, 0.0), axis=1, keepdims=True).astype(jnp.int32)
    one_hot = jnp.where(lane == place, 1.0, 0.0).astype(BF16)
    w_copies[0].wait()
    start[...] = mm(one_hot, pos[...])
    for copy in in_copies:
        copy.wait()
    start[...] += jnp.concatenate([x4[t] for t in range(parts)], axis=1).astype(F32)

    gain0, shift0 = gain_ref[0:1], shift_ref[0:1]

    def norm0(i, carry):
        x = start[at(i), :]
        off = x - row_mean(x)
        y = off * lax.rsqrt(row_mean(off * off) + LN_EPS) * gain0 + shift0
        normed0[at(i), :] = y
        xb[at(i), :] = y.astype(BF16)
        return carry

    lax.fori_loop(0, row_steps, norm0, 0, unroll=True)

    w_copies[1].wait()
    red[...] = mm(xb[...], down[...]).astype(BF16)
    out_copies[3].start()
    w_copies[2].wait()
    low_rows = red[:, 0 : up_ref.shape[1]]
    q[...] = (mm(xb[...], wqkv[0]) + bias_ref[0:1] + mm(low_rows, up_ref[0])).astype(BF16) * BF16(
        HEAD_DIM**-0.5
    )
    k[...] = (mm(xb[...], wqkv[1]) + bias_ref[1:2]).astype(BF16)
    out_copies[1].start()
    v[...] = (mm(xb[...], wqkv[2]) + bias_ref[2:3] + mm(low_rows, up_ref[1])).astype(BF16)
    out_copies[2].start()

    in_head, keep = head_masks()

    def far(b, c):
        hit = seg_col[b * BLOCK : (b + 1) * BLOCK] == seg_row[:, c * BLOCK : (c + 1) * BLOCK]
        return jnp.where(hit, 0.0, -1e9)

    away = {
        (b, c): far(b, c) for b in range(blocks) for c in range(max(b - 1, 0), min(b + 2, blocks))
    }

    def attention(g, carry):
        lanes = pl.ds(pl.multiple_of(g * GROUP, GROUP), GROUP)
        vg = v[:, lanes]
        scores = stacked_scores(q[:, lanes], k[:, lanes], keep)
        out = jnp.zeros((rows, GROUP), F32)
        low = jnp.zeros((rows, GROUP), F32)
        for h in range(PER_GROUP):
            vrh = vg * keep[h] + red[...] * (1 - keep[h])
            prob_tiles = [[] for _ in range(tiles)]
            for b in range(blocks):
                found = []
                for t, lo, hi in block_pieces(b, blocks):
                    first, last = tile_rows(t, rows)
                    top = h * (last - first) + b * BLOCK - first
                    s = scores[t][top : top + BLOCK, (lo - 2 * t) * BLOCK : (hi + 1 - 2 * t) * BLOCK]
                    found.append(
                        s + jnp.concatenate([away[b, c] for c in range(lo, hi + 1)], axis=1)
                    )
                peak = functools.reduce(
                    jnp.maximum, [jnp.max(s, axis=1, keepdims=True) for s in found]
                )
                found = [jnp.exp(s - peak) for s in found]
                inv = 1.0 / add_all([jnp.sum(s, axis=1, keepdims=True) for s in found])
                for (t, lo, hi), s in zip(block_pieces(b, blocks), found):
                    prob_tiles[t].append(spread((s * inv).astype(BF16), t, lo, hi))
            prob_tiles = [jnp.concatenate(tile, axis=0) for tile in prob_tiles]
            for t, tile in enumerate(prob_tiles):
                probs[g * PER_GROUP + h, t, 0 : tile.shape[0], :] = tile
            res = tile_product(prob_tiles, vrh)
            out = jnp.where(in_head[h], res, out)
            low = jnp.where(in_head[(h + 1) % PER_GROUP], res, low)
        mixed[:, lanes] = out.astype(BF16)
        pr[:, lanes] = low.astype(BF16)
        probs_copy(g).start()
        return carry

    lax.fori_loop(0, groups, attention, 0, unroll=True)
    out_copies[4].start()
    w_copies[3].wait()
    start[...] = normed0[...] + (mm(mixed[...], wo[...]) + bias_ref[3:4])
    out_copies[0].start()
    for copy in out_copies + [probs_copy(g) for g in range(groups)]:
        copy.wait()


def attend_call(pieces, seg, small, wqkv, wo, kept, unit, units):
    pos, gain, shift, bias, down, up = small
    parts = len(pieces)
    rows, feats = pieces[0].shape
    width = pos.shape[1]
    heads = width // HEAD_DIM
    tiles = rows // GROUP
    forms = [
        ((rows, width), F32),
        ((rows, width), BF16),
        ((rows, width), BF16),
        ((rows, GROUP), BF16),
        ((rows, width), BF16),
        ((heads, tiles, SPAN, GROUP), BF16),
    ]
    fresh = kept is None
    scratch = [
        pltpu.VMEM((parts, rows, feats), BF16),
        pltpu.VMEM(pos.shape, BF16),
        pltpu.VMEM(down.shape, BF16),
        pltpu.VMEM(wqkv.shape, BF16),
        pltpu.VMEM(wo.shape, BF16),
        pltpu.VMEM((rows, width), F32),
        pltpu.VMEM((rows, width), BF16),
        pltpu.VMEM((rows, width), F32),
        pltpu.VMEM((rows, width), BF16),
        pltpu.VMEM((rows, width), BF16),
        pltpu.VMEM((rows, width), BF16),
        pltpu.VMEM((rows, GROUP), BF16),
        pltpu.VMEM((rows, width), BF16),
        pltpu.VMEM((heads, tiles, SPAN, GROUP), BF16),
        pltpu.VMEM((rows, width), BF16),
        pltpu.SemaphoreType.DMA((parts + 9 + width // GROUP,)),
    ]
    args = [*pieces, seg, gain, shift, bias, up, pos, down, wqkv, wo]
    aliases = {} if fresh else {len(args) + i: i for i in range(len(forms))}
    return pl.pallas_call(
        functools.partial(attend_kernel, parts=parts, unit=unit, fresh=fresh),
        out_shape=[jax.ShapeDtypeStruct((units, *shape), kind) for shape, kind in forms],
        in_specs=[ANY] * parts + [VMEM] * 5 + [ANY] * 4 + ([] if fresh else [ANY] * len(forms)),
        out_specs=[ANY] * len(forms),
        input_output_aliases=aliases,
        scratch_shapes=scratch,
        compiler_params=pltpu.CompilerParams(vmem_limit_bytes=58 * MIB),
        cost_estimate=pl.CostEstimate(
            flops=rows * width,
            bytes_accessed=MIB // 4,
            transcendentals=0,
        ),
        name="attend",
    )(*args, *([] if fresh else kept))


def finish_kernel(*refs, plan, arrays, parts):
    seg_ref, label_ref, gain_ref, shift_ref, bias_ref, head_ref, *refs = refs
    wo_hbm, refs = refs[0], refs[1:]
    weight_refs, refs = refs[:arrays], refs[arrays:]
    kept, refs = refs[:6], refs[6:]
    acc_ref, refs = refs[0], refs[1:]
    bufs, refs = refs[:6], refs[6:]
    wo, win, wout, ffb, xb, mixed, xh1, stat1, acc, slope, act, sems, wsems = refs
    resid2buf, k2, v2, red2, pr2, probs2 = bufs
    units = kept[0].shape[0]
    rows, width = xh1.shape
    hidden_part = win.shape[2]
    chunk = GROUP if hidden_part % GROUP == 0 else hidden_part
    groups = width // GROUP
    blocks = rows // BLOCK
    tiles = rows // GROUP
    row_steps = rows // STEP_ROWS
    half = lax.rem(lax.axis_index("dp"), 2)

    def weight_copies():
        made = []
        for i, (matrix, array, first, n, r, mine) in enumerate(plan):
            src = weight_refs[array].at[pl.ds(first, n), :]
            dst = (win, wout, ffb)[matrix].at[r]
            if mine is not None:
                top = pl.multiple_of((half if mine else 1 - half) * n, 16)
                dst = (win, wout, ffb)[matrix].at[r, pl.ds(top, n), :]
            made.append(pltpu.make_async_copy(src, dst, wsems.at[i]))
        made.append(pltpu.make_async_copy(wo_hbm, wo, wsems.at[len(plan)]))
        return made

    def state_copies(u, slot):
        return [
            pltpu.make_async_copy(src.at[u], buf.at[slot], sems.at[slot, i])
            for i, (src, buf) in enumerate(zip(kept, bufs))
        ]

    for copy in state_copies(0, 0)[:1] + weight_copies() + state_copies(0, 0)[1:]:
        copy.start()

    gain1, gain2 = gain_ref[1:2], gain_ref[2:3]
    shift1, shift2 = shift_ref[1:2], shift_ref[2:3]
    head_row = head_ref[...].reshape(1, width + 1)
    head, head_bias = head_row[:, 0:width], head_row[:, width : width + 1]
    hg = head * gain2
    hg_mean = row_mean(hg)
    bias4 = bias_ref[4:5]
    base = jnp.sum(shift2 * head, axis=1, keepdims=True)
    in_head, keep = head_masks()
    acc_ref[...] = jnp.zeros(acc_ref.shape, F32)

    def unit(u, carry):
        slot = lax.rem(u, 2)
        now = state_copies(u, slot)

        @pl.when(u + 1 < units)
        def _():
            for copy in state_copies(u + 1, 1 - slot):
                copy.start()

        now[0].wait()

        def norm1(i, c):
            x = resid2buf[slot, at(i), :]
            off = x - row_mean(x)
            inv = lax.rsqrt(row_mean(off * off) + LN_EPS)
            xh = off * inv
            xh1[at(i), :] = xh
            stat1[at(i), :] = inv
            xb[at(i), :] = (xh * gain1 + shift1).astype(BF16)
            return c

        lax.fori_loop(0, row_steps, norm1, 0, unroll=True)

        @pl.when(u == 0)
        def _():
            for copy in weight_copies():
                copy.wait()

        for r in range(parts):
            for c in range(0, hidden_part, chunk):
                hid = slice(r * hidden_part + c, r * hidden_part + c + chunk)
                line = ffb[r, 0:1, c : c + chunk].astype(F32)
                pre = mm(xb[...], win[r, :, c : c + chunk]) + line
                phi = 0.5 + 0.5 * lax.erf(pre * INV_SQRT2)
                act[:, hid] = (pre * phi).astype(BF16)
                slope[:, hid] = phi + pre * jnp.exp(-0.5 * pre * pre) * INV_SQRT_2PI
        for n in range(0, width, GROUP):
            acc[:, n : n + GROUP] = add_all(
                [
                    mm(act[:, r * hidden_part : (r + 1) * hidden_part], wout[r, :, n : n + GROUP])
                    for r in range(parts)
                ]
            )

        inv_cols = []
        dot_cols = []
        for i in range(row_steps):
            part = slice(i * STEP_ROWS, (i + 1) * STEP_ROWS)
            x = xh1[part, :] * gain1 + shift1 + (acc[part, :] + bias4)
            off = x - row_mean(x)
            inv = lax.rsqrt(row_mean(off * off) + LN_EPS)
            xh = off * inv
            acc[part, :] = xh
            inv_cols.append(inv)
            dot_cols.append(jnp.sum(xh * hg, axis=1, keepdims=True))
        inv2 = jnp.concatenate(inv_cols, axis=0)
        dots = jnp.concatenate(dot_cols, axis=0)

        seg_row = seg_ref[u].astype(F32)
        seg_col = column(seg_row)
        label = label_ref[u]
        slots = label.shape[1]
        slot_no = lax.broadcasted_iota(jnp.int32, (rows, slots), 1).astype(F32)
        member = jnp.where(seg_col == slot_no, 1.0, 0.0)
        counts = jnp.sum(member, axis=0, keepdims=True)
        sums = jnp.sum(member * (dots + base), axis=0, keepdims=True)
        most = jnp.maximum(counts, 1.0)
        error = jnp.where(counts > 0, sums / most + head_bias - label, 0.0)
        grad_pred = 2.0 * error
        weight = jnp.sum(member * (grad_pred / most), axis=1, keepdims=True)
        loss = jnp.sum(error * error, axis=1, keepdims=True)
        weight_sum = jnp.sum(grad_pred, axis=1, keepdims=True)
        items = jnp.max(seg_row, axis=1, keepdims=True) + 1.0

        head_grad = jnp.zeros((8, width), F32)
        for i in range(row_steps):
            part = slice(i * STEP_ROWS, (i + 1) * STEP_ROWS)
            xh = acc[part, :]
            w = weight[part]
            weighted = xh * w
            for j in range(STEP_ROWS // 8):
                head_grad = head_grad + weighted[j * 8 : (j + 1) * 8]
            grad = (inv2[part] * w) * (hg - hg_mean - xh * (dots[part] * (1.0 / width)))
            acc[part, :] = grad
            xb[part, :] = grad.astype(BF16)
        head_grad = jnp.sum(head_grad, axis=0, keepdims=True) * gain2 + weight_sum * shift2
        acc_ref[16:17, :] += head_grad
        lane_row = lax.broadcasted_iota(jnp.int32, (1, width), 1)
        acc_ref[17:18, :] += jnp.where(
            lane_row == 0,
            loss,
            jnp.where(lane_row == 1, items, jnp.where(lane_row == 2, weight_sum, 0.0)),
        )

        for r in range(parts):
            for c in range(0, hidden_part, chunk):
                hid = slice(r * hidden_part + c, r * hidden_part + c + chunk)
                back = mm(xb[...], wout[r, c : c + chunk, :], NT)
                act[:, hid] = (back * slope[:, hid]).astype(BF16)
        for n in range(0, width, GROUP):
            acc[:, n : n + GROUP] = add_all(
                [acc[:, n : n + GROUP]]
                + [
                    mm(
                        act[:, r * hidden_part : (r + 1) * hidden_part],
                        win[r, n : n + GROUP, :],
                        NT,
                    )
                    for r in range(parts)
                ]
            )

        def back1(i, c):
            g = acc[at(i), :] * gain1
            xh = xh1[at(i), :]
            grad = stat1[at(i), :] * (g - row_mean(g) - xh * row_mean(g * xh))
            xb[at(i), :] = grad.astype(BF16)
            return c

        lax.fori_loop(0, row_steps, back1, 0, unroll=True)

        mixed[...] = mm(xb[...], wo[...], NT).astype(BF16)
        for copy in now[1:]:
            copy.wait()

        def attention_back(g, c):
            lanes = pl.ds(pl.multiple_of(g * GROUP, GROUP), GROUP)
            gg, kg = mixed[:, lanes], k2[slot, :, lanes]
            grads = stacked_scores(gg, v2[slot, :, lanes], keep)
            out = jnp.zeros((rows, GROUP), F32)
            for h in range(PER_GROUP):
                score_tiles = [[] for _ in range(tiles)]
                for b in range(blocks):
                    found = []
                    for t, lo, hi in block_pieces(b, blocks):
                        first, last = tile_rows(t, rows)
                        top = b * BLOCK - first
                        lane_at = slice((lo - 2 * t) * BLOCK, (hi + 1 - 2 * t) * BLOCK)
                        here = h * (last - first) + top
                        dp = grads[t][here : here + BLOCK, lane_at]
                        p = probs2[slot, g * PER_GROUP + h, t, top : top + BLOCK, lane_at]
                        found.append((p.astype(F32), dp))
                    shared = add_all([jnp.sum(p * dp, axis=1, keepdims=True) for p, dp in found])
                    for (t, lo, hi), (p, dp) in zip(block_pieces(b, blocks), found):
                        score_tiles[t].append(
                            spread((p * (dp - shared)).astype(BF16), t, lo, hi)
                        )
                res = tile_product([jnp.concatenate(tile, axis=0) for tile in score_tiles], kg)
                out = jnp.where(in_head[h], res, out)
            query_part = mm(red2[slot], out.astype(BF16), TN)[0:8]
            acc_ref[0:8, lanes] += query_part * (2.0 * HEAD_DIM**-0.5)
            cross = mm(pr2[slot, :, lanes], gg, TN)
            value_part = jnp.zeros((8, GROUP), F32)
            for h in range(PER_GROUP):
                top = ((h + 1) % PER_GROUP) * HEAD_DIM + 8
                value_part = jnp.where(in_head[h], cross[top : top + 8], value_part)
            acc_ref[8:16, lanes] += 2.0 * value_part
            return c

        lax.fori_loop(0, groups, attention_back, 0, unroll=True)
        return carry

    lax.fori_loop(0, units, unit, 0)


def finish_call(segs, labels, small, wo, arrays, plan, kept, parts):
    gain, shift, bias, head = small
    units, rows, width = kept[0].shape
    hidden_part = arrays[0].shape[1]
    hidden = hidden_part * parts
    scratch = [pltpu.VMEM((2, *a.shape[1:]), a.dtype) for a in kept]
    scratch += [
        pltpu.VMEM(wo.shape, BF16),
        pltpu.VMEM((parts, width, hidden_part), BF16),
        pltpu.VMEM((parts, hidden_part, width), BF16),
        pltpu.VMEM((parts, BIAS_ROWS, hidden_part), BF16),
        pltpu.VMEM((rows, width), BF16),
        pltpu.VMEM((rows, width), BF16),
        pltpu.VMEM((rows, width), F32),
        pltpu.VMEM((rows, 1), F32),
        pltpu.VMEM((rows, width), F32),
        pltpu.VMEM((rows, hidden), F32),
        pltpu.VMEM((rows, hidden), BF16),
        pltpu.SemaphoreType.DMA((2, len(kept))),
        pltpu.SemaphoreType.DMA((len(plan) + 1,)),
    ]
    return pl.pallas_call(
        functools.partial(finish_kernel, plan=plan, arrays=len(arrays), parts=parts),
        out_shape=jax.ShapeDtypeStruct((ACC_ROWS, width), F32),
        in_specs=[VMEM] * 6 + [ANY] * (1 + len(arrays) + len(kept)),
        out_specs=VMEM,
        scratch_shapes=scratch,
        compiler_params=pltpu.CompilerParams(vmem_limit_bytes=62 * MIB),
        cost_estimate=pl.CostEstimate(
            flops=rows * width,
            bytes_accessed=MIB // 4,
            transcendentals=0,
        ),
        name="finish",
    )(segs, labels, gain, shift, bias, head, wo, *arrays, *kept)


def update_kernel(
    acc_ref,
    other_ref,
    up_ref,
    momentum_ref,
    head_ref,
    first_ref,
    second_ref,
    loss_ref,
    items_ref,
    norm_ref,
    moment_out,
    up_out,
    low_out,
    first_out,
    second_out,
    head_out,
    head_low_out,
):
    total = acc_ref[...] + other_ref[...]
    width = total.shape[1]
    rank = up_ref.shape[0] // 2
    items = total[17:18, 1:2]
    loss_ref[...] = total[17:18, 0:1]
    items_ref[...] = items
    adapter = total[0:16] / items
    head_grad = jnp.concatenate([total[16:17], total[17:18, 2:3]], axis=1) / items
    norm = jnp.sqrt(jnp.sum(adapter * adapter) + jnp.sum(head_grad * head_grad))
    norm_ref[...] = jnp.full((1, 1), norm, F32)
    factor = jnp.minimum(1.0, CLIP_NORM / (norm_ref[...] + 1e-06))
    moment = ORTHO_MOMENTUM * momentum_ref[...] + factor * adapter
    moment_out[...] = moment

    def dot(left, right, dims=NN):
        return lax.dot_general(
            left, right, dims, preferred_element_type=F32, precision=lax.Precision.HIGHEST
        )

    basis = []
    for i in range(2):
        part = moment[i * rank : (i + 1) * rank]
        size = jnp.sqrt(jnp.sum(jnp.sum(part * part, axis=1, keepdims=True), axis=0, keepdims=True))
        basis.append(part / (size + 1e-07))
    for sweep in range(5):
        gram = [dot(x, x, NT) for x in basis]
        poly = [NS_B * g + NS_C * dot(g, g) for g in gram]
        basis = [NS_A * x + dot(p, x) for x, p in zip(basis, poly)]
    up = up_ref[...] - ORTHO_STEP_SIZE * jnp.concatenate(basis, axis=0)
    up_out[...] = up
    low_out[...] = up.astype(BF16)

    clipped = factor * head_grad
    def as_row(ref):
        return ref[...].reshape(1, width + 1)

    first = BETA_ONE * as_row(first_ref) + (1.0 - BETA_ONE) * clipped
    second = BETA_TWO * as_row(second_ref) + (1.0 - BETA_TWO) * clipped * clipped
    first_hat = first / (1.0 - BETA_ONE**STEP)
    second_hat = second / (1.0 - BETA_TWO**STEP)
    head = as_row(head_ref)
    new_head = head - ADAM_RATE * (first_hat / (jnp.sqrt(second_hat) + ADAM_EPS) + DECAY * head)
    first_out[...] = first[0]
    second_out[...] = second[0]
    head_out[...] = new_head[0]
    head_low_out[...] = new_head[0].astype(BF16)


def update_call(acc, other, up, momentum, head, first, second):
    one = jax.ShapeDtypeStruct((1, 1), F32)
    flat = jax.ShapeDtypeStruct(up.shape, F32)
    row = jax.ShapeDtypeStruct(head.shape, F32)
    return pl.pallas_call(
        update_kernel,
        out_shape=[
            one,
            one,
            one,
            flat,
            flat,
            jax.ShapeDtypeStruct(up.shape, BF16),
            row,
            row,
            row,
            jax.ShapeDtypeStruct(head.shape, BF16),
        ],
        in_specs=[VMEM] * 7,
        out_specs=[VMEM] * 10,
        name="update",
    )(acc, other, up, momentum, head, first, second)


def swap(value, axis, bit):
    size = lax.axis_size(axis)
    return lax.ppermute(value, axis, [(i, i ^ bit) for i in range(size)])


class Weights:
    def __init__(self, owns, bias):
        parts = lax.axis_size("tensor")
        half = lax.rem(lax.axis_index("dp"), 2)
        self.owns = owns
        self.sizes = [own.shape[0] // 2 for own in owns]
        self.bias = jnp.pad(bias[None, :], ((0, BIAS_ROWS - 1), (0, 0)))
        cuts = [
            lax.dynamic_slice_in_dim(own, half * n, n, 0) for own, n in zip(owns, self.sizes)
        ]
        if cuts[0].shape[1] == cuts[1].shape[1]:
            cuts = [jnp.concatenate([*cuts, self.bias], axis=0)]
        else:
            cuts.append(self.bias)
        self.one = len(cuts) == 1
        mine = {0: cuts}
        bit = parts // 2
        while bit > 1:
            mine.update({r ^ bit: [swap(a, "tensor", bit) for a in mine[r]] for r in list(mine)})
            bit //= 2
        del mine[0]
        self.mine = mine

    def core(self, pieces):
        return {r ^ 1: [swap(a, "tensor", 1) for a in arrays] for r, arrays in pieces.items()}

    def across(self, pieces):
        return {r: [swap(a, "dp", 1) for a in arrays] for r, arrays in pieces.items()}

    def operands(self):
        arrays = [*self.owns, *self.core_own, self.bias, self.core_bias]
        plan = [(2, 4, 0, BIAS_ROWS, 0, None), (2, 5, 0, BIAS_ROWS, 1, None)]
        for i in range(2):
            n = 2 * self.sizes[i]
            plan += [(i, i, 0, n, 0, None), (i, 2 + i, 0, n, 1, None)]
        for pieces, is_mine in (
            (self.mine, True),
            (self.core_mine, True),
            (self.other, False),
            (self.core_other, False),
        ):
            for r, found in pieces.items():
                first = 0
                for i, n in enumerate([*self.sizes, BIAS_ROWS]):
                    array = len(arrays) + (0 if self.one else i)
                    if i < 2:
                        plan.append((i, array, first, n, r, is_mine))
                    elif is_mine:
                        plan.append((i, array, first, n, r, None))
                    first += n if self.one else 0
                arrays += found
        return arrays, tuple(sorted(plan, key=lambda step: step[0]))


def local(
    input_token_ids,
    segments,
    labels,
    embedding,
    position_embedding_table,
    norm_gain_rows,
    norm_shift_rows,
    query_key_value_weight,
    attention_output_weight,
    attention_bias_stack,
    feedforward_in_weight,
    feedforward_bias,
    feedforward_out_weight,
    adapter_down_weight,
    adapter_up_weight,
    adapter_momentum,
    head,
    head_first_moment,
    head_second_moment,
):
    length = input_token_ids.shape[-1]
    slots = labels.shape[-1]
    width = position_embedding_table.shape[1]
    rank = adapter_up_weight.shape[1]
    parts = lax.axis_size("tensor")
    ids = input_token_ids.reshape(-1, 1, length)
    all_ids = [ids] + [swap(ids, "tensor", r) for r in range(1, parts)]
    segs = segments.reshape(-1, 1, length)
    labs = labels.reshape(-1, 1, slots)
    units = ids.shape[0]


    all_ids, owns, bias = lax.optimization_barrier(
        (all_ids, [feedforward_in_weight, feedforward_out_weight], feedforward_bias)
    )
    weights = Weights(owns, bias)
    weights.core_own = [swap(own, "tensor", 1) for own in owns]
    weights.core_bias = swap(weights.bias, "tensor", 1)
    picked = embed_call(all_ids, embedding)
    (
        picked,
        weights.mine,
        weights.core_own,
        weights.core_bias,
        adapter_down_weight,
        adapter_up_weight,
        head_rows,
    ) = lax.optimization_barrier(
        (
            picked,
            weights.mine,
            weights.core_own,
            weights.core_bias,
            adapter_down_weight,
            adapter_up_weight,
            (head, head_first_moment, head_second_moment),
        )
    )
    weights.other = weights.across(weights.mine)
    weights.core_mine = weights.core(weights.mine)
    down = jnp.concatenate(
        [
            adapter_down_weight[0],
            adapter_down_weight[1],
            jnp.zeros((width, HEAD_DIM - 2 * rank), BF16),
        ],
        axis=1,
    )
    down = jnp.concatenate([down] * PER_GROUP, axis=1)
    twice = 2.0 * adapter_up_weight.astype(BF16)
    up = jnp.stack(
        [jnp.pad(twice[0], ((0, rank), (0, 0))), jnp.pad(twice[1], ((rank, 0), (0, 0)))]
    )
    picked = [picked[u * parts : (u + 1) * parts] for u in range(units)]

    small = (
        position_embedding_table,
        norm_gain_rows,
        norm_shift_rows,
        attention_bias_stack,
        down,
        up,
    )
    kept = None
    moved = []
    for u in range(units):
        while len(moved) < min(u + 2, units):
            sends = picked[len(moved)][1:]
            if moved:
                sends = lax.optimization_barrier((sends, moved[-1], kept))[0]
            moved.append([swap(a, "tensor", r + 1) for r, a in enumerate(sends)])
        if u == 0:
            moved[0], weights.core_mine = lax.optimization_barrier((moved[0], weights.core_mine))
        kept = attend_call(
            [picked[u][0], *moved[u]],
            segs[u],
            small,
            query_key_value_weight,
            attention_output_weight,
            kept,
            u,
            units,
        )

    weights.core_other = weights.core(lax.optimization_barrier((weights.other, kept))[0])
    arrays, plan = weights.operands()
    acc = finish_call(
        segs,
        labs,
        (norm_gain_rows, norm_shift_rows, attention_bias_stack, head_rows[0]),
        attention_output_weight,
        arrays,
        plan,
        kept,
        parts,
    )
    steps = []
    for axis in ("tensor", "dp"):
        bit = 1
        while bit < lax.axis_size(axis):
            steps.append((axis, bit))
            bit *= 2
    for axis, bit in steps[:-1]:
        acc = acc + swap(acc, axis, bit)
    other = swap(acc, *steps[-1])

    flat = (2 * rank, width)
    outs = update_call(
        acc,
        other,
        adapter_up_weight.reshape(flat),
        adapter_momentum.reshape(flat),
        *head_rows,
    )
    loss, items, norm, moment, new_up, low, first, second, new_head, head_low = outs
    shape = adapter_up_weight.shape
    return (
        loss[0, 0],
        items[0, 0],
        norm[0, 0],
        moment.reshape(shape),
        new_up.reshape(shape),
        low.reshape(shape),
        first,
        second,
        new_head,
        head_low,
    )


def solution(mesh):
    rows = P(None, ("dp", "tensor"), None)
    placed = (
        (rows, rows, rows, P("tensor", None))
        + (P(),) * 6
        + (P(None, "tensor"), P("tensor"), P("tensor", None))
        + (P(),) * 6
    )
    return jax.shard_map(
        local, mesh=mesh, in_specs=placed, out_specs=(P(),) * 10, check_vma=False
    )
```

```python
import functools
import math

import jax
import jax.numpy as jnp
from jax import lax
from jax.experimental import pallas as pl
from jax.experimental.pallas import tpu as pltpu
from jax.sharding import PartitionSpec as P

HEAD_DIM = 64
STEP = 10
LN_EPS = 1e-05
CLIP_NORM = 0.5
ORTHO_MOMENTUM = 0.5
ORTHO_STEP_SIZE = 1.0
NS_A = 3.4445
NS_B = -4.775
NS_C = 2.0315
BETA_ONE = 0.9
BETA_TWO = 0.999
ADAM_RATE = 0.05
ADAM_EPS = 1e-08
DECAY = 0.01

F32 = jnp.float32
BF16 = jnp.bfloat16
LANES = 128
GROUP = 256
PER_GROUP = GROUP // HEAD_DIM
BLOCK = 128
SPAN = 3 * BLOCK
STEP_ROWS = 64
VOCAB_BLOCK = 2048
RING = 6
UNROLL = 64
ACC_ROWS = 24
BIAS_ROWS = 16
MIB = 1024 * 1024
NN = (((1,), (0,)), ((), ()))
NT = (((1,), (1,)), ((), ()))
TN = (((0,), (0,)), ((), ()))
INV_SQRT2 = 1.0 / math.sqrt(2.0)
INV_SQRT_2PI = 1.0 / math.sqrt(2.0 * math.pi)

VMEM = pl.BlockSpec(memory_space=pltpu.VMEM)
SMEM = pl.BlockSpec(memory_space=pltpu.SMEM)
ANY = pl.BlockSpec(memory_space=pl.ANY)


def mm(left, right, dims=NN):
    return lax.dot_general(left, right, dims, preferred_element_type=F32)


def row_mean(rows):
    return jnp.mean(rows, axis=-1, keepdims=True)


def add_all(terms):
    return functools.reduce(jnp.add, terms)


def at(i):
    return pl.ds(pl.multiple_of(i * STEP_ROWS, STEP_ROWS), STEP_ROWS)


def embed_kernel(*refs, parts, units):
    ids = refs[:parts]
    table, tail = refs[parts : parts + 2]
    outs = refs[parts + 2 : parts + 2 + parts * units]
    scratch = refs[parts + 2 + parts * units :]
    feats = table.shape[0]
    full = table.shape[1] // VOCAB_BLOCK
    lanes = [(lo, min(lo + LANES, feats)) for lo in range(0, feats, LANES)]
    turned = scratch[: len(lanes)]
    picked = scratch[len(lanes) : 2 * len(lanes)]
    ring, stage, ring_sems, sems = scratch[2 * len(lanes) :]

    def fetch(i):
        cols = pl.ds(pl.multiple_of(i * VOCAB_BLOCK, VOCAB_BLOCK), VOCAB_BLOCK)
        slot = lax.rem(i, RING)
        return pltpu.make_async_copy(table.at[:, cols], ring.at[slot], ring_sems.at[slot])

    def turn_block(base, block):
        for c in range(0, VOCAB_BLOCK, GROUP):
            rows_at = pl.ds(pl.multiple_of(base + c, GROUP), GROUP)
            for (lo, hi), turn in zip(lanes, turned):
                turn[rows_at, :] = block[lo:hi, c : c + GROUP].T.astype(F32)

    for i in range(min(RING, full)):
        fetch(i).start()
    turn_block(full * VOCAB_BLOCK, tail)

    def step(i, carry):
        fetch(i).wait()
        turn_block(i * VOCAB_BLOCK, ring.at[lax.rem(i, RING)])

        @pl.when(i + RING < full)
        def _():
            fetch(i + RING).start()

        return carry

    lax.fori_loop(0, full, step, 0)

    length = stage.shape[1]
    copies = []
    for p, out in enumerate(outs):
        u, r = p // parts, p % parts
        slot = p % 2

        def rows(i, carry, u=u, r=r):
            top = pl.multiple_of(i * UNROLL, UNROLL)
            for j in range(UNROLL):
                token = ids[r][u, 0, top + j]
                for turn, pick in zip(turned, picked):
                    pick[pl.ds(top + j, 1), :] = turn[pl.ds(token, 1), :]
            return carry

        lax.fori_loop(0, length // UNROLL, rows, 0)
        if p >= 2:
            copies[p - 2].wait()
        for (lo, hi), pick in zip(lanes, picked):
            stage[slot, :, lo:hi] = pick[...].astype(BF16)
        copies.append(pltpu.make_async_copy(stage.at[slot], out, sems.at[slot]))
        copies[p].start()
    for copy in copies[-2:]:
        copy.wait()


def embed_call(ids, table):
    parts = len(ids)
    units, _, length = ids[0].shape
    feats, vocab = table.shape
    full = vocab // VOCAB_BLOCK
    widths = [min(LANES, feats - lo) for lo in range(0, feats, LANES)]
    scratch = [pltpu.VMEM(((full + 1) * VOCAB_BLOCK, w), F32) for w in widths]
    scratch += [pltpu.VMEM((length, w), F32) for w in widths]
    scratch += [
        pltpu.VMEM((RING, feats, VOCAB_BLOCK), BF16),
        pltpu.VMEM((2, length, feats), BF16),
        pltpu.SemaphoreType.DMA((RING,)),
        pltpu.SemaphoreType.DMA((2,)),
    ]
    last = pl.cdiv(vocab, VOCAB_BLOCK) - 1
    tail = pl.BlockSpec((feats, VOCAB_BLOCK), lambda i: (0, last), pipeline_mode=pl.Buffered(1))
    return pl.pallas_call(
        functools.partial(embed_kernel, parts=parts, units=units),
        grid=(1,),
        in_specs=[SMEM] * parts + [ANY, tail],
        out_specs=[ANY] * (parts * units),
        out_shape=[jax.ShapeDtypeStruct((length, feats), BF16)] * (parts * units),
        scratch_shapes=scratch,
        compiler_params=pltpu.CompilerParams(vmem_limit_bytes=62 * MIB),
        name="embed",
    )(*ids, table, table)


def tile_rows(t, rows):
    lo = min(max(2 * t - 1, 0) * BLOCK, rows - min(SPAN, rows))
    return lo, min((2 * t + 3) * BLOCK, rows)


def block_pieces(b, blocks):
    first, last = max(b - 1, 0), min(b + 1, blocks - 1)
    found = []
    for t in range(blocks * BLOCK // GROUP):
        lo, hi = max(first, 2 * t), min(last, 2 * t + 1)
        if lo <= hi:
            found.append((t, lo, hi))
    return found


def spread(values, t, lo, hi):
    zero_block = jnp.zeros((BLOCK, BLOCK), BF16)
    parts = [values] if lo == 2 * t else [zero_block, values]
    if hi == 2 * t:
        parts.append(zero_block)
    return parts[0] if len(parts) == 1 else jnp.concatenate(parts, axis=1)


def head_masks():
    head_of = lax.broadcasted_iota(jnp.int32, (1, GROUP), 1) // HEAD_DIM
    in_head = [head_of == h for h in range(PER_GROUP)]
    return in_head, [jnp.where(m, 1.0, 0.0).astype(BF16) for m in in_head]


def column(row):
    return jnp.broadcast_to(row, (8, row.shape[1])).T[:, 0:1]


def tile_product(tiles, right):
    rows = right.shape[0]
    res = [None] * (rows // BLOCK)
    for t, left in enumerate(tiles):
        part = mm(left, right[t * GROUP : (t + 1) * GROUP])
        first = tile_rows(t, rows)[0] // BLOCK
        for i in range(left.shape[0] // BLOCK):
            piece = part[i * BLOCK : (i + 1) * BLOCK]
            res[first + i] = piece if res[first + i] is None else res[first + i] + piece
    return jnp.concatenate(res, axis=0)


def stacked_scores(left, right, keep):
    rows = left.shape[0]
    found = []
    for t in range(rows // GROUP):
        lo, hi = tile_rows(t, rows)
        stack = jnp.concatenate([left[lo:hi] * keep[h] for h in range(PER_GROUP)], axis=0)
        found.append(mm(stack, right[t * GROUP : (t + 1) * GROUP], NT))
    return found


def attend_kernel(*refs, parts, unit, fresh):
    pieces = refs[:parts]
    seg_ref, gain_ref, shift_ref, bias_ref, up_ref, pos_hbm, down_hbm, wqkv_hbm, wo_hbm = refs[
        parts : parts + 9
    ]
    refs = refs[parts + 9 + (0 if fresh else 6) :]
    outs, (x4, pos, down, wqkv, wo, start, xb, normed0, q, k, v, red, pr, probs, mixed, sems) = refs[:6], refs[6:]
    rows, width = normed0.shape
    groups = width // GROUP
    blocks = rows // BLOCK
    tiles = rows // GROUP
    row_steps = rows // STEP_ROWS
    me = lax.axis_index("tensor")

    in_copies = [
        pltpu.make_async_copy(piece, x4.at[jnp.bitwise_xor(me, r)], sems.at[r])
        for r, piece in enumerate(pieces)
    ]
    w_copies = [
        pltpu.make_async_copy(pos_hbm, pos, sems.at[parts]),
        pltpu.make_async_copy(down_hbm, down, sems.at[parts + 1]),
        pltpu.make_async_copy(wqkv_hbm, wqkv, sems.at[parts + 2]),
        pltpu.make_async_copy(wo_hbm, wo, sems.at[parts + 3]),
    ]
    out_copies = [
        pltpu.make_async_copy(ref, out.at[unit], sems.at[parts + 4 + i])
        for i, (ref, out) in enumerate(zip((start, k, v, red, pr), outs))
    ]

    def probs_copy(g):
        heads = pl.ds(g * PER_GROUP, PER_GROUP)
        return pltpu.make_async_copy(
            probs.at[heads], outs[5].at[unit, heads], sems.at[parts + 9 + g]
        )

    for copy in [w_copies[0], *in_copies, *w_copies[1:]]:
        copy.start()

    seg_row = seg_ref[...].astype(F32)
    seg_col = column(seg_row)
    lane = lax.broadcasted_iota(jnp.int32, (rows, rows), 1)
    sub = lax.broadcasted_iota(jnp.int32, (rows, rows), 0)
    before = (seg_col == seg_row) & (lane < sub)
    place = jnp.sum(jnp.where(before, 1.0, 0.0), axis=1, keepdims=True).astype(jnp.int32)
    one_hot = jnp.where(lane == place, 1.0, 0.0).astype(BF16)
    w_copies[0].wait()
    start[...] = mm(one_hot, pos[...])
    for copy in in_copies:
        copy.wait()
    start[...] += jnp.concatenate([x4[t] for t in range(parts)], axis=1).astype(F32)

    gain0, shift0 = gain_ref[0:1], shift_ref[0:1]

    def norm0(i, carry):
        x = start[at(i), :]
        off = x - row_mean(x)
        y = off * lax.rsqrt(row_mean(off * off) + LN_EPS) * gain0 + shift0
        normed0[at(i), :] = y
        xb[at(i), :] = y.astype(BF16)
        return carry

    lax.fori_loop(0, row_steps, norm0, 0, unroll=True)

    w_copies[1].wait()
    red[...] = mm(xb[...], down[...]).astype(BF16)
    out_copies[3].start()
    w_copies[2].wait()
    low_rows = red[:, 0 : up_ref.shape[1]]
    q[...] = (mm(xb[...], wqkv[0]) + bias_ref[0:1] + mm(low_rows, up_ref[0])).astype(BF16) * BF16(
        HEAD_DIM**-0.5
    )
    k[...] = (mm(xb[...], wqkv[1]) + bias_ref[1:2]).astype(BF16)
    out_copies[1].start()
    v[...] = (mm(xb[...], wqkv[2]) + bias_ref[2:3] + mm(low_rows, up_ref[1])).astype(BF16)
    out_copies[2].start()

    in_head, keep = head_masks()

    def far(b, c):
        hit = seg_col[b * BLOCK : (b + 1) * BLOCK] == seg_row[:, c * BLOCK : (c + 1) * BLOCK]
        return jnp.where(hit, 0.0, -1e9)

    away = {
        (b, c): far(b, c) for b in range(blocks) for c in range(max(b - 1, 0), min(b + 2, blocks))
    }

    def attention(g, carry):
        lanes = pl.ds(pl.multiple_of(g * GROUP, GROUP), GROUP)
        vg = v[:, lanes]
        scores = stacked_scores(q[:, lanes], k[:, lanes], keep)
        out = jnp.zeros((rows, GROUP), F32)
        low = jnp.zeros((rows, GROUP), F32)
        for h in range(PER_GROUP):
            vrh = vg * keep[h] + red[...] * (1 - keep[h])
            prob_tiles = [[] for _ in range(tiles)]
            for b in range(blocks):
                found = []
                for t, lo, hi in block_pieces(b, blocks):
                    first, last = tile_rows(t, rows)
                    top = h * (last - first) + b * BLOCK - first
                    s = scores[t][top : top + BLOCK, (lo - 2 * t) * BLOCK : (hi + 1 - 2 * t) * BLOCK]
                    found.append(
                        s + jnp.concatenate([away[b, c] for c in range(lo, hi + 1)], axis=1)
                    )
                peak = functools.reduce(
                    jnp.maximum, [jnp.max(s, axis=1, keepdims=True) for s in found]
                )
                found = [jnp.exp(s - peak) for s in found]
                inv = 1.0 / add_all([jnp.sum(s, axis=1, keepdims=True) for s in found])
                for (t, lo, hi), s in zip(block_pieces(b, blocks), found):
                    prob_tiles[t].append(spread((s * inv).astype(BF16), t, lo, hi))
            prob_tiles = [jnp.concatenate(tile, axis=0) for tile in prob_tiles]
            for t, tile in enumerate(prob_tiles):
                probs[g * PER_GROUP + h, t, 0 : tile.shape[0], :] = tile
            res = tile_product(prob_tiles, vrh)
            out = jnp.where(in_head[h], res, out)
            low = jnp.where(in_head[(h + 1) % PER_GROUP], res, low)
        mixed[:, lanes] = out.astype(BF16)
        pr[:, lanes] = low.astype(BF16)
        probs_copy(g).start()
        return carry

    lax.fori_loop(0, groups, attention, 0, unroll=True)
    out_copies[4].start()
    w_copies[3].wait()
    start[...] = normed0[...] + (mm(mixed[...], wo[...]) + bias_ref[3:4])
    out_copies[0].start()
    for copy in out_copies + [probs_copy(g) for g in range(groups)]:
        copy.wait()


def attend_call(pieces, seg, small, wqkv, wo, kept, unit, units):
    pos, gain, shift, bias, down, up = small
    parts = len(pieces)
    rows, feats = pieces[0].shape
    width = pos.shape[1]
    heads = width // HEAD_DIM
    tiles = rows // GROUP
    forms = [
        ((rows, width), F32),
        ((rows, width), BF16),
        ((rows, width), BF16),
        ((rows, GROUP), BF16),
        ((rows, width), BF16),
        ((heads, tiles, SPAN, GROUP), BF16),
    ]
    fresh = kept is None
    scratch = [
        pltpu.VMEM((parts, rows, feats), BF16),
        pltpu.VMEM(pos.shape, BF16),
        pltpu.VMEM(down.shape, BF16),
        pltpu.VMEM(wqkv.shape, BF16),
        pltpu.VMEM(wo.shape, BF16),
        pltpu.VMEM((rows, width), F32),
        pltpu.VMEM((rows, width), BF16),
        pltpu.VMEM((rows, width), F32),
        pltpu.VMEM((rows, width), BF16),
        pltpu.VMEM((rows, width), BF16),
        pltpu.VMEM((rows, width), BF16),
        pltpu.VMEM((rows, GROUP), BF16),
        pltpu.VMEM((rows, width), BF16),
        pltpu.VMEM((heads, tiles, SPAN, GROUP), BF16),
        pltpu.VMEM((rows, width), BF16),
        pltpu.SemaphoreType.DMA((parts + 9 + width // GROUP,)),
    ]
    args = [*pieces, seg, gain, shift, bias, up, pos, down, wqkv, wo]
    aliases = {} if fresh else {len(args) + i: i for i in range(len(forms))}
    return pl.pallas_call(
        functools.partial(attend_kernel, parts=parts, unit=unit, fresh=fresh),
        out_shape=[jax.ShapeDtypeStruct((units, *shape), kind) for shape, kind in forms],
        in_specs=[ANY] * parts + [VMEM] * 5 + [ANY] * 4 + ([] if fresh else [ANY] * len(forms)),
        out_specs=[ANY] * len(forms),
        input_output_aliases=aliases,
        scratch_shapes=scratch,
        compiler_params=pltpu.CompilerParams(vmem_limit_bytes=58 * MIB),
        cost_estimate=pl.CostEstimate(
            flops=rows * width,
            bytes_accessed=MIB // 4,
            transcendentals=0,
        ),
        name="attend",
    )(*args, *([] if fresh else kept))


def interleave(*lists):
    done = [0] * len(lists)
    while any(n < len(steps) for n, steps in zip(done, lists)):
        share = [n / len(steps) if steps else 1.0 for n, steps in zip(done, lists)]
        i = share.index(min(share))
        lists[i][done[i]]()
        done[i] += 1


def finish_kernel(*refs, plan, arrays, parts):
    seg_ref, label_ref, gain_ref, shift_ref, bias_ref, head_ref, wo_hbm, *refs = refs
    weight_refs, refs = refs[:arrays], refs[arrays:]
    kept, refs = refs[:6], refs[6:]
    acc_ref, refs = refs[0], refs[1:]
    bufs, refs = (refs[:6], refs[6:12]), refs[12:]
    xbs, xh1s, stats, refs = refs[:3], refs[3:6], refs[6:9], refs[9:]
    accs, slopes, acts, refs = refs[:2], refs[2:4], refs[4:6], refs[6:]
    wo, win, wout, ffb, mixed, sems, wsems = refs
    units = kept[0].shape[0]
    rows, width = mixed.shape
    hidden_part = win.shape[2]
    chunk = GROUP if hidden_part % GROUP == 0 else hidden_part
    groups = width // GROUP
    blocks = rows // BLOCK
    tiles = rows // GROUP
    row_parts = [slice(i, i + STEP_ROWS) for i in range(0, rows, STEP_ROWS)]
    chunks = [(r, c) for r in range(parts) for c in range(0, hidden_part, chunk)]
    half = lax.rem(lax.axis_index("dp"), 2)

    weight_copies = [[], [], [], []]
    for i, (matrix, array, first, n, r, mine) in enumerate(plan):
        dst = (win, wout, ffb)[matrix].at[r]
        if mine is not None:
            top = pl.multiple_of((half if mine else 1 - half) * n, 16)
            dst = (win, wout, ffb)[matrix].at[r, pl.ds(top, n), :]
        src = weight_refs[array].at[pl.ds(first, n), :]
        weight_copies[matrix].append(pltpu.make_async_copy(src, dst, wsems.at[i]))
    weight_copies[3].append(pltpu.make_async_copy(wo_hbm, wo, wsems.at[len(plan)]))

    state_copies = [
        [
            pltpu.make_async_copy(src.at[u], buf, sems.at[u % 2, i])
            for i, (src, buf) in enumerate(zip(kept, bufs[u % 2]))
        ]
        for u in range(units)
    ]

    def start(copies):
        for copy in copies:
            copy.start()

    def wait(copies):
        for copy in copies:
            copy.wait()

    start(state_copies[0][:1] + weight_copies[2] + weight_copies[0] + weight_copies[1])
    for u in range(1, min(2, units)):
        start(state_copies[u][:1])
    start(weight_copies[3] + state_copies[0][1:])

    gain1, gain2 = gain_ref[1:2], gain_ref[2:3]
    shift1, shift2 = shift_ref[1:2], shift_ref[2:3]
    head_row = head_ref[...].reshape(1, width + 1)
    head, head_bias = head_row[:, 0:width], head_row[:, width : width + 1]
    hg = head * gain2
    hg_mean = row_mean(hg)
    bias4 = bias_ref[4:5]
    base = jnp.sum(shift2 * head, axis=1, keepdims=True)
    in_head, keep = head_masks()
    acc_ref[...] = jnp.zeros(acc_ref.shape, F32)

    def norm1(u):
        resid, xb, xh1, stat1 = bufs[u % 2][0], xbs[u % 3], xh1s[u % 3], stats[u % 3]

        def step(part):
            x = resid[part, :]
            off = x - row_mean(x)
            inv = lax.rsqrt(row_mean(off * off) + LN_EPS)
            xh = off * inv
            xh1[part, :] = xh
            stat1[part, :] = inv
            xb[part, :] = (xh * gain1 + shift1).astype(BF16)

        return [lambda: wait(state_copies[u][:1])] + [
            functools.partial(step, part) for part in row_parts
        ]

    def hidden(r, c):
        return slice(r * hidden_part + c, r * hidden_part + c + chunk)

    def feed_in(u):
        xb, act, slope = xbs[u % 3], acts[u % 2], slopes[u % 2]

        def step(r, c):
            line = ffb[r, 0:1, c : c + chunk].astype(F32)
            pre = mm(xb[...], win[r, :, c : c + chunk]) + line
            phi = 0.5 + 0.5 * lax.erf(pre * INV_SQRT2)
            act[:, hidden(r, c)] = (pre * phi).astype(BF16)
            tail = pre * jnp.exp(-0.5 * pre * pre) * INV_SQRT_2PI
            slope[:, hidden(r, c)] = (phi + tail).astype(BF16)

        return [functools.partial(step, r, c) for r, c in chunks]

    def feed_out(u):
        act, acc = acts[u % 2], accs[u % 2]

        def step(n, r):
            lanes = slice(n, n + GROUP)
            add = mm(act[:, r * hidden_part : (r + 1) * hidden_part], wout[r, :, lanes])
            acc[:, lanes] = add if r == 0 else acc[:, lanes] + add

        return [
            functools.partial(step, n, r) for n in range(0, width, GROUP) for r in range(parts)
        ]

    def head_part(u):
        xb, xh1, acc = xbs[u % 3], xh1s[u % 3], accs[u % 2]
        memo = {"inv": [], "dots": [], "grad": jnp.zeros((8, width), F32)}

        def norm2(part):
            x = xh1[part, :] * gain1 + shift1 + (acc[part, :] + bias4)
            off = x - row_mean(x)
            inv = lax.rsqrt(row_mean(off * off) + LN_EPS)
            xh = off * inv
            acc[part, :] = xh
            memo["inv"].append(inv)
            memo["dots"].append(jnp.sum(xh * hg, axis=1, keepdims=True))

        def items():
            dots = jnp.concatenate(memo["dots"], axis=0)
            seg_row = seg_ref[u].astype(F32)
            seg_col = column(seg_row)
            label = label_ref[u]
            slots = label.shape[1]
            slot_no = lax.broadcasted_iota(jnp.int32, (rows, slots), 1).astype(F32)
            member = jnp.where(seg_col == slot_no, 1.0, 0.0)
            counts = jnp.sum(member, axis=0, keepdims=True)
            sums = jnp.sum(member * (dots + base), axis=0, keepdims=True)
            most = jnp.maximum(counts, 1.0)
            error = jnp.where(counts > 0, sums / most + head_bias - label, 0.0)
            grad_pred = 2.0 * error
            memo["weight"] = jnp.sum(member * (grad_pred / most), axis=1, keepdims=True)
            loss = jnp.sum(error * error, axis=1, keepdims=True)
            weight_sum = jnp.sum(grad_pred, axis=1, keepdims=True)
            memo["sum"] = weight_sum
            count = jnp.max(seg_row, axis=1, keepdims=True) + 1.0
            lane_row = lax.broadcasted_iota(jnp.int32, (1, width), 1)
            acc_ref[17:18, :] += jnp.where(
                lane_row == 0,
                loss,
                jnp.where(lane_row == 1, count, jnp.where(lane_row == 2, weight_sum, 0.0)),
            )

        def back2(i, part):
            xh = acc[part, :]
            w = memo["weight"][part]
            weighted = xh * w
            for j in range(STEP_ROWS // 8):
                memo["grad"] = memo["grad"] + weighted[j * 8 : (j + 1) * 8]
            scaled = memo["dots"][i] * (1.0 / width)
            grad = (memo["inv"][i] * w) * (hg - hg_mean - xh * scaled)
            acc[part, :] = grad
            xb[part, :] = grad.astype(BF16)

        def close():
            total = jnp.sum(memo["grad"], axis=0, keepdims=True)
            acc_ref[16:17, :] += total * gain2 + memo["sum"] * shift2

        return (
            [functools.partial(norm2, part) for part in row_parts]
            + [items]
            + [functools.partial(back2, i, part) for i, part in enumerate(row_parts)]
            + [close]
        )

    def feed_back(u):
        xb, act, slope, acc = xbs[u % 3], acts[u % 2], slopes[u % 2], accs[u % 2]

        def up(r, c):
            back = mm(xb[...], wout[r, c : c + chunk, :], NT)
            act[:, hidden(r, c)] = (back * slope[:, hidden(r, c)].astype(F32)).astype(BF16)

        def down(n, r):
            lanes = slice(n, n + GROUP)
            acc[:, lanes] += mm(
                act[:, r * hidden_part : (r + 1) * hidden_part], win[r, lanes, :], NT
            )

        return [functools.partial(up, r, c) for r, c in chunks] + [
            functools.partial(down, n, r) for n in range(0, width, GROUP) for r in range(parts)
        ]

    def attention_back(u):
        xb, xh1, stat1, acc = xbs[u % 3], xh1s[u % 3], stats[u % 3], accs[u % 2]
        _, k2, v2, red2, pr2, probs2 = bufs[u % 2]
        memo = {}

        def back1(part):
            g = acc[part, :] * gain1
            xh = xh1[part, :]
            grad = stat1[part, :] * (g - row_mean(g) - xh * row_mean(g * xh))
            xb[part, :] = grad.astype(BF16)

        def project(n):
            mixed[:, n : n + GROUP] = mm(xb[...], wo[n : n + GROUP, :], NT).astype(BF16)

        def begin(g):
            lanes = slice(g * GROUP, (g + 1) * GROUP)
            memo["grads"] = stacked_scores(mixed[:, lanes], v2[:, lanes], keep)
            memo["out"] = jnp.zeros((rows, GROUP), F32)

        def one_head(g, h):
            lanes = slice(g * GROUP, (g + 1) * GROUP)
            score_tiles = [[] for _ in range(tiles)]
            for b in range(blocks):
                found = []
                for t, lo, hi in block_pieces(b, blocks):
                    first, last = tile_rows(t, rows)
                    top = b * BLOCK - first
                    lane_at = slice((lo - 2 * t) * BLOCK, (hi + 1 - 2 * t) * BLOCK)
                    here = h * (last - first) + top
                    dp = memo["grads"][t][here : here + BLOCK, lane_at]
                    p = probs2[g * PER_GROUP + h, t, top : top + BLOCK, lane_at]
                    found.append((p.astype(F32), dp))
                shared = add_all([jnp.sum(p * dp, axis=1, keepdims=True) for p, dp in found])
                for (t, lo, hi), (p, dp) in zip(block_pieces(b, blocks), found):
                    score_tiles[t].append(spread((p * (dp - shared)).astype(BF16), t, lo, hi))
            tiles_ = [jnp.concatenate(tile, axis=0) for tile in score_tiles]
            memo["out"] = jnp.where(in_head[h], tile_product(tiles_, k2[:, lanes]), memo["out"])

        def end(g):
            lanes = slice(g * GROUP, (g + 1) * GROUP)
            query_part = mm(red2[...], memo["out"].astype(BF16), TN)[0:8]
            acc_ref[0:8, lanes] += query_part * (2.0 * HEAD_DIM**-0.5)
            cross = mm(pr2[:, lanes], mixed[:, lanes], TN)
            value_part = jnp.zeros((8, GROUP), F32)
            for h in range(PER_GROUP):
                top = ((h + 1) % PER_GROUP) * HEAD_DIM + 8
                value_part = jnp.where(in_head[h], cross[top : top + 8], value_part)
            acc_ref[8:16, lanes] += 2.0 * value_part

        steps = [functools.partial(back1, part) for part in row_parts]
        if u == 0:
            steps.append(lambda: wait(weight_copies[3]))
        steps += [functools.partial(project, n) for n in range(0, width, GROUP)]
        steps.append(lambda: wait(state_copies[u][1:]))
        for g in range(groups):
            steps.append(functools.partial(begin, g))
            steps += [functools.partial(one_head, g, h) for h in range(PER_GROUP)]
            steps.append(functools.partial(end, g))
        return steps

    interleave(norm1(0))
    wait(weight_copies[2] + weight_copies[0])
    interleave(feed_in(0))
    wait(weight_copies[1])
    interleave(feed_out(0), norm1(1) if units > 1 else [])
    for u in range(units):
        later = u + 1 < units
        if u + 2 < units:
            start(state_copies[u + 2][:1])
        if later:
            start(state_copies[u + 1][1:])
        interleave(head_part(u), feed_in(u + 1) if later else [])
        interleave(feed_back(u), norm1(u + 2) if u + 2 < units else [])
        interleave(attention_back(u), feed_out(u + 1) if later else [])


def finish_call(segs, labels, small, wo, arrays, plan, kept, parts):
    gain, shift, bias, head = small
    units, rows, width = kept[0].shape
    hidden_part = arrays[0].shape[1]
    hidden = hidden_part * parts
    scratch = [pltpu.VMEM(a.shape[1:], a.dtype) for a in kept] * 2
    scratch += [pltpu.VMEM((rows, width), BF16)] * 3
    scratch += [pltpu.VMEM((rows, width), F32)] * 3
    scratch += [pltpu.VMEM((rows, 1), F32)] * 3
    scratch += [pltpu.VMEM((rows, width), F32)] * 2
    scratch += [pltpu.VMEM((rows, hidden), BF16)] * 4
    scratch += [
        pltpu.VMEM(wo.shape, BF16),
        pltpu.VMEM((parts, width, hidden_part), BF16),
        pltpu.VMEM((parts, hidden_part, width), BF16),
        pltpu.VMEM((parts, BIAS_ROWS, hidden_part), BF16),
        pltpu.VMEM((rows, width), BF16),
        pltpu.SemaphoreType.DMA((2, len(kept))),
        pltpu.SemaphoreType.DMA((len(plan) + 1,)),
    ]
    return pl.pallas_call(
        functools.partial(finish_kernel, plan=plan, arrays=len(arrays), parts=parts),
        out_shape=jax.ShapeDtypeStruct((ACC_ROWS, width), F32),
        in_specs=[VMEM] * 6 + [ANY] * (1 + len(arrays) + len(kept)),
        out_specs=VMEM,
        scratch_shapes=scratch,
        compiler_params=pltpu.CompilerParams(vmem_limit_bytes=62 * MIB),
        name="finish",
    )(segs, labels, gain, shift, bias, head, wo, *arrays, *kept)


def update_kernel(
    acc_ref,
    other_ref,
    up_ref,
    momentum_ref,
    head_ref,
    first_ref,
    second_ref,
    loss_ref,
    items_ref,
    norm_ref,
    moment_out,
    up_out,
    low_out,
    first_out,
    second_out,
    head_out,
    head_low_out,
):
    total = acc_ref[...] + other_ref[...]
    width = total.shape[1]
    rank = up_ref.shape[0] // 2
    items = total[17:18, 1:2]
    loss_ref[...] = total[17:18, 0:1]
    items_ref[...] = items
    adapter = total[0:16] / items
    head_grad = jnp.concatenate([total[16:17], total[17:18, 2:3]], axis=1) / items
    norm = jnp.sqrt(jnp.sum(adapter * adapter) + jnp.sum(head_grad * head_grad))
    norm_ref[...] = jnp.full((1, 1), norm, F32)
    factor = jnp.minimum(1.0, CLIP_NORM / (norm_ref[...] + 1e-06))
    moment = ORTHO_MOMENTUM * momentum_ref[...] + factor * adapter
    moment_out[...] = moment

    def dot(left, right, dims=NN):
        return lax.dot_general(
            left, right, dims, preferred_element_type=F32, precision=lax.Precision.HIGHEST
        )

    basis = []
    for i in range(2):
        part = moment[i * rank : (i + 1) * rank]
        size = jnp.sqrt(jnp.sum(jnp.sum(part * part, axis=1, keepdims=True), axis=0, keepdims=True))
        basis.append(part / (size + 1e-07))
    for sweep in range(5):
        gram = [dot(x, x, NT) for x in basis]
        poly = [NS_B * g + NS_C * dot(g, g) for g in gram]
        basis = [NS_A * x + dot(p, x) for x, p in zip(basis, poly)]
    up = up_ref[...] - ORTHO_STEP_SIZE * jnp.concatenate(basis, axis=0)
    up_out[...] = up
    low_out[...] = up.astype(BF16)

    clipped = factor * head_grad
    def as_row(ref):
        return ref[...].reshape(1, width + 1)

    first = BETA_ONE * as_row(first_ref) + (1.0 - BETA_ONE) * clipped
    second = BETA_TWO * as_row(second_ref) + (1.0 - BETA_TWO) * clipped * clipped
    first_hat = first / (1.0 - BETA_ONE**STEP)
    second_hat = second / (1.0 - BETA_TWO**STEP)
    head = as_row(head_ref)
    new_head = head - ADAM_RATE * (first_hat / (jnp.sqrt(second_hat) + ADAM_EPS) + DECAY * head)
    first_out[...] = first[0]
    second_out[...] = second[0]
    head_out[...] = new_head[0]
    head_low_out[...] = new_head[0].astype(BF16)


def update_call(acc, other, up, momentum, head, first, second):
    one = jax.ShapeDtypeStruct((1, 1), F32)
    flat = jax.ShapeDtypeStruct(up.shape, F32)
    row = jax.ShapeDtypeStruct(head.shape, F32)
    return pl.pallas_call(
        update_kernel,
        out_shape=[
            one,
            one,
            one,
            flat,
            flat,
            jax.ShapeDtypeStruct(up.shape, BF16),
            row,
            row,
            row,
            jax.ShapeDtypeStruct(head.shape, BF16),
        ],
        in_specs=[VMEM] * 7,
        out_specs=[VMEM] * 10,
        name="update",
    )(acc, other, up, momentum, head, first, second)


def swap(value, axis, bit):
    size = lax.axis_size(axis)
    return lax.ppermute(value, axis, [(i, i ^ bit) for i in range(size)])


class Weights:
    def __init__(self, owns, bias):
        parts = lax.axis_size("tensor")
        half = lax.rem(lax.axis_index("dp"), 2)
        self.owns = owns
        self.sizes = [own.shape[0] // 2 for own in owns]
        self.bias = jnp.pad(bias[None, :], ((0, BIAS_ROWS - 1), (0, 0)))
        cuts = [
            lax.dynamic_slice_in_dim(own, half * n, n, 0) for own, n in zip(owns, self.sizes)
        ]
        if cuts[0].shape[1] == cuts[1].shape[1]:
            cuts = [jnp.concatenate([*cuts, self.bias], axis=0)]
        else:
            cuts.append(self.bias)
        self.one = len(cuts) == 1
        mine = {0: cuts}
        bit = parts // 2
        while bit > 1:
            mine.update({r ^ bit: [swap(a, "tensor", bit) for a in mine[r]] for r in list(mine)})
            bit //= 2
        del mine[0]
        self.mine = mine

    def core(self, pieces):
        return {r ^ 1: [swap(a, "tensor", 1) for a in arrays] for r, arrays in pieces.items()}

    def across(self, pieces):
        return {r: [swap(a, "dp", 1) for a in arrays] for r, arrays in pieces.items()}

    def operands(self):
        arrays = [*self.owns, *self.core_own, self.bias, self.core_bias]
        plan = [(2, 4, 0, BIAS_ROWS, 0, None), (2, 5, 0, BIAS_ROWS, 1, None)]
        for i in range(2):
            n = 2 * self.sizes[i]
            plan += [(i, i, 0, n, 0, None), (i, 2 + i, 0, n, 1, None)]
        for pieces, is_mine in (
            (self.mine, True),
            (self.core_mine, True),
            (self.other, False),
            (self.core_other, False),
        ):
            for r, found in pieces.items():
                first = 0
                for i, n in enumerate([*self.sizes, BIAS_ROWS]):
                    array = len(arrays) + (0 if self.one else i)
                    if i < 2:
                        plan.append((i, array, first, n, r, is_mine))
                    elif is_mine:
                        plan.append((i, array, first, n, r, None))
                    first += n if self.one else 0
                arrays += found
        return arrays, tuple(sorted(plan, key=lambda step: step[0]))


def local(
    input_token_ids,
    segments,
    labels,
    embedding,
    position_embedding_table,
    norm_gain_rows,
    norm_shift_rows,
    query_key_value_weight,
    attention_output_weight,
    attention_bias_stack,
    feedforward_in_weight,
    feedforward_bias,
    feedforward_out_weight,
    adapter_down_weight,
    adapter_up_weight,
    adapter_momentum,
    head,
    head_first_moment,
    head_second_moment,
):
    length = input_token_ids.shape[-1]
    slots = labels.shape[-1]
    width = position_embedding_table.shape[1]
    rank = adapter_up_weight.shape[1]
    parts = lax.axis_size("tensor")
    ids = input_token_ids.reshape(-1, 1, length)
    all_ids = [ids] + [swap(ids, "tensor", r) for r in range(1, parts)]
    segs = segments.reshape(-1, 1, length)
    labs = labels.reshape(-1, 1, slots)
    units = ids.shape[0]


    all_ids, owns, bias = lax.optimization_barrier(
        (all_ids, [feedforward_in_weight, feedforward_out_weight], feedforward_bias)
    )
    weights = Weights(owns, bias)
    weights.core_own = [swap(own, "tensor", 1) for own in owns]
    weights.core_bias = swap(weights.bias, "tensor", 1)
    picked = embed_call(all_ids, embedding)
    (
        picked,
        weights.mine,
        weights.core_own,
        weights.core_bias,
        adapter_down_weight,
        adapter_up_weight,
        head_rows,
    ) = lax.optimization_barrier(
        (
            picked,
            weights.mine,
            weights.core_own,
            weights.core_bias,
            adapter_down_weight,
            adapter_up_weight,
            (head, head_first_moment, head_second_moment),
        )
    )
    weights.other = weights.across(weights.mine)
    weights.core_mine = weights.core(weights.mine)
    down = jnp.concatenate(
        [
            adapter_down_weight[0],
            adapter_down_weight[1],
            jnp.zeros((width, HEAD_DIM - 2 * rank), BF16),
        ],
        axis=1,
    )
    down = jnp.concatenate([down] * PER_GROUP, axis=1)
    twice = 2.0 * adapter_up_weight.astype(BF16)
    up = jnp.stack(
        [jnp.pad(twice[0], ((0, rank), (0, 0))), jnp.pad(twice[1], ((rank, 0), (0, 0)))]
    )
    picked = [picked[u * parts : (u + 1) * parts] for u in range(units)]

    small = (
        position_embedding_table,
        norm_gain_rows,
        norm_shift_rows,
        attention_bias_stack,
        down,
        up,
    )
    kept = None
    moved = []
    for u in range(units):
        while len(moved) < min(u + 2, units):
            sends = picked[len(moved)][1:]
            if moved:
                sends = lax.optimization_barrier((sends, moved[-1], kept))[0]
            moved.append([swap(a, "tensor", r + 1) for r, a in enumerate(sends)])
        if u == 0:
            moved[0], weights.core_mine = lax.optimization_barrier((moved[0], weights.core_mine))
        kept = attend_call(
            [picked[u][0], *moved[u]],
            segs[u],
            small,
            query_key_value_weight,
            attention_output_weight,
            kept,
            u,
            units,
        )

    weights.core_other = weights.core(lax.optimization_barrier((weights.other, kept))[0])
    arrays, plan = weights.operands()
    acc = finish_call(
        segs,
        labs,
        (norm_gain_rows, norm_shift_rows, attention_bias_stack, head_rows[0]),
        attention_output_weight,
        arrays,
        plan,
        kept,
        parts,
    )
    steps = []
    for axis in ("tensor", "dp"):
        bit = 1
        while bit < lax.axis_size(axis):
            steps.append((axis, bit))
            bit *= 2
    for axis, bit in steps[:-1]:
        acc = acc + swap(acc, axis, bit)
    other = swap(acc, *steps[-1])

    flat = (2 * rank, width)
    outs = update_call(
        acc,
        other,
        adapter_up_weight.reshape(flat),
        adapter_momentum.reshape(flat),
        *head_rows,
    )
    loss, items, norm, moment, new_up, low, first, second, new_head, head_low = outs
    shape = adapter_up_weight.shape
    return (
        loss[0, 0],
        items[0, 0],
        norm[0, 0],
        moment.reshape(shape),
        new_up.reshape(shape),
        low.reshape(shape),
        first,
        second,
        new_head,
        head_low,
    )


def solution(mesh):
    rows = P(None, ("dp", "tensor"), None)
    placed = (
        (rows, rows, rows, P("tensor", None))
        + (P(),) * 6
        + (P(None, "tensor"), P("tensor"), P("tensor", None))
        + (P(),) * 6
    )
    return jax.shard_map(
        local, mesh=mesh, in_specs=placed, out_specs=(P(),) * 10, check_vma=False
    )
```

```python
import functools
import math

import jax
import jax.numpy as jnp
from jax import lax
from jax.experimental import pallas as pl
from jax.experimental.pallas import tpu as pltpu
from jax.sharding import PartitionSpec as P

HEAD_DIM = 64
STEP = 10
LN_EPS = 1e-05
CLIP_NORM = 0.5
ORTHO_MOMENTUM = 0.5
ORTHO_STEP_SIZE = 1.0
NS_A = 3.4445
NS_B = -4.775
NS_C = 2.0315
BETA_ONE = 0.9
BETA_TWO = 0.999
ADAM_RATE = 0.05
ADAM_EPS = 1e-08
DECAY = 0.01

F32 = jnp.float32
BF16 = jnp.bfloat16
LANES = 128
GROUP = 256
PER_GROUP = GROUP // HEAD_DIM
BLOCK = 128
SPAN = 3 * BLOCK
STEP_ROWS = 64
VOCAB_BLOCK = 2048
RING = 6
UNROLL = 64
ACC_ROWS = 24
BIAS_ROWS = 16
MIB = 1024 * 1024
NN = (((1,), (0,)), ((), ()))
NT = (((1,), (1,)), ((), ()))
TN = (((0,), (0,)), ((), ()))
INV_SQRT2 = 1.0 / math.sqrt(2.0)
INV_SQRT_2PI = 1.0 / math.sqrt(2.0 * math.pi)

VMEM = pl.BlockSpec(memory_space=pltpu.VMEM)
SMEM = pl.BlockSpec(memory_space=pltpu.SMEM)
ANY = pl.BlockSpec(memory_space=pl.ANY)


def mm(left, right, dims=NN):
    return lax.dot_general(left, right, dims, preferred_element_type=F32)


def row_mean(rows):
    return jnp.mean(rows, axis=-1, keepdims=True)


def add_all(terms):
    return functools.reduce(jnp.add, terms)


def at(i):
    return pl.ds(pl.multiple_of(i * STEP_ROWS, STEP_ROWS), STEP_ROWS)


def embed_kernel(*refs, parts, units):
    ids = refs[:parts]
    table, tail = refs[parts : parts + 2]
    outs = refs[parts + 2 : parts + 2 + parts * units]
    scratch = refs[parts + 2 + parts * units :]
    feats = table.shape[0]
    full = table.shape[1] // VOCAB_BLOCK
    lanes = [(lo, min(lo + LANES, feats)) for lo in range(0, feats, LANES)]
    turned = scratch[: len(lanes)]
    picked = scratch[len(lanes) : 2 * len(lanes)]
    ring, stage, ring_sems, sems = scratch[2 * len(lanes) :]

    def fetch(i):
        cols = pl.ds(pl.multiple_of(i * VOCAB_BLOCK, VOCAB_BLOCK), VOCAB_BLOCK)
        slot = lax.rem(i, RING)
        return pltpu.make_async_copy(table.at[:, cols], ring.at[slot], ring_sems.at[slot])

    def turn_block(base, block):
        for c in range(0, VOCAB_BLOCK, GROUP):
            rows_at = pl.ds(pl.multiple_of(base + c, GROUP), GROUP)
            for (lo, hi), turn in zip(lanes, turned):
                turn[rows_at, :] = block[lo:hi, c : c + GROUP].T.astype(F32)

    for i in range(min(RING, full)):
        fetch(i).start()
    turn_block(full * VOCAB_BLOCK, tail)

    def step(i, carry):
        fetch(i).wait()
        turn_block(i * VOCAB_BLOCK, ring.at[lax.rem(i, RING)])

        @pl.when(i + RING < full)
        def _():
            fetch(i + RING).start()

        return carry

    lax.fori_loop(0, full, step, 0)

    length = stage.shape[1]
    copies = []
    for p, out in enumerate(outs):
        u, r = p // parts, p % parts
        slot = p % 2

        def rows(i, carry, u=u, r=r):
            top = pl.multiple_of(i * UNROLL, UNROLL)
            for j in range(UNROLL):
                token = ids[r][u, 0, top + j]
                for turn, pick in zip(turned, picked):
                    pick[pl.ds(top + j, 1), :] = turn[pl.ds(token, 1), :]
            return carry

        lax.fori_loop(0, length // UNROLL, rows, 0)
        if p >= 2:
            copies[p - 2].wait()
        for (lo, hi), pick in zip(lanes, picked):
            stage[slot, :, lo:hi] = pick[...].astype(BF16)
        copies.append(pltpu.make_async_copy(stage.at[slot], out, sems.at[slot]))
        copies[p].start()
    for copy in copies[-2:]:
        copy.wait()


def embed_call(ids, table):
    parts = len(ids)
    units, _, length = ids[0].shape
    feats, vocab = table.shape
    full = vocab // VOCAB_BLOCK
    widths = [min(LANES, feats - lo) for lo in range(0, feats, LANES)]
    scratch = [pltpu.VMEM(((full + 1) * VOCAB_BLOCK, w), F32) for w in widths]
    scratch += [pltpu.VMEM((length, w), F32) for w in widths]
    scratch += [
        pltpu.VMEM((RING, feats, VOCAB_BLOCK), BF16),
        pltpu.VMEM((2, length, feats), BF16),
        pltpu.SemaphoreType.DMA((RING,)),
        pltpu.SemaphoreType.DMA((2,)),
    ]
    last = pl.cdiv(vocab, VOCAB_BLOCK) - 1
    tail = pl.BlockSpec((feats, VOCAB_BLOCK), lambda i: (0, last), pipeline_mode=pl.Buffered(1))
    return pl.pallas_call(
        functools.partial(embed_kernel, parts=parts, units=units),
        grid=(1,),
        in_specs=[SMEM] * parts + [ANY, tail],
        out_specs=[ANY] * (parts * units),
        out_shape=[jax.ShapeDtypeStruct((length, feats), BF16)] * (parts * units),
        scratch_shapes=scratch,
        compiler_params=pltpu.CompilerParams(vmem_limit_bytes=62 * MIB),
        name="embed",
    )(*ids, table, table)


def interleave(*lists):
    done = [0] * len(lists)
    while any(n < len(steps) for n, steps in zip(done, lists)):
        share = [n / len(steps) if steps else 1.0 for n, steps in zip(done, lists)]
        i = share.index(min(share))
        lists[i][done[i]]()
        done[i] += 1


def tile_rows(t, rows):
    lo = min(max(2 * t - 1, 0) * BLOCK, rows - min(SPAN, rows))
    return lo, min((2 * t + 3) * BLOCK, rows)


def block_pieces(b, blocks):
    first, last = max(b - 1, 0), min(b + 1, blocks - 1)
    found = []
    for t in range(blocks * BLOCK // GROUP):
        lo, hi = max(first, 2 * t), min(last, 2 * t + 1)
        if lo <= hi:
            found.append((t, lo, hi))
    return found


def spread(values, t, lo, hi):
    zero_block = jnp.zeros((BLOCK, BLOCK), BF16)
    parts = [values] if lo == 2 * t else [zero_block, values]
    if hi == 2 * t:
        parts.append(zero_block)
    return parts[0] if len(parts) == 1 else jnp.concatenate(parts, axis=1)


def head_masks():
    head_of = lax.broadcasted_iota(jnp.int32, (1, GROUP), 1) // HEAD_DIM
    in_head = [head_of == h for h in range(PER_GROUP)]
    return in_head, [jnp.where(m, 1.0, 0.0).astype(BF16) for m in in_head]


def column(row):
    return jnp.broadcast_to(row, (8, row.shape[1])).T[:, 0:1]


def tile_product(tiles, right):
    rows = right.shape[0]
    res = [None] * (rows // BLOCK)
    for t, left in enumerate(tiles):
        part = mm(left, right[t * GROUP : (t + 1) * GROUP])
        first = tile_rows(t, rows)[0] // BLOCK
        for i in range(left.shape[0] // BLOCK):
            piece = part[i * BLOCK : (i + 1) * BLOCK]
            res[first + i] = piece if res[first + i] is None else res[first + i] + piece
    return jnp.concatenate(res, axis=0)


def stacked_scores(left, right, keep):
    rows = left.shape[0]
    found = []
    for t in range(rows // GROUP):
        lo, hi = tile_rows(t, rows)
        stack = jnp.concatenate([left[lo:hi] * keep[h] for h in range(PER_GROUP)], axis=0)
        found.append(mm(stack, right[t * GROUP : (t + 1) * GROUP], NT))
    return found


def attend_kernel(*refs, parts, unit, fresh):
    pieces = refs[:parts]
    seg_ref, gain_ref, shift_ref, bias_ref, down_ref, up_ref, pos_hbm, wqkv_hbm, wo_hbm = refs[
        parts : parts + 9
    ]
    refs = refs[parts + 9 + (0 if fresh else 6) :]
    outs, (x4, pos, wqkv, wo, start, xb, normed0, q, k, v, red, pr, probs, mixed, sems) = (
        refs[:6],
        refs[6:],
    )
    rows, width = normed0.shape
    groups = width // GROUP
    blocks = rows // BLOCK
    tiles = rows // GROUP
    row_parts = [slice(i, i + STEP_ROWS) for i in range(0, rows, STEP_ROWS)]
    me = lax.axis_index("tensor")

    in_copies = [
        pltpu.make_async_copy(piece, x4.at[jnp.bitwise_xor(me, r)], sems.at[r])
        for r, piece in enumerate(pieces)
    ]
    pos_copy = pltpu.make_async_copy(pos_hbm, pos, sems.at[parts])
    qkv_copy = pltpu.make_async_copy(wqkv_hbm, wqkv, sems.at[parts + 1])
    wo_copy = pltpu.make_async_copy(wo_hbm, wo, sems.at[parts + 2])
    start_out, k_out, v_out, red_out, pr_out = [
        pltpu.make_async_copy(ref, out.at[unit], sems.at[parts + 3 + i])
        for i, (ref, out) in enumerate(zip((start, k, v, red, pr), outs))
    ]

    def probs_copy(g):
        heads = pl.ds(g * PER_GROUP, PER_GROUP)
        return pltpu.make_async_copy(
            probs.at[heads], outs[5].at[unit, heads], sems.at[parts + 8 + g]
        )

    for copy in [pos_copy, *in_copies, qkv_copy, wo_copy]:
        copy.start()

    seg_row = seg_ref[unit].astype(F32)
    seg_col = column(seg_row)
    lane = lax.broadcasted_iota(jnp.int32, (rows, rows), 1)
    sub = lax.broadcasted_iota(jnp.int32, (rows, rows), 0)
    before = (seg_col == seg_row) & (lane < sub)
    place = jnp.sum(jnp.where(before, 1.0, 0.0), axis=1, keepdims=True).astype(jnp.int32)
    one_hot = jnp.where(lane == place, 1.0, 0.0).astype(BF16)
    pos_copy.wait()
    start[...] = mm(one_hot, pos[...])
    for copy in in_copies:
        copy.wait()
    start[...] += jnp.concatenate([x4[t] for t in range(parts)], axis=1).astype(F32)

    gain0, shift0 = gain_ref[0:1], shift_ref[0:1]
    for part in row_parts:
        x = start[part, :]
        off = x - row_mean(x)
        y = off * lax.rsqrt(row_mean(off * off) + LN_EPS) * gain0 + shift0
        normed0[part, :] = y + bias_ref[3:4]
        xb[part, :] = y.astype(BF16)

    rank = up_ref.shape[1]
    spot = lax.broadcasted_iota(jnp.int32, (rank, GROUP), 1) % HEAD_DIM
    line = lax.broadcasted_iota(jnp.int32, (rank, GROUP), 0)
    lows = [mm(xb[...], down_ref[i]).astype(BF16) for i in range(2)]
    ups = [up_ref[i].astype(BF16) * BF16(2.0) for i in range(2)]
    red[...] = add_all(
        [
            mm(low, jnp.where(spot == line + i * rank, 1.0, 0.0).astype(BF16))
            for i, low in enumerate(lows)
        ]
    ).astype(BF16)
    red_out.start()

    in_head, keep = head_masks()

    def far(b, c):
        hit = seg_col[b * BLOCK : (b + 1) * BLOCK] == seg_row[:, c * BLOCK : (c + 1) * BLOCK]
        return jnp.where(hit, 0.0, -1e9)

    away = {
        (b, c): far(b, c) for b in range(blocks) for c in range(max(b - 1, 0), min(b + 2, blocks))
    }
    memo = {}

    def project(g):
        lanes = slice(g * GROUP, (g + 1) * GROUP)

        def queries():
            new = mm(xb[...], wqkv[0, :, lanes]) + mm(lows[0], ups[0][:, lanes])
            q[:, lanes] = (new + bias_ref[0:1, lanes]).astype(BF16) * BF16(HEAD_DIM**-0.5)

        def keys():
            k[:, lanes] = (mm(xb[...], wqkv[1, :, lanes]) + bias_ref[1:2, lanes]).astype(BF16)

        def values():
            new = mm(xb[...], wqkv[2, :, lanes]) + mm(lows[1], ups[1][:, lanes])
            v[:, lanes] = (new + bias_ref[2:3, lanes]).astype(BF16)

        return [queries, keys, values]

    def attention(g):
        lanes = slice(g * GROUP, (g + 1) * GROUP)

        def begin():
            memo["scores"] = stacked_scores(q[:, lanes], k[:, lanes], keep)
            memo["out"] = jnp.zeros((rows, GROUP), F32)
            memo["low"] = jnp.zeros((rows, GROUP), F32)

        def one_head(h):
            vrh = v[:, lanes] * keep[h] + red[...] * (1 - keep[h])
            prob_tiles = [[] for _ in range(tiles)]
            for b in range(blocks):
                found = []
                for t, lo, hi in block_pieces(b, blocks):
                    first, last = tile_rows(t, rows)
                    top = h * (last - first) + b * BLOCK - first
                    lane_at = slice((lo - 2 * t) * BLOCK, (hi + 1 - 2 * t) * BLOCK)
                    s = memo["scores"][t][top : top + BLOCK, lane_at]
                    found.append(
                        s + jnp.concatenate([away[b, c] for c in range(lo, hi + 1)], axis=1)
                    )
                peak = functools.reduce(
                    jnp.maximum, [jnp.max(s, axis=1, keepdims=True) for s in found]
                )
                found = [jnp.exp(s - peak) for s in found]
                inv = 1.0 / add_all([jnp.sum(s, axis=1, keepdims=True) for s in found])
                for (t, lo, hi), s in zip(block_pieces(b, blocks), found):
                    prob_tiles[t].append(spread((s * inv).astype(BF16), t, lo, hi))
            prob_tiles = [jnp.concatenate(tile, axis=0) for tile in prob_tiles]
            for t, tile in enumerate(prob_tiles):
                probs[g * PER_GROUP + h, t, 0 : tile.shape[0], :] = tile
            res = tile_product(prob_tiles, vrh)
            memo["out"] = jnp.where(in_head[h], res, memo["out"])
            memo["low"] = jnp.where(in_head[(h + 1) % PER_GROUP], res, memo["low"])

        def end():
            mixed[:, lanes] = memo["out"].astype(BF16)
            pr[:, lanes] = memo["low"].astype(BF16)
            probs_copy(g).start()

        return [begin] + [functools.partial(one_head, h) for h in range(PER_GROUP)] + [end]

    def output(g):
        def step(n):
            lanes = slice(n, n + GROUP)
            add = mm(mixed[:, g * GROUP : (g + 1) * GROUP], wo[g * GROUP : (g + 1) * GROUP, lanes])
            start[:, lanes] = (normed0 if g == 0 else start)[:, lanes] + add

        return [functools.partial(step, n) for n in range(0, width, GROUP)]

    qkv_copy.wait()
    interleave(project(0))
    wo_copy.wait()
    for g in range(groups):
        others = project(g + 1) if g + 1 < groups else []
        if g + 1 == groups:
            k_out.start()
            v_out.start()
        interleave(attention(g), others + (output(g - 1) if g else []))
    pr_out.start()
    interleave(output(groups - 1))
    start_out.start()
    for copy in [start_out, k_out, v_out, red_out, pr_out] + [probs_copy(g) for g in range(groups)]:
        copy.wait()


def attend_call(pieces, seg, small, wqkv, wo, kept, unit, units):
    pos, gain, shift, bias, down, up = small
    parts = len(pieces)
    rows, feats = pieces[0].shape
    width = pos.shape[1]
    heads = width // HEAD_DIM
    tiles = rows // GROUP
    forms = [
        ((rows, width), F32),
        ((rows, width), BF16),
        ((rows, width), BF16),
        ((rows, GROUP), BF16),
        ((rows, width), BF16),
        ((heads, tiles, SPAN, GROUP), BF16),
    ]
    fresh = kept is None
    scratch = [
        pltpu.VMEM((parts, rows, feats), BF16),
        pltpu.VMEM(pos.shape, BF16),
        pltpu.VMEM(wqkv.shape, BF16),
        pltpu.VMEM(wo.shape, BF16),
        pltpu.VMEM((rows, width), F32),
        pltpu.VMEM((rows, width), BF16),
        pltpu.VMEM((rows, width), F32),
        pltpu.VMEM((rows, width), BF16),
        pltpu.VMEM((rows, width), BF16),
        pltpu.VMEM((rows, width), BF16),
        pltpu.VMEM((rows, GROUP), BF16),
        pltpu.VMEM((rows, width), BF16),
        pltpu.VMEM((heads, tiles, SPAN, GROUP), BF16),
        pltpu.VMEM((rows, width), BF16),
        pltpu.SemaphoreType.DMA((parts + 8 + width // GROUP,)),
    ]
    args = [*pieces, seg, gain, shift, bias, down, up, pos, wqkv, wo]
    aliases = {} if fresh else {len(args) + i: i for i in range(len(forms))}
    return pl.pallas_call(
        functools.partial(attend_kernel, parts=parts, unit=unit, fresh=fresh),
        out_shape=[jax.ShapeDtypeStruct((units, *shape), kind) for shape, kind in forms],
        in_specs=[ANY] * parts + [VMEM] * 6 + [ANY] * 3 + ([] if fresh else [ANY] * len(forms)),
        out_specs=[ANY] * len(forms),
        input_output_aliases=aliases,
        scratch_shapes=scratch,
        compiler_params=pltpu.CompilerParams(vmem_limit_bytes=58 * MIB),
        cost_estimate=pl.CostEstimate(
            flops=rows * width,
            bytes_accessed=MIB // 4,
            transcendentals=0,
        ),
        name="attend",
    )(*args, *([] if fresh else kept))


def finish_kernel(*refs, plan, arrays, parts):
    seg_ref, label_ref, gain_ref, shift_ref, bias_ref, head_ref, wo_hbm, *refs = refs
    weight_refs, refs = refs[:arrays], refs[arrays:]
    kept, refs = refs[:6], refs[6:]
    acc_ref, refs = refs[0], refs[1:]
    bufs, refs = (refs[:6], refs[6:12]), refs[12:]
    xbs, xh1s, stats, refs = refs[:3], refs[3:6], refs[6:9], refs[9:]
    accs, slopes, acts, refs = refs[:2], refs[2:4], refs[4:6], refs[6:]
    wo, win, wout, ffb, mixed, sems, wsems = refs
    units = kept[0].shape[0]
    rows, width = mixed.shape
    hidden_part = win.shape[2]
    chunk = GROUP if hidden_part % GROUP == 0 else hidden_part
    groups = width // GROUP
    blocks = rows // BLOCK
    tiles = rows // GROUP
    row_parts = [slice(i, i + STEP_ROWS) for i in range(0, rows, STEP_ROWS)]
    chunks = [(r, c) for r in range(parts) for c in range(0, hidden_part, chunk)]
    half = lax.rem(lax.axis_index("dp"), 2)

    weight_copies = [[], [], [], []]
    for i, (matrix, array, first, n, r, mine) in enumerate(plan):
        dst = (win, wout, ffb)[matrix].at[r]
        if mine is not None:
            top = pl.multiple_of((half if mine else 1 - half) * n, 16)
            dst = (win, wout, ffb)[matrix].at[r, pl.ds(top, n), :]
        src = weight_refs[array].at[pl.ds(first, n), :]
        weight_copies[matrix].append(pltpu.make_async_copy(src, dst, wsems.at[i]))
    weight_copies[3].append(pltpu.make_async_copy(wo_hbm, wo, wsems.at[len(plan)]))

    state_copies = [
        [
            pltpu.make_async_copy(src.at[u], buf, sems.at[u % 2, i])
            for i, (src, buf) in enumerate(zip(kept, bufs[u % 2]))
        ]
        for u in range(units)
    ]

    def start(copies):
        for copy in copies:
            copy.start()

    def wait(copies):
        for copy in copies:
            copy.wait()

    start(state_copies[0][:1] + weight_copies[2] + weight_copies[0] + weight_copies[1])
    for u in range(1, min(2, units)):
        start(state_copies[u][:1])
    start(weight_copies[3] + state_copies[0][1:])

    gain1, gain2 = gain_ref[1:2], gain_ref[2:3]
    shift1, shift2 = shift_ref[1:2], shift_ref[2:3]
    head_row = head_ref[...].reshape(1, width + 1)
    head, head_bias = head_row[:, 0:width], head_row[:, width : width + 1]
    hg = head * gain2
    hg_mean = row_mean(hg)
    bias4 = bias_ref[4:5]
    base = jnp.sum(shift2 * head, axis=1, keepdims=True)
    in_head, keep = head_masks()
    acc_ref[...] = jnp.zeros(acc_ref.shape, F32)

    def norm1(u):
        resid, xb, xh1, stat1 = bufs[u % 2][0], xbs[u % 3], xh1s[u % 3], stats[u % 3]

        def step(part):
            x = resid[part, :]
            off = x - row_mean(x)
            inv = lax.rsqrt(row_mean(off * off) + LN_EPS)
            xh = off * inv
            xh1[part, :] = xh
            stat1[part, :] = inv
            xb[part, :] = (xh * gain1 + shift1).astype(BF16)

        return [lambda: wait(state_copies[u][:1])] + [
            functools.partial(step, part) for part in row_parts
        ]

    def hidden(r, c):
        return slice(r * hidden_part + c, r * hidden_part + c + chunk)

    def feed_in(u):
        xb, act, slope = xbs[u % 3], acts[u % 2], slopes[u % 2]

        def step(r, c):
            line = ffb[r, 0:1, c : c + chunk].astype(F32)
            pre = mm(xb[...], win[r, :, c : c + chunk]) + line
            phi = 0.5 + 0.5 * lax.erf(pre * INV_SQRT2)
            act[:, hidden(r, c)] = (pre * phi).astype(BF16)
            tail = pre * jnp.exp(-0.5 * pre * pre) * INV_SQRT_2PI
            slope[:, hidden(r, c)] = (phi + tail).astype(BF16)

        return [functools.partial(step, r, c) for r, c in chunks]

    def feed_out(u):
        act, acc = acts[u % 2], accs[u % 2]

        def step(n, r):
            lanes = slice(n, n + GROUP)
            add = mm(act[:, r * hidden_part : (r + 1) * hidden_part], wout[r, :, lanes])
            acc[:, lanes] = add if r == 0 else acc[:, lanes] + add

        return [
            functools.partial(step, n, r) for n in range(0, width, GROUP) for r in range(parts)
        ]

    def head_part(u):
        xb, xh1, acc = xbs[u % 3], xh1s[u % 3], accs[u % 2]
        memo = {"inv": [], "dots": [], "grad": jnp.zeros((8, width), F32)}

        def norm2(part):
            x = xh1[part, :] * gain1 + shift1 + (acc[part, :] + bias4)
            off = x - row_mean(x)
            inv = lax.rsqrt(row_mean(off * off) + LN_EPS)
            xh = off * inv
            acc[part, :] = xh
            memo["inv"].append(inv)
            memo["dots"].append(jnp.sum(xh * hg, axis=1, keepdims=True))

        def items():
            dots = jnp.concatenate(memo["dots"], axis=0)
            seg_row = seg_ref[u].astype(F32)
            seg_col = column(seg_row)
            label = label_ref[u]
            slots = label.shape[1]
            slot_no = lax.broadcasted_iota(jnp.int32, (rows, slots), 1).astype(F32)
            member = jnp.where(seg_col == slot_no, 1.0, 0.0)
            counts = jnp.sum(member, axis=0, keepdims=True)
            sums = jnp.sum(member * (dots + base), axis=0, keepdims=True)
            most = jnp.maximum(counts, 1.0)
            error = jnp.where(counts > 0, sums / most + head_bias - label, 0.0)
            grad_pred = 2.0 * error
            memo["weight"] = jnp.sum(member * (grad_pred / most), axis=1, keepdims=True)
            loss = jnp.sum(error * error, axis=1, keepdims=True)
            weight_sum = jnp.sum(grad_pred, axis=1, keepdims=True)
            memo["sum"] = weight_sum
            count = jnp.max(seg_row, axis=1, keepdims=True) + 1.0
            lane_row = lax.broadcasted_iota(jnp.int32, (1, width), 1)
            acc_ref[17:18, :] += jnp.where(
                lane_row == 0,
                loss,
                jnp.where(lane_row == 1, count, jnp.where(lane_row == 2, weight_sum, 0.0)),
            )

        def back2(i, part):
            xh = acc[part, :]
            w = memo["weight"][part]
            weighted = xh * w
            for j in range(STEP_ROWS // 8):
                memo["grad"] = memo["grad"] + weighted[j * 8 : (j + 1) * 8]
            scaled = memo["dots"][i] * (1.0 / width)
            grad = (memo["inv"][i] * w) * (hg - hg_mean - xh * scaled)
            acc[part, :] = grad
            xb[part, :] = grad.astype(BF16)

        def close():
            total = jnp.sum(memo["grad"], axis=0, keepdims=True)
            acc_ref[16:17, :] += total * gain2 + memo["sum"] * shift2

        return (
            [functools.partial(norm2, part) for part in row_parts]
            + [items]
            + [functools.partial(back2, i, part) for i, part in enumerate(row_parts)]
            + [close]
        )

    def feed_back(u):
        xb, act, slope, acc = xbs[u % 3], acts[u % 2], slopes[u % 2], accs[u % 2]

        def up(r, c):
            back = mm(xb[...], wout[r, c : c + chunk, :], NT)
            act[:, hidden(r, c)] = (back * slope[:, hidden(r, c)].astype(F32)).astype(BF16)

        def down(n, r):
            lanes = slice(n, n + GROUP)
            acc[:, lanes] += mm(
                act[:, r * hidden_part : (r + 1) * hidden_part], win[r, lanes, :], NT
            )

        return [functools.partial(up, r, c) for r, c in chunks] + [
            functools.partial(down, n, r) for n in range(0, width, GROUP) for r in range(parts)
        ]

    def attention_back(u):
        xb, xh1, stat1, acc = xbs[u % 3], xh1s[u % 3], stats[u % 3], accs[u % 2]
        _, k2, v2, red2, pr2, probs2 = bufs[u % 2]
        memo = {}

        def back1(part):
            g = acc[part, :] * gain1
            xh = xh1[part, :]
            grad = stat1[part, :] * (g - row_mean(g) - xh * row_mean(g * xh))
            xb[part, :] = grad.astype(BF16)

        def project(n):
            mixed[:, n : n + GROUP] = mm(xb[...], wo[n : n + GROUP, :], NT).astype(BF16)

        def begin(g):
            lanes = slice(g * GROUP, (g + 1) * GROUP)
            memo["grads"] = stacked_scores(mixed[:, lanes], v2[:, lanes], keep)
            memo["out"] = jnp.zeros((rows, GROUP), F32)

        def one_head(g, h):
            lanes = slice(g * GROUP, (g + 1) * GROUP)
            score_tiles = [[] for _ in range(tiles)]
            for b in range(blocks):
                found = []
                for t, lo, hi in block_pieces(b, blocks):
                    first, last = tile_rows(t, rows)
                    top = b * BLOCK - first
                    lane_at = slice((lo - 2 * t) * BLOCK, (hi + 1 - 2 * t) * BLOCK)
                    here = h * (last - first) + top
                    dp = memo["grads"][t][here : here + BLOCK, lane_at]
                    p = probs2[g * PER_GROUP + h, t, top : top + BLOCK, lane_at]
                    found.append((p.astype(F32), dp))
                shared = add_all([jnp.sum(p * dp, axis=1, keepdims=True) for p, dp in found])
                for (t, lo, hi), (p, dp) in zip(block_pieces(b, blocks), found):
                    score_tiles[t].append(spread((p * (dp - shared)).astype(BF16), t, lo, hi))
            tiles_ = [jnp.concatenate(tile, axis=0) for tile in score_tiles]
            memo["out"] = jnp.where(in_head[h], tile_product(tiles_, k2[:, lanes]), memo["out"])

        def end(g):
            lanes = slice(g * GROUP, (g + 1) * GROUP)
            query_part = mm(red2[...], memo["out"].astype(BF16), TN)[0:8]
            acc_ref[0:8, lanes] += query_part * (2.0 * HEAD_DIM**-0.5)
            cross = mm(pr2[:, lanes], mixed[:, lanes], TN)
            value_part = jnp.zeros((8, GROUP), F32)
            for h in range(PER_GROUP):
                top = ((h + 1) % PER_GROUP) * HEAD_DIM + 8
                value_part = jnp.where(in_head[h], cross[top : top + 8], value_part)
            acc_ref[8:16, lanes] += 2.0 * value_part

        steps = [functools.partial(back1, part) for part in row_parts]
        if u == 0:
            steps.append(lambda: wait(weight_copies[3]))
        steps += [functools.partial(project, n) for n in range(0, width, GROUP)]
        steps.append(lambda: wait(state_copies[u][1:]))
        for g in range(groups):
            steps.append(functools.partial(begin, g))
            steps += [functools.partial(one_head, g, h) for h in range(PER_GROUP)]
            steps.append(functools.partial(end, g))
        return steps

    interleave(norm1(0))
    wait(weight_copies[2] + weight_copies[0])
    interleave(feed_in(0))
    wait(weight_copies[1])
    interleave(feed_out(0), norm1(1) if units > 1 else [])
    for u in range(units):
        later = u + 1 < units
        if u + 2 < units:
            start(state_copies[u + 2][:1])
        if later:
            start(state_copies[u + 1][1:])
        interleave(head_part(u), feed_in(u + 1) if later else [])
        interleave(feed_back(u), norm1(u + 2) if u + 2 < units else [])
        interleave(attention_back(u), feed_out(u + 1) if later else [])


def finish_call(segs, labels, small, wo, arrays, plan, kept, parts):
    gain, shift, bias, head = small
    units, rows, width = kept[0].shape
    hidden_part = arrays[0].shape[1]
    hidden = hidden_part * parts
    scratch = [pltpu.VMEM(a.shape[1:], a.dtype) for a in kept] * 2
    scratch += [pltpu.VMEM((rows, width), BF16)] * 3
    scratch += [pltpu.VMEM((rows, width), F32)] * 3
    scratch += [pltpu.VMEM((rows, 1), F32)] * 3
    scratch += [pltpu.VMEM((rows, width), F32)] * 2
    scratch += [pltpu.VMEM((rows, hidden), BF16)] * 4
    scratch += [
        pltpu.VMEM(wo.shape, BF16),
        pltpu.VMEM((parts, width, hidden_part), BF16),
        pltpu.VMEM((parts, hidden_part, width), BF16),
        pltpu.VMEM((parts, BIAS_ROWS, hidden_part), BF16),
        pltpu.VMEM((rows, width), BF16),
        pltpu.SemaphoreType.DMA((2, len(kept))),
        pltpu.SemaphoreType.DMA((len(plan) + 1,)),
    ]
    return pl.pallas_call(
        functools.partial(finish_kernel, plan=plan, arrays=len(arrays), parts=parts),
        out_shape=jax.ShapeDtypeStruct((ACC_ROWS, width), F32),
        in_specs=[VMEM] * 6 + [ANY] * (1 + len(arrays) + len(kept)),
        out_specs=VMEM,
        scratch_shapes=scratch,
        compiler_params=pltpu.CompilerParams(vmem_limit_bytes=62 * MIB),
        name="finish",
    )(segs, labels, gain, shift, bias, head, wo, *arrays, *kept)


def update_kernel(
    acc_ref,
    other_ref,
    up_ref,
    momentum_ref,
    head_ref,
    first_ref,
    second_ref,
    loss_ref,
    items_ref,
    norm_ref,
    moment_out,
    up_out,
    low_out,
    first_out,
    second_out,
    head_out,
    head_low_out,
):
    total = acc_ref[...] + other_ref[...]
    width = total.shape[1]
    rank = up_ref.shape[0] // 2
    items = total[17:18, 1:2]
    loss_ref[...] = total[17:18, 0:1]
    items_ref[...] = items
    adapter = total[0:16] / items
    head_grad = jnp.concatenate([total[16:17], total[17:18, 2:3]], axis=1) / items
    norm = jnp.sqrt(jnp.sum(adapter * adapter) + jnp.sum(head_grad * head_grad))
    norm_ref[...] = jnp.full((1, 1), norm, F32)
    factor = jnp.minimum(1.0, CLIP_NORM / (norm_ref[...] + 1e-06))
    moment = ORTHO_MOMENTUM * momentum_ref[...] + factor * adapter
    moment_out[...] = moment

    def dot(left, right, dims=NN):
        return lax.dot_general(
            left, right, dims, preferred_element_type=F32, precision=lax.Precision.HIGHEST
        )

    basis = []
    for i in range(2):
        part = moment[i * rank : (i + 1) * rank]
        size = jnp.sqrt(jnp.sum(jnp.sum(part * part, axis=1, keepdims=True), axis=0, keepdims=True))
        basis.append(part / (size + 1e-07))
    for sweep in range(5):
        gram = [dot(x, x, NT) for x in basis]
        poly = [NS_B * g + NS_C * dot(g, g) for g in gram]
        basis = [NS_A * x + dot(p, x) for x, p in zip(basis, poly)]
    up = up_ref[...] - ORTHO_STEP_SIZE * jnp.concatenate(basis, axis=0)
    up_out[...] = up
    low_out[...] = up.astype(BF16)

    clipped = factor * head_grad
    def as_row(ref):
        return ref[...].reshape(1, width + 1)

    first = BETA_ONE * as_row(first_ref) + (1.0 - BETA_ONE) * clipped
    second = BETA_TWO * as_row(second_ref) + (1.0 - BETA_TWO) * clipped * clipped
    first_hat = first / (1.0 - BETA_ONE**STEP)
    second_hat = second / (1.0 - BETA_TWO**STEP)
    head = as_row(head_ref)
    new_head = head - ADAM_RATE * (first_hat / (jnp.sqrt(second_hat) + ADAM_EPS) + DECAY * head)
    first_out[...] = first[0]
    second_out[...] = second[0]
    head_out[...] = new_head[0]
    head_low_out[...] = new_head[0].astype(BF16)


def update_call(acc, other, up, momentum, head, first, second):
    one = jax.ShapeDtypeStruct((1, 1), F32)
    flat = jax.ShapeDtypeStruct(up.shape, F32)
    row = jax.ShapeDtypeStruct(head.shape, F32)
    return pl.pallas_call(
        update_kernel,
        out_shape=[
            one,
            one,
            one,
            flat,
            flat,
            jax.ShapeDtypeStruct(up.shape, BF16),
            row,
            row,
            row,
            jax.ShapeDtypeStruct(head.shape, BF16),
        ],
        in_specs=[VMEM] * 7,
        out_specs=[VMEM] * 10,
        name="update",
    )(acc, other, up, momentum, head, first, second)


def swap(value, axis, bit):
    size = lax.axis_size(axis)
    return lax.ppermute(value, axis, [(i, i ^ bit) for i in range(size)])


class Weights:
    def __init__(self, owns, bias, after):
        parts = lax.axis_size("tensor")
        half = lax.rem(lax.axis_index("dp"), 2)
        self.owns = owns
        self.sizes = [own.shape[0] // 2 for own in owns]
        self.bias = jnp.pad(bias[None, :], ((0, BIAS_ROWS - 1), (0, 0)))
        cuts = [
            lax.dynamic_slice_in_dim(own, half * n, n, 0) for own, n in zip(owns, self.sizes)
        ]
        if cuts[0].shape[1] == cuts[1].shape[1]:
            cuts = [jnp.concatenate([*cuts, self.bias], axis=0)]
        else:
            cuts.append(self.bias)
        self.one = len(cuts) == 1
        cuts, self.first = lax.optimization_barrier((cuts, after))
        mine = {0: cuts}
        bit = parts // 2
        while bit > 1:
            mine.update({r ^ bit: [swap(a, "tensor", bit) for a in mine[r]] for r in list(mine)})
            bit //= 2
        del mine[0]
        self.mine = mine

    def core(self, pieces):
        return {r ^ 1: [swap(a, "tensor", 1) for a in arrays] for r, arrays in pieces.items()}

    def across(self, pieces):
        return {r: [swap(a, "dp", 1) for a in arrays] for r, arrays in pieces.items()}

    def operands(self):
        arrays = [*self.owns, *self.core_own, self.bias, self.core_bias]
        plan = [(2, 4, 0, BIAS_ROWS, 0, None), (2, 5, 0, BIAS_ROWS, 1, None)]
        for i in range(2):
            n = 2 * self.sizes[i]
            plan += [(i, i, 0, n, 0, None), (i, 2 + i, 0, n, 1, None)]
        for pieces, is_mine in (
            (self.mine, True),
            (self.core_mine, True),
            (self.other, False),
            (self.core_other, False),
        ):
            for r, found in pieces.items():
                first = 0
                for i, n in enumerate([*self.sizes, BIAS_ROWS]):
                    array = len(arrays) + (0 if self.one else i)
                    if i < 2:
                        plan.append((i, array, first, n, r, is_mine))
                    elif is_mine:
                        plan.append((i, array, first, n, r, None))
                    first += n if self.one else 0
                arrays += found
        return arrays, tuple(sorted(plan, key=lambda step: step[0]))


def local(
    input_token_ids,
    segments,
    labels,
    embedding,
    position_embedding_table,
    norm_gain_rows,
    norm_shift_rows,
    query_key_value_weight,
    attention_output_weight,
    attention_bias_stack,
    feedforward_in_weight,
    feedforward_bias,
    feedforward_out_weight,
    adapter_down_weight,
    adapter_up_weight,
    adapter_momentum,
    head,
    head_first_moment,
    head_second_moment,
):
    length = input_token_ids.shape[-1]
    slots = labels.shape[-1]
    width = position_embedding_table.shape[1]
    rank = adapter_up_weight.shape[1]
    parts = lax.axis_size("tensor")
    ids = input_token_ids.reshape(-1, 1, length)
    all_ids = [ids] + [swap(ids, "tensor", r) for r in range(1, parts)]
    segs = segments.reshape(-1, 1, length)
    labs = labels.reshape(-1, 1, slots)
    units = ids.shape[0]


    weights = Weights([feedforward_in_weight, feedforward_out_weight], feedforward_bias, all_ids)
    all_ids, owns = lax.optimization_barrier((weights.first, weights.owns))
    weights.core_own = [swap(own, "tensor", 1) for own in owns]
    weights.core_bias = swap(weights.bias, "tensor", 1)
    picked = embed_call(all_ids, embedding)
    (
        picked,
        weights.mine,
        weights.core_own,
        weights.core_bias,
        head_rows,
    ) = lax.optimization_barrier(
        (
            picked,
            weights.mine,
            weights.core_own,
            weights.core_bias,
            (head, head_first_moment, head_second_moment),
        )
    )
    picked = [picked[u * parts : (u + 1) * parts] for u in range(units)]

    small = (
        position_embedding_table,
        norm_gain_rows,
        norm_shift_rows,
        attention_bias_stack,
        adapter_down_weight,
        adapter_up_weight,
    )
    kept = None
    moved = []
    for u in range(units):
        while len(moved) < min(u + 2, units):
            sends = picked[len(moved)][1:]
            if moved:
                sends = lax.optimization_barrier((sends, moved[-1], kept))[0]
            moved.append([swap(a, "tensor", r + 1) for r, a in enumerate(sends)])
        if u == units - 1:
            other, moved[u], _ = lax.optimization_barrier((weights.other, moved[u], kept))
            weights.core_other = weights.core(other)
        if u == 0:
            mine, moved[0] = lax.optimization_barrier((weights.mine, moved[0]))
            weights.other = weights.across(mine)
            weights.core_mine = weights.core(mine)
        kept = attend_call(
            [picked[u][0], *moved[u]],
            segs,
            small,
            query_key_value_weight,
            attention_output_weight,
            kept,
            u,
            units,
        )

    arrays, plan = weights.operands()
    acc = finish_call(
        segs,
        labs,
        (norm_gain_rows, norm_shift_rows, attention_bias_stack, head_rows[0]),
        attention_output_weight,
        arrays,
        plan,
        kept,
        parts,
    )
    steps = []
    for axis in ("tensor", "dp"):
        bit = 1
        while bit < lax.axis_size(axis):
            steps.append((axis, bit))
            bit *= 2
    for axis, bit in steps[:-1]:
        acc = acc + swap(acc, axis, bit)
    other = swap(acc, *steps[-1])

    flat = (2 * rank, width)
    outs = update_call(
        acc,
        other,
        adapter_up_weight.reshape(flat),
        adapter_momentum.reshape(flat),
        *head_rows,
    )
    loss, items, norm, moment, new_up, low, first, second, new_head, head_low = outs
    shape = adapter_up_weight.shape
    return (
        loss[0, 0],
        items[0, 0],
        norm[0, 0],
        moment.reshape(shape),
        new_up.reshape(shape),
        low.reshape(shape),
        first,
        second,
        new_head,
        head_low,
    )


def solution(mesh):
    rows = P(None, ("dp", "tensor"), None)
    placed = (
        (rows, rows, rows, P("tensor", None))
        + (P(),) * 6
        + (P(None, "tensor"), P("tensor"), P("tensor", None))
        + (P(),) * 6
    )
    return jax.shard_map(
        local, mesh=mesh, in_specs=placed, out_specs=(P(),) * 10, check_vma=False
    )
```

```python
import functools
import math

import jax
import jax.numpy as jnp
from jax import lax
from jax.experimental import pallas as pl
from jax.experimental.pallas import tpu as pltpu
from jax.sharding import PartitionSpec as P

HEAD_DIM = 64
STEP = 10
LN_EPS = 1e-05
CLIP_NORM = 0.5
ORTHO_MOMENTUM = 0.5
ORTHO_STEP_SIZE = 1.0
NS_A = 3.4445
NS_B = -4.775
NS_C = 2.0315
BETA_ONE = 0.9
BETA_TWO = 0.999
ADAM_RATE = 0.05
ADAM_EPS = 1e-08
DECAY = 0.01

F32 = jnp.float32
BF16 = jnp.bfloat16
LANES = 128
GROUP = 256
PER_GROUP = GROUP // HEAD_DIM
BLOCK = 128
SPAN = 3 * BLOCK
STEP_ROWS = 64
VOCAB_BLOCK = 2048
RING = 6
UNROLL = 64
ACC_ROWS = 24
ADAPTER_ROWS = 16
BIAS_ROWS = 16
MIB = 1024 * 1024
NN = (((1,), (0,)), ((), ()))
NT = (((1,), (1,)), ((), ()))
TN = (((0,), (0,)), ((), ()))
INV_SQRT2 = 1.0 / math.sqrt(2.0)
INV_SQRT_2PI = 1.0 / math.sqrt(2.0 * math.pi)

VMEM = pl.BlockSpec(memory_space=pltpu.VMEM)
SMEM = pl.BlockSpec(memory_space=pltpu.SMEM)
ANY = pl.BlockSpec(memory_space=pl.ANY)


def mm(left, right, dims=NN):
    return lax.dot_general(left, right, dims, preferred_element_type=F32)


def row_mean(rows):
    return jnp.mean(rows, axis=-1, keepdims=True)


def add_all(terms):
    return functools.reduce(jnp.add, terms)


def at(i):
    return pl.ds(pl.multiple_of(i * STEP_ROWS, STEP_ROWS), STEP_ROWS)


def embed_kernel(*refs, parts, units):
    ids = refs[:parts]
    table, tail = refs[parts : parts + 2]
    outs = refs[parts + 2 : parts + 2 + parts * units]
    scratch = refs[parts + 2 + parts * units :]
    feats = table.shape[0]
    full = table.shape[1] // VOCAB_BLOCK
    lanes = [(lo, min(lo + LANES, feats)) for lo in range(0, feats, LANES)]
    turned = scratch[: len(lanes)]
    picked = scratch[len(lanes) : 2 * len(lanes)]
    ring, stage, ring_sems, sems = scratch[2 * len(lanes) :]

    def fetch(i):
        cols = pl.ds(pl.multiple_of(i * VOCAB_BLOCK, VOCAB_BLOCK), VOCAB_BLOCK)
        slot = lax.rem(i, RING)
        return pltpu.make_async_copy(table.at[:, cols], ring.at[slot], ring_sems.at[slot])

    def turn_block(base, block):
        for c in range(0, VOCAB_BLOCK, GROUP):
            rows_at = pl.ds(pl.multiple_of(base + c, GROUP), GROUP)
            for (lo, hi), turn in zip(lanes, turned):
                turn[rows_at, :] = block[lo:hi, c : c + GROUP].T.astype(F32)

    for i in range(min(RING, full)):
        fetch(i).start()
    turn_block(full * VOCAB_BLOCK, tail)

    def step(i, carry):
        fetch(i).wait()
        turn_block(i * VOCAB_BLOCK, ring.at[lax.rem(i, RING)])

        @pl.when(i + RING < full)
        def _():
            fetch(i + RING).start()

        return carry

    lax.fori_loop(0, full, step, 0)

    length = stage.shape[1]
    copies = []
    for p, out in enumerate(outs):
        u, r = p // parts, p % parts
        slot = p % 2

        def rows(i, carry, u=u, r=r):
            top = pl.multiple_of(i * UNROLL, UNROLL)
            for j in range(UNROLL):
                token = ids[r][u, 0, top + j]
                for turn, pick in zip(turned, picked):
                    pick[pl.ds(top + j, 1), :] = turn[pl.ds(token, 1), :]
            return carry

        lax.fori_loop(0, length // UNROLL, rows, 0)
        if p >= 2:
            copies[p - 2].wait()
        for (lo, hi), pick in zip(lanes, picked):
            stage[slot, :, lo:hi] = pick[...].astype(BF16)
        copies.append(pltpu.make_async_copy(stage.at[slot], out, sems.at[slot]))
        copies[p].start()
    for copy in copies[-2:]:
        copy.wait()


def embed_call(ids, table):
    parts = len(ids)
    units, _, length = ids[0].shape
    feats, vocab = table.shape
    full = vocab // VOCAB_BLOCK
    widths = [min(LANES, feats - lo) for lo in range(0, feats, LANES)]
    scratch = [pltpu.VMEM(((full + 1) * VOCAB_BLOCK, w), F32) for w in widths]
    scratch += [pltpu.VMEM((length, w), F32) for w in widths]
    scratch += [
        pltpu.VMEM((RING, feats, VOCAB_BLOCK), BF16),
        pltpu.VMEM((2, length, feats), BF16),
        pltpu.SemaphoreType.DMA((RING,)),
        pltpu.SemaphoreType.DMA((2,)),
    ]
    last = pl.cdiv(vocab, VOCAB_BLOCK) - 1
    tail = pl.BlockSpec((feats, VOCAB_BLOCK), lambda i: (0, last), pipeline_mode=pl.Buffered(1))
    return pl.pallas_call(
        functools.partial(embed_kernel, parts=parts, units=units),
        grid=(1,),
        in_specs=[SMEM] * parts + [ANY, tail],
        out_specs=[ANY] * (parts * units),
        out_shape=[jax.ShapeDtypeStruct((length, feats), BF16)] * (parts * units),
        scratch_shapes=scratch,
        compiler_params=pltpu.CompilerParams(vmem_limit_bytes=62 * MIB),
        name="embed",
    )(*ids, table, table)


def interleave(*lists):
    done = [0] * len(lists)
    while any(n < len(steps) for n, steps in zip(done, lists)):
        share = [n / len(steps) if steps else 1.0 for n, steps in zip(done, lists)]
        i = share.index(min(share))
        lists[i][done[i]]()
        done[i] += 1


def tile_rows(t, rows):
    lo = min(max(2 * t - 1, 0) * BLOCK, rows - min(SPAN, rows))
    return lo, min((2 * t + 3) * BLOCK, rows)


def block_pieces(b, blocks):
    first, last = max(b - 1, 0), min(b + 1, blocks - 1)
    found = []
    for t in range(blocks * BLOCK // GROUP):
        lo, hi = max(first, 2 * t), min(last, 2 * t + 1)
        if lo <= hi:
            found.append((t, lo, hi))
    return found


def spread(values, t, lo, hi):
    zero_block = jnp.zeros((BLOCK, BLOCK), BF16)
    parts = [values] if lo == 2 * t else [zero_block, values]
    if hi == 2 * t:
        parts.append(zero_block)
    return parts[0] if len(parts) == 1 else jnp.concatenate(parts, axis=1)


def head_masks():
    head_of = lax.broadcasted_iota(jnp.int32, (1, GROUP), 1) // HEAD_DIM
    in_head = [head_of == h for h in range(PER_GROUP)]
    return in_head, [jnp.where(m, 1.0, 0.0).astype(BF16) for m in in_head]


def column(row):
    return jnp.broadcast_to(row, (8, row.shape[1])).T[:, 0:1]


def tile_product(tiles, right):
    rows = right.shape[0]
    res = [None] * (rows // BLOCK)
    for t, left in enumerate(tiles):
        part = mm(left, right[t * GROUP : (t + 1) * GROUP])
        first = tile_rows(t, rows)[0] // BLOCK
        for i in range(left.shape[0] // BLOCK):
            piece = part[i * BLOCK : (i + 1) * BLOCK]
            res[first + i] = piece if res[first + i] is None else res[first + i] + piece
    return jnp.concatenate(res, axis=0)


def stacked_scores(left, right, keep):
    rows = left.shape[0]
    found = []
    for t in range(rows // GROUP):
        lo, hi = tile_rows(t, rows)
        stack = jnp.concatenate([left[lo:hi] * keep[h] for h in range(PER_GROUP)], axis=0)
        found.append(mm(stack, right[t * GROUP : (t + 1) * GROUP], NT))
    return found


def attend_kernel(*refs, parts, unit, fresh):
    pieces = refs[:parts]
    seg_ref, gain_ref, shift_ref, bias_ref, down_ref, up_ref, pos_hbm, wqkv_hbm, wo_hbm = refs[
        parts : parts + 9
    ]
    refs = refs[parts + 9 + (0 if fresh else 6) :]
    outs, (x4, pos, wqkv, wo, start, xb, normed0, q, k, v, red, pr, probs, mixed, sems) = (
        refs[:6],
        refs[6:],
    )
    rows, width = normed0.shape
    groups = width // GROUP
    blocks = rows // BLOCK
    tiles = rows // GROUP
    row_parts = [slice(i, i + STEP_ROWS) for i in range(0, rows, STEP_ROWS)]
    me = lax.axis_index("tensor")

    in_copies = [
        pltpu.make_async_copy(piece, x4.at[jnp.bitwise_xor(me, r)], sems.at[r])
        for r, piece in enumerate(pieces)
    ]
    pos_copy = pltpu.make_async_copy(pos_hbm, pos, sems.at[parts])
    qkv_copy = pltpu.make_async_copy(wqkv_hbm, wqkv, sems.at[parts + 1])
    wo_copy = pltpu.make_async_copy(wo_hbm, wo, sems.at[parts + 2])
    start_out, k_out, v_out, red_out, pr_out = [
        pltpu.make_async_copy(ref, out.at[unit], sems.at[parts + 3 + i])
        for i, (ref, out) in enumerate(zip((start, k, v, red, pr), outs))
    ]

    def probs_copy(g):
        heads = pl.ds(g * PER_GROUP, PER_GROUP)
        return pltpu.make_async_copy(
            probs.at[heads], outs[5].at[unit, heads], sems.at[parts + 8 + g]
        )

    for copy in [pos_copy, *in_copies, qkv_copy, wo_copy]:
        copy.start()

    seg_row = seg_ref[unit].astype(F32)
    seg_col = column(seg_row)
    lane = lax.broadcasted_iota(jnp.int32, (rows, rows), 1)
    sub = lax.broadcasted_iota(jnp.int32, (rows, rows), 0)
    before = (seg_col == seg_row) & (lane < sub)
    place = jnp.sum(jnp.where(before, 1.0, 0.0), axis=1, keepdims=True).astype(jnp.int32)
    one_hot = jnp.where(lane == place, 1.0, 0.0).astype(BF16)
    pos_copy.wait()
    start[...] = mm(one_hot, pos[...])
    for copy in in_copies:
        copy.wait()
    start[...] += jnp.concatenate([x4[t] for t in range(parts)], axis=1).astype(F32)

    gain0, shift0 = gain_ref[0:1], shift_ref[0:1]
    for part in row_parts:
        x = start[part, :]
        off = x - row_mean(x)
        y = off * lax.rsqrt(row_mean(off * off) + LN_EPS) * gain0 + shift0
        normed0[part, :] = y + bias_ref[3:4]
        xb[part, :] = y.astype(BF16)

    rank = up_ref.shape[1]
    spot = lax.broadcasted_iota(jnp.int32, (rank, GROUP), 1) % HEAD_DIM
    line = lax.broadcasted_iota(jnp.int32, (rank, GROUP), 0)
    lows = [mm(xb[...], down_ref[i], NT).astype(BF16) for i in range(2)]
    ups = [up_ref[i].astype(BF16) * BF16(2.0) for i in range(2)]
    red[...] = add_all(
        [
            mm(low, jnp.where(spot == line + i * rank, 1.0, 0.0).astype(BF16))
            for i, low in enumerate(lows)
        ]
    ).astype(BF16)
    red_out.start()

    in_head, keep = head_masks()

    def far(b, c):
        hit = seg_col[b * BLOCK : (b + 1) * BLOCK] == seg_row[:, c * BLOCK : (c + 1) * BLOCK]
        return jnp.where(hit, 0.0, -1e9)

    away = {
        (b, c): far(b, c) for b in range(blocks) for c in range(max(b - 1, 0), min(b + 2, blocks))
    }
    memo = {}

    def project(g):
        lanes = slice(g * GROUP, (g + 1) * GROUP)

        def queries():
            new = mm(xb[...], wqkv[0, :, lanes]) + mm(lows[0], ups[0][:, lanes])
            q[:, lanes] = (new + bias_ref[0:1, lanes]).astype(BF16) * BF16(HEAD_DIM**-0.5)

        def keys():
            k[:, lanes] = (mm(xb[...], wqkv[1, :, lanes]) + bias_ref[1:2, lanes]).astype(BF16)

        def values():
            new = mm(xb[...], wqkv[2, :, lanes]) + mm(lows[1], ups[1][:, lanes])
            v[:, lanes] = (new + bias_ref[2:3, lanes]).astype(BF16)

        return [queries, keys, values]

    def attention(g):
        lanes = slice(g * GROUP, (g + 1) * GROUP)

        def begin():
            memo["scores"] = stacked_scores(q[:, lanes], k[:, lanes], keep)
            memo["out"] = jnp.zeros((rows, GROUP), F32)
            memo["low"] = jnp.zeros((rows, GROUP), F32)

        def one_head(h):
            vrh = v[:, lanes] * keep[h] + red[...] * (1 - keep[h])
            prob_tiles = [[] for _ in range(tiles)]
            for b in range(blocks):
                found = []
                for t, lo, hi in block_pieces(b, blocks):
                    first, last = tile_rows(t, rows)
                    top = h * (last - first) + b * BLOCK - first
                    lane_at = slice((lo - 2 * t) * BLOCK, (hi + 1 - 2 * t) * BLOCK)
                    s = memo["scores"][t][top : top + BLOCK, lane_at]
                    found.append(
                        s + jnp.concatenate([away[b, c] for c in range(lo, hi + 1)], axis=1)
                    )
                peak = functools.reduce(
                    jnp.maximum, [jnp.max(s, axis=1, keepdims=True) for s in found]
                )
                found = [jnp.exp(s - peak) for s in found]
                inv = 1.0 / add_all([jnp.sum(s, axis=1, keepdims=True) for s in found])
                for (t, lo, hi), s in zip(block_pieces(b, blocks), found):
                    prob_tiles[t].append(spread((s * inv).astype(BF16), t, lo, hi))
            prob_tiles = [jnp.concatenate(tile, axis=0) for tile in prob_tiles]
            for t, tile in enumerate(prob_tiles):
                probs[g * PER_GROUP + h, t, 0 : tile.shape[0], :] = tile
            res = tile_product(prob_tiles, vrh)
            memo["out"] = jnp.where(in_head[h], res, memo["out"])
            memo["low"] = jnp.where(in_head[(h + 1) % PER_GROUP], res, memo["low"])

        def end():
            mixed[:, lanes] = memo["out"].astype(BF16)
            pr[:, lanes] = memo["low"].astype(BF16)
            probs_copy(g).start()

        return [begin] + [functools.partial(one_head, h) for h in range(PER_GROUP)] + [end]

    def output(g):
        def step(n):
            lanes = slice(n, n + GROUP)
            add = mm(mixed[:, g * GROUP : (g + 1) * GROUP], wo[g * GROUP : (g + 1) * GROUP, lanes])
            start[:, lanes] = (normed0 if g == 0 else start)[:, lanes] + add

        return [functools.partial(step, n) for n in range(0, width, GROUP)]

    qkv_copy.wait()
    interleave(project(0))
    wo_copy.wait()
    for g in range(groups):
        others = project(g + 1) if g + 1 < groups else []
        if g + 1 == groups:
            k_out.start()
            v_out.start()
        interleave(attention(g), others + (output(g - 1) if g else []))
    pr_out.start()
    interleave(output(groups - 1))
    start_out.start()
    for copy in [start_out, k_out, v_out, red_out, pr_out] + [probs_copy(g) for g in range(groups)]:
        copy.wait()


def attend_call(pieces, seg, small, wqkv, wo, kept, unit, units):
    pos, gain, shift, bias, down, up = small
    parts = len(pieces)
    rows, feats = pieces[0].shape
    width = pos.shape[1]
    heads = width // HEAD_DIM
    tiles = rows // GROUP
    forms = [
        ((rows, width), F32),
        ((rows, width), BF16),
        ((rows, width), BF16),
        ((rows, GROUP), BF16),
        ((rows, width), BF16),
        ((heads, tiles, SPAN, GROUP), BF16),
    ]
    fresh = kept is None
    scratch = [
        pltpu.VMEM((parts, rows, feats), BF16),
        pltpu.VMEM(pos.shape, BF16),
        pltpu.VMEM(wqkv.shape, BF16),
        pltpu.VMEM(wo.shape, BF16),
        pltpu.VMEM((rows, width), F32),
        pltpu.VMEM((rows, width), BF16),
        pltpu.VMEM((rows, width), F32),
        pltpu.VMEM((rows, width), BF16),
        pltpu.VMEM((rows, width), BF16),
        pltpu.VMEM((rows, width), BF16),
        pltpu.VMEM((rows, GROUP), BF16),
        pltpu.VMEM((rows, width), BF16),
        pltpu.VMEM((heads, tiles, SPAN, GROUP), BF16),
        pltpu.VMEM((rows, width), BF16),
        pltpu.SemaphoreType.DMA((parts + 8 + width // GROUP,)),
    ]
    args = [*pieces, seg, gain, shift, bias, down, up, pos, wqkv, wo]
    aliases = {} if fresh else {len(args) + i: i for i in range(len(forms))}
    return pl.pallas_call(
        functools.partial(attend_kernel, parts=parts, unit=unit, fresh=fresh),
        out_shape=[jax.ShapeDtypeStruct((units, *shape), kind) for shape, kind in forms],
        in_specs=[ANY] * parts + [VMEM] * 6 + [ANY] * 3 + ([] if fresh else [ANY] * len(forms)),
        out_specs=[ANY] * len(forms),
        input_output_aliases=aliases,
        scratch_shapes=scratch,
        compiler_params=pltpu.CompilerParams(vmem_limit_bytes=58 * MIB),
        cost_estimate=pl.CostEstimate(
            flops=rows * width,
            bytes_accessed=MIB // 4,
            transcendentals=0,
        ),
        name="attend",
    )(*args, *([] if fresh else kept))


def finish_kernel(*refs, plan, arrays, parts):
    seg_ref, label_ref, gain_ref, shift_ref, bias_ref, head_ref, wo_hbm, *refs = refs
    weight_refs, refs = refs[:arrays], refs[arrays:]
    kept, refs = refs[:6], refs[6:]
    packed_ref, acc_ref, refs = refs[0], refs[1], refs[2:]
    bufs, refs = (refs[:6], refs[6:12]), refs[12:]
    xbs, xh1s, stats, refs = refs[:3], refs[3:6], refs[6:9], refs[9:]
    accs, slopes, acts, refs = refs[:2], refs[2:4], refs[4:6], refs[6:]
    wo, win, wout, ffb, mixed, sems, wsems = refs
    units = kept[0].shape[0]
    rows, width = mixed.shape
    hidden_part = win.shape[2]
    chunk = GROUP if hidden_part % GROUP == 0 else hidden_part
    groups = width // GROUP
    blocks = rows // BLOCK
    tiles = rows // GROUP
    row_parts = [slice(i, i + STEP_ROWS) for i in range(0, rows, STEP_ROWS)]
    chunks = [(r, c) for r in range(parts) for c in range(0, hidden_part, chunk)]
    half = lax.rem(lax.axis_index("dp"), 2)

    weight_copies = [[], [], [], []]
    for i, (matrix, array, first, n, r, mine) in enumerate(plan):
        dst = (win, wout, ffb)[matrix].at[r]
        if mine is not None:
            top = pl.multiple_of((half if mine else 1 - half) * n, 16)
            dst = (win, wout, ffb)[matrix].at[r, pl.ds(top, n), :]
        src = weight_refs[array].at[pl.ds(first, n), :]
        weight_copies[matrix].append(pltpu.make_async_copy(src, dst, wsems.at[i]))
    weight_copies[3].append(pltpu.make_async_copy(wo_hbm, wo, wsems.at[len(plan)]))

    state_copies = [
        [
            pltpu.make_async_copy(src.at[u], buf, sems.at[u % 2, i])
            for i, (src, buf) in enumerate(zip(kept, bufs[u % 2]))
        ]
        for u in range(units)
    ]

    def start(copies):
        for copy in copies:
            copy.start()

    def wait(copies):
        for copy in copies:
            copy.wait()

    start(state_copies[0][:1] + weight_copies[2] + weight_copies[0] + weight_copies[1])
    for u in range(1, min(2, units)):
        start(state_copies[u][:1])
    start(weight_copies[3] + state_copies[0][1:])

    gain1, gain2 = gain_ref[1:2], gain_ref[2:3]
    shift1, shift2 = shift_ref[1:2], shift_ref[2:3]
    head_row = head_ref[...].reshape(1, width + 1)
    head, head_bias = head_row[:, 0:width], head_row[:, width : width + 1]
    hg = head * gain2
    hg_mean = row_mean(hg)
    bias4 = bias_ref[4:5]
    base = jnp.sum(shift2 * head, axis=1, keepdims=True)
    in_head, keep = head_masks()
    acc_ref[...] = jnp.zeros(acc_ref.shape, F32)

    def norm1(u):
        resid, xb, xh1, stat1 = bufs[u % 2][0], xbs[u % 3], xh1s[u % 3], stats[u % 3]

        def step(part):
            x = resid[part, :]
            off = x - row_mean(x)
            inv = lax.rsqrt(row_mean(off * off) + LN_EPS)
            xh = off * inv
            xh1[part, :] = xh
            stat1[part, :] = inv
            xb[part, :] = (xh * gain1 + shift1).astype(BF16)

        return [lambda: wait(state_copies[u][:1])] + [
            functools.partial(step, part) for part in row_parts
        ]

    def hidden(r, c):
        return slice(r * hidden_part + c, r * hidden_part + c + chunk)

    def feed_in(u):
        xb, act, slope = xbs[u % 3], acts[u % 2], slopes[u % 2]

        def step(r, c):
            line = ffb[r, 0:1, c : c + chunk].astype(F32)
            pre = mm(xb[...], win[r, :, c : c + chunk]) + line
            phi = 0.5 + 0.5 * lax.erf(pre * INV_SQRT2)
            act[:, hidden(r, c)] = (pre * phi).astype(BF16)
            tail = pre * jnp.exp(-0.5 * pre * pre) * INV_SQRT_2PI
            slope[:, hidden(r, c)] = (phi + tail).astype(BF16)

        return [functools.partial(step, r, c) for r, c in chunks]

    def feed_out(u):
        act, acc = acts[u % 2], accs[u % 2]

        def step(n, r):
            lanes = slice(n, n + GROUP)
            add = mm(act[:, r * hidden_part : (r + 1) * hidden_part], wout[r, :, lanes])
            acc[:, lanes] = add if r == 0 else acc[:, lanes] + add

        return [
            functools.partial(step, n, r) for n in range(0, width, GROUP) for r in range(parts)
        ]

    def head_part(u):
        xb, xh1, acc = xbs[u % 3], xh1s[u % 3], accs[u % 2]
        memo = {"inv": [], "dots": [], "grad": jnp.zeros((8, width), F32)}

        def norm2(part):
            x = xh1[part, :] * gain1 + shift1 + (acc[part, :] + bias4)
            off = x - row_mean(x)
            inv = lax.rsqrt(row_mean(off * off) + LN_EPS)
            xh = off * inv
            acc[part, :] = xh
            memo["inv"].append(inv)
            memo["dots"].append(jnp.sum(xh * hg, axis=1, keepdims=True))

        def items():
            dots = jnp.concatenate(memo["dots"], axis=0)
            seg_row = seg_ref[u].astype(F32)
            seg_col = column(seg_row)
            label = label_ref[u]
            slots = label.shape[1]
            slot_no = lax.broadcasted_iota(jnp.int32, (rows, slots), 1).astype(F32)
            member = jnp.where(seg_col == slot_no, 1.0, 0.0)
            counts = jnp.sum(member, axis=0, keepdims=True)
            sums = jnp.sum(member * (dots + base), axis=0, keepdims=True)
            most = jnp.maximum(counts, 1.0)
            error = jnp.where(counts > 0, sums / most + head_bias - label, 0.0)
            grad_pred = 2.0 * error
            memo["weight"] = jnp.sum(member * (grad_pred / most), axis=1, keepdims=True)
            loss = jnp.sum(error * error, axis=1, keepdims=True)
            weight_sum = jnp.sum(grad_pred, axis=1, keepdims=True)
            memo["sum"] = weight_sum
            count = jnp.max(seg_row, axis=1, keepdims=True) + 1.0
            lane_row = lax.broadcasted_iota(jnp.int32, (1, width), 1)
            acc_ref[17:18, :] += jnp.where(
                lane_row == 0,
                loss,
                jnp.where(lane_row == 1, count, jnp.where(lane_row == 2, weight_sum, 0.0)),
            )

        def back2(i, part):
            xh = acc[part, :]
            w = memo["weight"][part]
            weighted = xh * w
            for j in range(STEP_ROWS // 8):
                memo["grad"] = memo["grad"] + weighted[j * 8 : (j + 1) * 8]
            scaled = memo["dots"][i] * (1.0 / width)
            grad = (memo["inv"][i] * w) * (hg - hg_mean - xh * scaled)
            acc[part, :] = grad
            xb[part, :] = grad.astype(BF16)

        def close():
            total = jnp.sum(memo["grad"], axis=0, keepdims=True)
            acc_ref[16:17, :] += total * gain2 + memo["sum"] * shift2

        return (
            [functools.partial(norm2, part) for part in row_parts]
            + [items]
            + [functools.partial(back2, i, part) for i, part in enumerate(row_parts)]
            + [close]
        )

    def feed_back(u):
        xb, act, slope, acc = xbs[u % 3], acts[u % 2], slopes[u % 2], accs[u % 2]

        def up(r, c):
            back = mm(xb[...], wout[r, c : c + chunk, :], NT)
            act[:, hidden(r, c)] = (back * slope[:, hidden(r, c)].astype(F32)).astype(BF16)

        def down(n, r):
            lanes = slice(n, n + GROUP)
            acc[:, lanes] += mm(
                act[:, r * hidden_part : (r + 1) * hidden_part], win[r, lanes, :], NT
            )

        return [functools.partial(up, r, c) for r, c in chunks] + [
            functools.partial(down, n, r) for n in range(0, width, GROUP) for r in range(parts)
        ]

    def attention_back(u):
        xb, xh1, stat1, acc = xbs[u % 3], xh1s[u % 3], stats[u % 3], accs[u % 2]
        _, k2, v2, red2, pr2, probs2 = bufs[u % 2]
        memo = {}

        def back1(part):
            g = acc[part, :] * gain1
            xh = xh1[part, :]
            grad = stat1[part, :] * (g - row_mean(g) - xh * row_mean(g * xh))
            xb[part, :] = grad.astype(BF16)

        def project(n):
            mixed[:, n : n + GROUP] = mm(xb[...], wo[n : n + GROUP, :], NT).astype(BF16)

        def begin(g):
            lanes = slice(g * GROUP, (g + 1) * GROUP)
            memo["grads"] = stacked_scores(mixed[:, lanes], v2[:, lanes], keep)
            memo["out"] = jnp.zeros((rows, GROUP), F32)

        def one_head(g, h):
            lanes = slice(g * GROUP, (g + 1) * GROUP)
            score_tiles = [[] for _ in range(tiles)]
            for b in range(blocks):
                found = []
                for t, lo, hi in block_pieces(b, blocks):
                    first, last = tile_rows(t, rows)
                    top = b * BLOCK - first
                    lane_at = slice((lo - 2 * t) * BLOCK, (hi + 1 - 2 * t) * BLOCK)
                    here = h * (last - first) + top
                    dp = memo["grads"][t][here : here + BLOCK, lane_at]
                    p = probs2[g * PER_GROUP + h, t, top : top + BLOCK, lane_at]
                    found.append((p.astype(F32), dp))
                shared = add_all([jnp.sum(p * dp, axis=1, keepdims=True) for p, dp in found])
                for (t, lo, hi), (p, dp) in zip(block_pieces(b, blocks), found):
                    score_tiles[t].append(spread((p * (dp - shared)).astype(BF16), t, lo, hi))
            tiles_ = [jnp.concatenate(tile, axis=0) for tile in score_tiles]
            memo["out"] = jnp.where(in_head[h], tile_product(tiles_, k2[:, lanes]), memo["out"])

        def end(g):
            lanes = slice(g * GROUP, (g + 1) * GROUP)
            query_part = mm(red2[...], memo["out"].astype(BF16), TN)[0:8]
            acc_ref[0:8, lanes] += query_part * (2.0 * HEAD_DIM**-0.5)
            cross = mm(pr2[:, lanes], mixed[:, lanes], TN)
            value_part = jnp.zeros((8, GROUP), F32)
            for h in range(PER_GROUP):
                top = ((h + 1) % PER_GROUP) * HEAD_DIM + 8
                value_part = jnp.where(in_head[h], cross[top : top + 8], value_part)
            acc_ref[8:16, lanes] += 2.0 * value_part

        steps = [functools.partial(back1, part) for part in row_parts]
        if u == 0:
            steps.append(lambda: wait(weight_copies[3]))
        steps += [functools.partial(project, n) for n in range(0, width, GROUP)]
        steps.append(lambda: wait(state_copies[u][1:]))
        for g in range(groups):
            steps.append(functools.partial(begin, g))
            steps += [functools.partial(one_head, g, h) for h in range(PER_GROUP)]
            steps.append(functools.partial(end, g))
        return steps

    interleave(norm1(0))
    wait(weight_copies[2] + weight_copies[0])
    interleave(feed_in(0))
    wait(weight_copies[1])
    interleave(feed_out(0), norm1(1) if units > 1 else [])
    for u in range(units):
        later = u + 1 < units
        if u + 2 < units:
            start(state_copies[u + 2][:1])
        if later:
            start(state_copies[u + 1][1:])
        interleave(head_part(u), feed_in(u + 1) if later else [])
        interleave(feed_back(u), norm1(u + 2) if u + 2 < units else [])
        interleave(attention_back(u), feed_out(u + 1) if later else [])

    slabs = width // LANES
    for j in range(slabs):
        lanes = slice(j * LANES, (j + 1) * LANES)
        packed_ref[j * ADAPTER_ROWS : (j + 1) * ADAPTER_ROWS, :] = acc_ref[0:ADAPTER_ROWS, lanes]
    rest = [acc_ref[16:17, j * LANES : (j + 1) * LANES] for j in range(slabs)]
    rest.append(acc_ref[17:18, 0:LANES])
    empty = packed_ref.shape[0] - slabs * ADAPTER_ROWS - len(rest)
    if empty:
        rest.append(jnp.zeros((empty, LANES), F32))
    packed_ref[slabs * ADAPTER_ROWS :, :] = jnp.concatenate(rest, axis=0)


def packed_rows(width):
    slabs = width // LANES
    return pl.cdiv(slabs * ADAPTER_ROWS + slabs + 1, 8) * 8


def finish_call(segs, labels, small, wo, arrays, plan, kept, parts):
    gain, shift, bias, head = small
    units, rows, width = kept[0].shape
    hidden_part = arrays[0].shape[1]
    hidden = hidden_part * parts
    scratch = [pltpu.VMEM((ACC_ROWS, width), F32)]
    scratch += [pltpu.VMEM(a.shape[1:], a.dtype) for a in kept] * 2
    scratch += [pltpu.VMEM((rows, width), BF16)] * 3
    scratch += [pltpu.VMEM((rows, width), F32)] * 3
    scratch += [pltpu.VMEM((rows, 1), F32)] * 3
    scratch += [pltpu.VMEM((rows, width), F32)] * 2
    scratch += [pltpu.VMEM((rows, hidden), BF16)] * 4
    scratch += [
        pltpu.VMEM(wo.shape, BF16),
        pltpu.VMEM((parts, width, hidden_part), BF16),
        pltpu.VMEM((parts, hidden_part, width), BF16),
        pltpu.VMEM((parts, BIAS_ROWS, hidden_part), BF16),
        pltpu.VMEM((rows, width), BF16),
        pltpu.SemaphoreType.DMA((2, len(kept))),
        pltpu.SemaphoreType.DMA((len(plan) + 1,)),
    ]
    return pl.pallas_call(
        functools.partial(finish_kernel, plan=plan, arrays=len(arrays), parts=parts),
        out_shape=jax.ShapeDtypeStruct((packed_rows(width), LANES), F32),
        in_specs=[VMEM] * 6 + [ANY] * (1 + len(arrays) + len(kept)),
        out_specs=VMEM,
        scratch_shapes=scratch,
        compiler_params=pltpu.CompilerParams(vmem_limit_bytes=62 * MIB),
        name="finish",
    )(segs, labels, gain, shift, bias, head, wo, *arrays, *kept)


def update_kernel(
    acc_ref,
    other_ref,
    up_ref,
    momentum_ref,
    head_ref,
    first_ref,
    second_ref,
    loss_ref,
    items_ref,
    norm_ref,
    moment_out,
    up_out,
    low_out,
    first_out,
    second_out,
    head_out,
    head_low_out,
):
    total = acc_ref[...] + other_ref[...]
    width = up_ref.shape[1]
    rank = up_ref.shape[0] // 2
    slabs = width // LANES
    top = slabs * ADAPTER_ROWS
    sums = total[top + slabs : top + slabs + 1]
    items = sums[:, 1:2]
    loss_ref[...] = sums[:, 0:1]
    items_ref[...] = items
    adapter = (
        jnp.concatenate(
            [total[j * ADAPTER_ROWS : (j + 1) * ADAPTER_ROWS] for j in range(slabs)], axis=1
        )
        / items
    )
    head_grad = [total[top + j : top + j + 1] for j in range(slabs)] + [sums[:, 2:3]]
    head_grad = jnp.concatenate(head_grad, axis=1) / items
    norm = jnp.sqrt(jnp.sum(adapter * adapter) + jnp.sum(head_grad * head_grad))
    norm_ref[...] = jnp.full((1, 1), norm, F32)
    factor = jnp.minimum(1.0, CLIP_NORM / (norm_ref[...] + 1e-06))
    moment = ORTHO_MOMENTUM * momentum_ref[...] + factor * adapter
    moment_out[...] = moment

    def dot(left, right, dims=NN):
        return lax.dot_general(
            left, right, dims, preferred_element_type=F32, precision=lax.Precision.HIGHEST
        )

    basis = []
    for i in range(2):
        part = moment[i * rank : (i + 1) * rank]
        size = jnp.sqrt(jnp.sum(jnp.sum(part * part, axis=1, keepdims=True), axis=0, keepdims=True))
        basis.append(part / (size + 1e-07))
    for sweep in range(5):
        gram = [dot(x, x, NT) for x in basis]
        poly = [NS_B * g + NS_C * dot(g, g) for g in gram]
        basis = [NS_A * x + dot(p, x) for x, p in zip(basis, poly)]
    up = up_ref[...] - ORTHO_STEP_SIZE * jnp.concatenate(basis, axis=0)
    up_out[...] = up
    low_out[...] = up.astype(BF16)

    clipped = factor * head_grad
    def as_row(ref):
        return ref[...].reshape(1, width + 1)

    first = BETA_ONE * as_row(first_ref) + (1.0 - BETA_ONE) * clipped
    second = BETA_TWO * as_row(second_ref) + (1.0 - BETA_TWO) * clipped * clipped
    first_hat = first / (1.0 - BETA_ONE**STEP)
    second_hat = second / (1.0 - BETA_TWO**STEP)
    head = as_row(head_ref)
    new_head = head - ADAM_RATE * (first_hat / (jnp.sqrt(second_hat) + ADAM_EPS) + DECAY * head)
    first_out[...] = first[0]
    second_out[...] = second[0]
    head_out[...] = new_head[0]
    head_low_out[...] = new_head[0].astype(BF16)


def update_call(acc, other, up, momentum, head, first, second):
    one = jax.ShapeDtypeStruct((1, 1), F32)
    flat = jax.ShapeDtypeStruct(up.shape, F32)
    row = jax.ShapeDtypeStruct(head.shape, F32)
    return pl.pallas_call(
        update_kernel,
        out_shape=[
            one,
            one,
            one,
            flat,
            flat,
            jax.ShapeDtypeStruct(up.shape, BF16),
            row,
            row,
            row,
            jax.ShapeDtypeStruct(head.shape, BF16),
        ],
        in_specs=[VMEM] * 7,
        out_specs=[VMEM] * 10,
        name="update",
    )(acc, other, up, momentum, head, first, second)


def swap(value, axis, bit):
    size = lax.axis_size(axis)
    return lax.ppermute(value, axis, [(i, i ^ bit) for i in range(size)])


class Weights:
    def __init__(self, owns, bias, after):
        parts = lax.axis_size("tensor")
        half = lax.rem(lax.axis_index("dp"), 2)
        self.owns = owns
        self.sizes = [own.shape[0] // 2 for own in owns]
        self.bias = jnp.pad(bias[None, :], ((0, BIAS_ROWS - 1), (0, 0)))
        cuts = [
            lax.dynamic_slice_in_dim(own, half * n, n, 0) for own, n in zip(owns, self.sizes)
        ]
        if cuts[0].shape[1] == cuts[1].shape[1]:
            cuts = [jnp.concatenate([*cuts, self.bias], axis=0)]
        else:
            cuts.append(self.bias)
        self.one = len(cuts) == 1
        cuts, self.first = lax.optimization_barrier((cuts, after))
        mine = {0: cuts}
        bit = parts // 2
        while bit > 1:
            mine.update({r ^ bit: [swap(a, "tensor", bit) for a in mine[r]] for r in list(mine)})
            bit //= 2
        del mine[0]
        self.mine = mine

    def core(self, pieces):
        return {r ^ 1: [swap(a, "tensor", 1) for a in arrays] for r, arrays in pieces.items()}

    def across(self, pieces):
        return {r: [swap(a, "dp", 1) for a in arrays] for r, arrays in pieces.items()}

    def operands(self):
        arrays = [*self.owns, *self.core_own, self.bias, self.core_bias]
        plan = [(2, 4, 0, BIAS_ROWS, 0, None), (2, 5, 0, BIAS_ROWS, 1, None)]
        for i in range(2):
            n = 2 * self.sizes[i]
            plan += [(i, i, 0, n, 0, None), (i, 2 + i, 0, n, 1, None)]
        for pieces, is_mine in (
            (self.mine, True),
            (self.core_mine, True),
            (self.other, False),
            (self.core_other, False),
        ):
            for r, found in pieces.items():
                first = 0
                for i, n in enumerate([*self.sizes, BIAS_ROWS]):
                    array = len(arrays) + (0 if self.one else i)
                    if i < 2:
                        plan.append((i, array, first, n, r, is_mine))
                    elif is_mine:
                        plan.append((i, array, first, n, r, None))
                    first += n if self.one else 0
                arrays += found
        return arrays, tuple(sorted(plan, key=lambda step: step[0]))


def local(
    input_token_ids,
    segments,
    labels,
    embedding,
    position_embedding_table,
    norm_gain_rows,
    norm_shift_rows,
    query_key_value_weight,
    attention_output_weight,
    attention_bias_stack,
    feedforward_in_weight,
    feedforward_bias,
    feedforward_out_weight,
    adapter_down_weight,
    adapter_up_weight,
    adapter_momentum,
    head,
    head_first_moment,
    head_second_moment,
):
    length = input_token_ids.shape[-1]
    slots = labels.shape[-1]
    width = position_embedding_table.shape[1]
    rank = adapter_up_weight.shape[1]
    parts = lax.axis_size("tensor")
    ids = input_token_ids.reshape(-1, 1, length)
    all_ids = [ids] + [swap(ids, "tensor", r) for r in range(1, parts)]
    segs = segments.reshape(-1, 1, length)
    labs = labels.reshape(-1, 1, slots)
    units = ids.shape[0]


    weights = Weights([feedforward_in_weight, feedforward_out_weight], feedforward_bias, all_ids)
    all_ids, owns = lax.optimization_barrier((weights.first, weights.owns))
    weights.core_own = [swap(own, "tensor", 1) for own in owns]
    weights.core_bias = swap(weights.bias, "tensor", 1)
    picked = embed_call(all_ids, embedding)
    (
        picked,
        weights.mine,
        weights.core_own,
        weights.core_bias,
        head_rows,
    ) = lax.optimization_barrier(
        (
            picked,
            weights.mine,
            weights.core_own,
            weights.core_bias,
            (head, head_first_moment, head_second_moment),
        )
    )
    picked = [picked[u * parts : (u + 1) * parts] for u in range(units)]

    small = (
        position_embedding_table,
        norm_gain_rows,
        norm_shift_rows,
        attention_bias_stack,
        jnp.swapaxes(adapter_down_weight, 1, 2),
        adapter_up_weight,
    )
    kept = None
    moved = []
    for u in range(units):
        while len(moved) < min(u + 2, units):
            sends = picked[len(moved)][1:]
            if moved:
                sends = lax.optimization_barrier((sends, moved[-1], kept))[0]
            moved.append([swap(a, "tensor", r + 1) for r, a in enumerate(sends)])
        if u == units - 1:
            other, moved[u], _ = lax.optimization_barrier((weights.other, moved[u], kept))
            weights.core_other = weights.core(other)
        if u == 0:
            mine, moved[0] = lax.optimization_barrier((weights.mine, moved[0]))
            weights.other = weights.across(mine)
            weights.core_mine = weights.core(mine)
        kept = attend_call(
            [picked[u][0], *moved[u]],
            segs,
            small,
            query_key_value_weight,
            attention_output_weight,
            kept,
            u,
            units,
        )

    arrays, plan = weights.operands()
    acc = finish_call(
        segs,
        labs,
        (norm_gain_rows, norm_shift_rows, attention_bias_stack, head_rows[0]),
        attention_output_weight,
        arrays,
        plan,
        kept,
        parts,
    )
    steps = []
    for axis in ("tensor", "dp"):
        bit = 1
        while bit < lax.axis_size(axis):
            steps.append((axis, bit))
            bit *= 2
    for axis, bit in steps[:-1]:
        acc = acc + swap(acc, axis, bit)
    other = swap(acc, *steps[-1])

    flat = (2 * rank, width)
    outs = update_call(
        acc,
        other,
        adapter_up_weight.reshape(flat),
        adapter_momentum.reshape(flat),
        *head_rows,
    )
    loss, items, norm, moment, new_up, low, first, second, new_head, head_low = outs
    shape = adapter_up_weight.shape
    return (
        loss[0, 0],
        items[0, 0],
        norm[0, 0],
        moment.reshape(shape),
        new_up.reshape(shape),
        low.reshape(shape),
        first,
        second,
        new_head,
        head_low,
    )


def solution(mesh):
    rows = P(None, ("dp", "tensor"), None)
    placed = (
        (rows, rows, rows, P("tensor", None))
        + (P(),) * 6
        + (P(None, "tensor"), P("tensor"), P("tensor", None))
        + (P(),) * 6
    )
    return jax.shard_map(
        local, mesh=mesh, in_specs=placed, out_specs=(P(),) * 10, check_vma=False
    )
```

```python
import functools
import math

import jax
import jax.numpy as jnp
from jax import lax
from jax.experimental import pallas as pl
from jax.experimental.pallas import tpu as pltpu
from jax.sharding import PartitionSpec as P

HEAD_DIM = 64
STEP = 10
LN_EPS = 1e-05
CLIP_NORM = 0.5
ORTHO_MOMENTUM = 0.5
ORTHO_STEP_SIZE = 1.0
NS_A = 3.4445
NS_B = -4.775
NS_C = 2.0315
BETA_ONE = 0.9
BETA_TWO = 0.999
ADAM_RATE = 0.05
ADAM_EPS = 1e-08
DECAY = 0.01

F32 = jnp.float32
BF16 = jnp.bfloat16
LANES = 128
GROUP = 256
PER_GROUP = GROUP // HEAD_DIM
BLOCK = 128
SPAN = 3 * BLOCK
STEP_ROWS = 64
VOCAB_BLOCK = 2048
RING = 6
UNROLL = 128
ACC_ROWS = 24
ADAPTER_ROWS = 16
BIAS_ROWS = 16
MIB = 1024 * 1024
NN = (((1,), (0,)), ((), ()))
NT = (((1,), (1,)), ((), ()))
TN = (((0,), (0,)), ((), ()))
INV_SQRT2 = 1.0 / math.sqrt(2.0)
INV_SQRT_2PI = 1.0 / math.sqrt(2.0 * math.pi)

VMEM = pl.BlockSpec(memory_space=pltpu.VMEM)
SMEM = pl.BlockSpec(memory_space=pltpu.SMEM)
ANY = pl.BlockSpec(memory_space=pl.ANY)


def mm(left, right, dims=NN):
    return lax.dot_general(left, right, dims, preferred_element_type=F32)


def row_mean(rows):
    return jnp.mean(rows, axis=-1, keepdims=True)


def add_all(terms):
    return functools.reduce(jnp.add, terms)


def at(i):
    return pl.ds(pl.multiple_of(i * STEP_ROWS, STEP_ROWS), STEP_ROWS)


def embed_kernel(*refs, parts, units):
    ids = refs[:parts]
    table, tail = refs[parts : parts + 2]
    outs = refs[parts + 2 : parts + 2 + parts * units]
    scratch = refs[parts + 2 + parts * units :]
    feats = table.shape[0]
    full = table.shape[1] // VOCAB_BLOCK
    lanes = [(lo, min(lo + LANES, feats)) for lo in range(0, feats, LANES)]
    turned = scratch[: len(lanes)]
    picked = scratch[len(lanes) : 2 * len(lanes)]
    ring, stage, ring_sems, sems = scratch[2 * len(lanes) :]

    def fetch(i):
        cols = pl.ds(pl.multiple_of(i * VOCAB_BLOCK, VOCAB_BLOCK), VOCAB_BLOCK)
        slot = lax.rem(i, RING)
        return pltpu.make_async_copy(table.at[:, cols], ring.at[slot], ring_sems.at[slot])

    def turn_block(base, block):
        for c in range(0, VOCAB_BLOCK, GROUP):
            rows_at = pl.ds(pl.multiple_of(base + c, GROUP), GROUP)
            for (lo, hi), turn in zip(lanes, turned):
                turn[rows_at, :] = block[lo:hi, c : c + GROUP].T.astype(F32)

    for i in range(min(RING, full)):
        fetch(i).start()
    turn_block(full * VOCAB_BLOCK, tail)

    def step(i, carry):
        fetch(i).wait()
        turn_block(i * VOCAB_BLOCK, ring.at[lax.rem(i, RING)])

        @pl.when(i + RING < full)
        def _():
            fetch(i + RING).start()

        return carry

    lax.fori_loop(0, full, step, 0)

    length = stage.shape[1]
    copies = []
    for p, out in enumerate(outs):
        u, r = p // parts, p % parts
        slot = p % 2

        def rows(i, carry, u=u, r=r):
            top = pl.multiple_of(i * UNROLL, UNROLL)
            for j in range(UNROLL):
                token = ids[r][u, 0, top + j]
                for turn, pick in zip(turned, picked):
                    pick[pl.ds(top + j, 1), :] = turn[pl.ds(token, 1), :]
            return carry

        lax.fori_loop(0, length // UNROLL, rows, 0)
        if p >= 2:
            copies[p - 2].wait()
        for (lo, hi), pick in zip(lanes, picked):
            stage[slot, :, lo:hi] = pick[...].astype(BF16)
        copies.append(pltpu.make_async_copy(stage.at[slot], out, sems.at[slot]))
        copies[p].start()
    for copy in copies[-2:]:
        copy.wait()


def embed_call(ids, table):
    parts = len(ids)
    units, _, length = ids[0].shape
    feats, vocab = table.shape
    full = vocab // VOCAB_BLOCK
    widths = [min(LANES, feats - lo) for lo in range(0, feats, LANES)]
    scratch = [pltpu.VMEM(((full + 1) * VOCAB_BLOCK, w), F32) for w in widths]
    scratch += [pltpu.VMEM((length, w), F32) for w in widths]
    scratch += [
        pltpu.VMEM((RING, feats, VOCAB_BLOCK), BF16),
        pltpu.VMEM((2, length, feats), BF16),
        pltpu.SemaphoreType.DMA((RING,)),
        pltpu.SemaphoreType.DMA((2,)),
    ]
    last = pl.cdiv(vocab, VOCAB_BLOCK) - 1
    tail = pl.BlockSpec((feats, VOCAB_BLOCK), lambda i: (0, last), pipeline_mode=pl.Buffered(1))
    return pl.pallas_call(
        functools.partial(embed_kernel, parts=parts, units=units),
        grid=(1,),
        in_specs=[SMEM] * parts + [ANY, tail],
        out_specs=[ANY] * (parts * units),
        out_shape=[jax.ShapeDtypeStruct((length, feats), BF16)] * (parts * units),
        scratch_shapes=scratch,
        compiler_params=pltpu.CompilerParams(vmem_limit_bytes=62 * MIB),
        name="embed",
    )(*ids, table, table)


def interleave(*lists):
    done = [0] * len(lists)
    while any(n < len(steps) for n, steps in zip(done, lists)):
        share = [n / len(steps) if steps else 1.0 for n, steps in zip(done, lists)]
        i = share.index(min(share))
        lists[i][done[i]]()
        done[i] += 1


def tile_rows(t, rows):
    lo = min(max(2 * t - 1, 0) * BLOCK, rows - min(SPAN, rows))
    return lo, min((2 * t + 3) * BLOCK, rows)


def block_pieces(b, blocks):
    first, last = max(b - 1, 0), min(b + 1, blocks - 1)
    found = []
    for t in range(blocks * BLOCK // GROUP):
        lo, hi = max(first, 2 * t), min(last, 2 * t + 1)
        if lo <= hi:
            found.append((t, lo, hi))
    return found


def spread(values, t, lo, hi):
    zero_block = jnp.zeros((BLOCK, BLOCK), BF16)
    parts = [values] if lo == 2 * t else [zero_block, values]
    if hi == 2 * t:
        parts.append(zero_block)
    return parts[0] if len(parts) == 1 else jnp.concatenate(parts, axis=1)


def head_masks():
    head_of = lax.broadcasted_iota(jnp.int32, (1, GROUP), 1) // HEAD_DIM
    in_head = [head_of == h for h in range(PER_GROUP)]
    return in_head, [jnp.where(m, 1.0, 0.0).astype(BF16) for m in in_head]


def column(row):
    return jnp.broadcast_to(row, (8, row.shape[1])).T[:, 0:1]


def tile_product(tiles, right):
    rows = right.shape[0]
    res = [None] * (rows // BLOCK)
    for t, left in enumerate(tiles):
        part = mm(left, right[t * GROUP : (t + 1) * GROUP])
        first = tile_rows(t, rows)[0] // BLOCK
        for i in range(left.shape[0] // BLOCK):
            piece = part[i * BLOCK : (i + 1) * BLOCK]
            res[first + i] = piece if res[first + i] is None else res[first + i] + piece
    return jnp.concatenate(res, axis=0)


def stacked_scores(left, right, keep):
    rows = left.shape[0]
    found = []
    for t in range(rows // GROUP):
        lo, hi = tile_rows(t, rows)
        stack = jnp.concatenate([left[lo:hi] * keep[h] for h in range(PER_GROUP)], axis=0)
        found.append(mm(stack, right[t * GROUP : (t + 1) * GROUP], NT))
    return found


def attend_kernel(*refs, parts, unit, fresh):
    pieces = refs[:parts]
    seg_ref, gain_ref, shift_ref, bias_ref, down_ref, up_ref, pos_hbm, wqkv_hbm, wo_hbm = refs[
        parts : parts + 9
    ]
    refs = refs[parts + 9 + (0 if fresh else 6) :]
    outs, (x4, pos, wqkv, wo, start, xb, normed0, q, k, v, red, pr, probs, mixed, sems) = (
        refs[:6],
        refs[6:],
    )
    rows, width = normed0.shape
    groups = width // GROUP
    blocks = rows // BLOCK
    tiles = rows // GROUP
    row_parts = [slice(i, i + STEP_ROWS) for i in range(0, rows, STEP_ROWS)]
    me = lax.axis_index("tensor")

    in_copies = [
        pltpu.make_async_copy(piece, x4.at[jnp.bitwise_xor(me, r)], sems.at[r])
        for r, piece in enumerate(pieces)
    ]
    pos_copy = pltpu.make_async_copy(pos_hbm, pos, sems.at[parts])
    qkv_copy = pltpu.make_async_copy(wqkv_hbm, wqkv, sems.at[parts + 1])
    wo_copy = pltpu.make_async_copy(wo_hbm, wo, sems.at[parts + 2])
    start_out, k_out, v_out, red_out, pr_out = [
        pltpu.make_async_copy(ref, out.at[unit], sems.at[parts + 3 + i])
        for i, (ref, out) in enumerate(zip((start, k, v, red, pr), outs))
    ]

    def probs_copy(g):
        heads = pl.ds(g * PER_GROUP, PER_GROUP)
        return pltpu.make_async_copy(
            probs.at[heads], outs[5].at[unit, heads], sems.at[parts + 8 + g]
        )

    for copy in [pos_copy, *in_copies, qkv_copy, wo_copy]:
        copy.start()

    seg_row = seg_ref[unit].astype(F32)
    seg_col = column(seg_row)
    lane = lax.broadcasted_iota(jnp.int32, (rows, rows), 1)
    sub = lax.broadcasted_iota(jnp.int32, (rows, rows), 0)
    before = (seg_col == seg_row) & (lane < sub)
    place = jnp.sum(jnp.where(before, 1.0, 0.0), axis=1, keepdims=True).astype(jnp.int32)
    one_hot = jnp.where(lane == place, 1.0, 0.0).astype(BF16)
    pos_copy.wait()
    start[...] = mm(one_hot, pos[...])
    for copy in in_copies:
        copy.wait()
    start[...] += jnp.concatenate([x4[t] for t in range(parts)], axis=1).astype(F32)

    gain0, shift0 = gain_ref[0:1], shift_ref[0:1]
    for part in row_parts:
        x = start[part, :]
        off = x - row_mean(x)
        y = off * lax.rsqrt(row_mean(off * off) + LN_EPS) * gain0 + shift0
        normed0[part, :] = y + bias_ref[3:4]
        xb[part, :] = y.astype(BF16)

    rank = up_ref.shape[1]
    spot = lax.broadcasted_iota(jnp.int32, (rank, GROUP), 1) % HEAD_DIM
    line = lax.broadcasted_iota(jnp.int32, (rank, GROUP), 0)
    lows = [mm(xb[...], down_ref[i], NT).astype(BF16) for i in range(2)]
    ups = [up_ref[i].astype(BF16) * BF16(2.0) for i in range(2)]
    red[...] = add_all(
        [
            mm(low, jnp.where(spot == line + i * rank, 1.0, 0.0).astype(BF16))
            for i, low in enumerate(lows)
        ]
    ).astype(BF16)
    red_out.start()

    in_head, keep = head_masks()

    def far(b, c):
        hit = seg_col[b * BLOCK : (b + 1) * BLOCK] == seg_row[:, c * BLOCK : (c + 1) * BLOCK]
        return jnp.where(hit, 0.0, -1e9)

    away = {
        (b, c): far(b, c) for b in range(blocks) for c in range(max(b - 1, 0), min(b + 2, blocks))
    }
    memo = {}

    def project(g):
        lanes = slice(g * GROUP, (g + 1) * GROUP)

        def queries():
            new = mm(xb[...], wqkv[0, :, lanes]) + mm(lows[0], ups[0][:, lanes])
            q[:, lanes] = (new + bias_ref[0:1, lanes]).astype(BF16) * BF16(HEAD_DIM**-0.5)

        def keys():
            k[:, lanes] = (mm(xb[...], wqkv[1, :, lanes]) + bias_ref[1:2, lanes]).astype(BF16)

        def values():
            new = mm(xb[...], wqkv[2, :, lanes]) + mm(lows[1], ups[1][:, lanes])
            v[:, lanes] = (new + bias_ref[2:3, lanes]).astype(BF16)

        return [queries, keys, values]

    def attention(g):
        lanes = slice(g * GROUP, (g + 1) * GROUP)

        def begin():
            memo["scores"] = stacked_scores(q[:, lanes], k[:, lanes], keep)
            memo["out"] = jnp.zeros((rows, GROUP), F32)
            memo["low"] = jnp.zeros((rows, GROUP), F32)

        def one_head(h):
            vrh = v[:, lanes] * keep[h] + red[...] * (1 - keep[h])
            prob_tiles = [[] for _ in range(tiles)]
            for b in range(blocks):
                found = []
                for t, lo, hi in block_pieces(b, blocks):
                    first, last = tile_rows(t, rows)
                    top = h * (last - first) + b * BLOCK - first
                    lane_at = slice((lo - 2 * t) * BLOCK, (hi + 1 - 2 * t) * BLOCK)
                    s = memo["scores"][t][top : top + BLOCK, lane_at]
                    found.append(
                        s + jnp.concatenate([away[b, c] for c in range(lo, hi + 1)], axis=1)
                    )
                peak = functools.reduce(
                    jnp.maximum, [jnp.max(s, axis=1, keepdims=True) for s in found]
                )
                found = [jnp.exp(s - peak) for s in found]
                inv = 1.0 / add_all([jnp.sum(s, axis=1, keepdims=True) for s in found])
                for (t, lo, hi), s in zip(block_pieces(b, blocks), found):
                    prob_tiles[t].append(spread((s * inv).astype(BF16), t, lo, hi))
            prob_tiles = [jnp.concatenate(tile, axis=0) for tile in prob_tiles]
            for t, tile in enumerate(prob_tiles):
                probs[g * PER_GROUP + h, t, 0 : tile.shape[0], :] = tile
            res = tile_product(prob_tiles, vrh)
            memo["out"] = jnp.where(in_head[h], res, memo["out"])
            memo["low"] = jnp.where(in_head[(h + 1) % PER_GROUP], res, memo["low"])

        def end():
            mixed[:, lanes] = memo["out"].astype(BF16)
            pr[:, lanes] = memo["low"].astype(BF16)
            probs_copy(g).start()

        return [begin] + [functools.partial(one_head, h) for h in range(PER_GROUP)] + [end]

    def output(g):
        def step(n):
            lanes = slice(n, n + GROUP)
            add = mm(mixed[:, g * GROUP : (g + 1) * GROUP], wo[g * GROUP : (g + 1) * GROUP, lanes])
            start[:, lanes] = (normed0 if g == 0 else start)[:, lanes] + add

        return [functools.partial(step, n) for n in range(0, width, GROUP)]

    qkv_copy.wait()
    interleave(project(0))
    wo_copy.wait()
    for g in range(groups):
        others = project(g + 1) if g + 1 < groups else []
        if g + 1 == groups:
            k_out.start()
            v_out.start()
        interleave(attention(g), others + (output(g - 1) if g else []))
    pr_out.start()
    interleave(output(groups - 1))
    start_out.start()
    for copy in [start_out, k_out, v_out, red_out, pr_out] + [probs_copy(g) for g in range(groups)]:
        copy.wait()


def attend_call(pieces, seg, small, wqkv, wo, kept, unit, units):
    pos, gain, shift, bias, down, up = small
    parts = len(pieces)
    rows, feats = pieces[0].shape
    width = pos.shape[1]
    heads = width // HEAD_DIM
    tiles = rows // GROUP
    forms = [
        ((rows, width), F32),
        ((rows, width), BF16),
        ((rows, width), BF16),
        ((rows, GROUP), BF16),
        ((rows, width), BF16),
        ((heads, tiles, SPAN, GROUP), BF16),
    ]
    fresh = kept is None
    scratch = [
        pltpu.VMEM((parts, rows, feats), BF16),
        pltpu.VMEM(pos.shape, BF16),
        pltpu.VMEM(wqkv.shape, BF16),
        pltpu.VMEM(wo.shape, BF16),
        pltpu.VMEM((rows, width), F32),
        pltpu.VMEM((rows, width), BF16),
        pltpu.VMEM((rows, width), F32),
        pltpu.VMEM((rows, width), BF16),
        pltpu.VMEM((rows, width), BF16),
        pltpu.VMEM((rows, width), BF16),
        pltpu.VMEM((rows, GROUP), BF16),
        pltpu.VMEM((rows, width), BF16),
        pltpu.VMEM((heads, tiles, SPAN, GROUP), BF16),
        pltpu.VMEM((rows, width), BF16),
        pltpu.SemaphoreType.DMA((parts + 8 + width // GROUP,)),
    ]
    args = [*pieces, seg, gain, shift, bias, down, up, pos, wqkv, wo]
    aliases = {} if fresh else {len(args) + i: i for i in range(len(forms))}
    return pl.pallas_call(
        functools.partial(attend_kernel, parts=parts, unit=unit, fresh=fresh),
        out_shape=[jax.ShapeDtypeStruct((units, *shape), kind) for shape, kind in forms],
        in_specs=[ANY] * parts + [VMEM] * 6 + [ANY] * 3 + ([] if fresh else [ANY] * len(forms)),
        out_specs=[ANY] * len(forms),
        input_output_aliases=aliases,
        scratch_shapes=scratch,
        compiler_params=pltpu.CompilerParams(vmem_limit_bytes=58 * MIB),
        cost_estimate=pl.CostEstimate(
            flops=rows * width,
            bytes_accessed=MIB // 4,
            transcendentals=0,
        ),
        name="attend",
    )(*args, *([] if fresh else kept))


def finish_kernel(*refs, plan, arrays, parts):
    seg_ref, label_ref, gain_ref, shift_ref, bias_ref, head_ref, wo_hbm, *refs = refs
    weight_refs, refs = refs[:arrays], refs[arrays:]
    kept, refs = refs[:6], refs[6:]
    packed_ref, acc_ref, refs = refs[0], refs[1], refs[2:]
    bufs, refs = (refs[:6], refs[6:12]), refs[12:]
    xbs, xh1s, stats, refs = refs[:3], refs[3:6], refs[6:9], refs[9:]
    accs, slopes, acts, refs = refs[:2], refs[2:4], refs[4:6], refs[6:]
    wo, win, wout, ffb, mixed, sems, wsems = refs
    units = kept[0].shape[0]
    rows, width = mixed.shape
    hidden_part = win.shape[2]
    chunk = GROUP if hidden_part % GROUP == 0 else hidden_part
    groups = width // GROUP
    blocks = rows // BLOCK
    tiles = rows // GROUP
    row_parts = [slice(i, i + STEP_ROWS) for i in range(0, rows, STEP_ROWS)]
    chunks = [(r, c) for r in range(parts) for c in range(0, hidden_part, chunk)]
    half = lax.rem(lax.axis_index("dp"), 2)

    weight_copies = [[], [], [], []]
    for i, (matrix, array, first, n, r, mine) in enumerate(plan):
        dst = (win, wout, ffb)[matrix].at[r]
        if mine is not None:
            top = pl.multiple_of((half if mine else 1 - half) * n, 16)
            dst = (win, wout, ffb)[matrix].at[r, pl.ds(top, n), :]
        src = weight_refs[array].at[pl.ds(first, n), :]
        weight_copies[matrix].append(pltpu.make_async_copy(src, dst, wsems.at[i]))
    weight_copies[3].append(pltpu.make_async_copy(wo_hbm, wo, wsems.at[len(plan)]))

    state_copies = [
        [
            pltpu.make_async_copy(src.at[u], buf, sems.at[u % 2, i])
            for i, (src, buf) in enumerate(zip(kept, bufs[u % 2]))
        ]
        for u in range(units)
    ]

    def start(copies):
        for copy in copies:
            copy.start()

    def wait(copies):
        for copy in copies:
            copy.wait()

    start(state_copies[0][:1] + weight_copies[2] + weight_copies[0] + weight_copies[1])
    for u in range(1, min(2, units)):
        start(state_copies[u][:1])
    start(weight_copies[3] + state_copies[0][1:])

    gain1, gain2 = gain_ref[1:2], gain_ref[2:3]
    shift1, shift2 = shift_ref[1:2], shift_ref[2:3]
    head_row = head_ref[...].reshape(1, width + 1)
    head, head_bias = head_row[:, 0:width], head_row[:, width : width + 1]
    hg = head * gain2
    hg_mean = row_mean(hg)
    bias4 = bias_ref[4:5]
    base = jnp.sum(shift2 * head, axis=1, keepdims=True)
    in_head, keep = head_masks()
    acc_ref[...] = jnp.zeros(acc_ref.shape, F32)

    def norm1(u):
        resid, xb, xh1, stat1 = bufs[u % 2][0], xbs[u % 3], xh1s[u % 3], stats[u % 3]

        def step(part):
            x = resid[part, :]
            off = x - row_mean(x)
            inv = lax.rsqrt(row_mean(off * off) + LN_EPS)
            xh = off * inv
            xh1[part, :] = xh
            stat1[part, :] = inv
            xb[part, :] = (xh * gain1 + shift1).astype(BF16)

        return [lambda: wait(state_copies[u][:1])] + [
            functools.partial(step, part) for part in row_parts
        ]

    def hidden(r, c):
        return slice(r * hidden_part + c, r * hidden_part + c + chunk)

    def feed_in(u):
        xb, act, slope = xbs[u % 3], acts[u % 2], slopes[u % 2]

        def step(r, c):
            line = ffb[r, 0:1, c : c + chunk].astype(F32)
            pre = mm(xb[...], win[r, :, c : c + chunk]) + line
            phi = 0.5 + 0.5 * lax.erf(pre * INV_SQRT2)
            act[:, hidden(r, c)] = (pre * phi).astype(BF16)
            tail = pre * jnp.exp(-0.5 * pre * pre) * INV_SQRT_2PI
            slope[:, hidden(r, c)] = (phi + tail).astype(BF16)

        return [functools.partial(step, r, c) for r, c in chunks]

    def feed_out(u):
        act, acc = acts[u % 2], accs[u % 2]

        def step(n, r):
            lanes = slice(n, n + GROUP)
            add = mm(act[:, r * hidden_part : (r + 1) * hidden_part], wout[r, :, lanes])
            acc[:, lanes] = add if r == 0 else acc[:, lanes] + add

        return [
            functools.partial(step, n, r) for n in range(0, width, GROUP) for r in range(parts)
        ]

    def head_part(u):
        xb, xh1, acc = xbs[u % 3], xh1s[u % 3], accs[u % 2]
        memo = {"inv": [], "dots": [], "grad": jnp.zeros((8, width), F32)}

        def norm2(part):
            x = xh1[part, :] * gain1 + shift1 + (acc[part, :] + bias4)
            off = x - row_mean(x)
            inv = lax.rsqrt(row_mean(off * off) + LN_EPS)
            xh = off * inv
            acc[part, :] = xh
            memo["inv"].append(inv)
            memo["dots"].append(jnp.sum(xh * hg, axis=1, keepdims=True))

        def items():
            dots = jnp.concatenate(memo["dots"], axis=0)
            seg_row = seg_ref[u].astype(F32)
            seg_col = column(seg_row)
            label = label_ref[u]
            slots = label.shape[1]
            slot_no = lax.broadcasted_iota(jnp.int32, (rows, slots), 1).astype(F32)
            member = jnp.where(seg_col == slot_no, 1.0, 0.0)
            counts = jnp.sum(member, axis=0, keepdims=True)
            sums = jnp.sum(member * (dots + base), axis=0, keepdims=True)
            most = jnp.maximum(counts, 1.0)
            error = jnp.where(counts > 0, sums / most + head_bias - label, 0.0)
            grad_pred = 2.0 * error
            memo["weight"] = jnp.sum(member * (grad_pred / most), axis=1, keepdims=True)
            loss = jnp.sum(error * error, axis=1, keepdims=True)
            weight_sum = jnp.sum(grad_pred, axis=1, keepdims=True)
            memo["sum"] = weight_sum
            count = jnp.max(seg_row, axis=1, keepdims=True) + 1.0
            lane_row = lax.broadcasted_iota(jnp.int32, (1, width), 1)
            acc_ref[17:18, :] += jnp.where(
                lane_row == 0,
                loss,
                jnp.where(lane_row == 1, count, jnp.where(lane_row == 2, weight_sum, 0.0)),
            )

        def back2(i, part):
            xh = acc[part, :]
            w = memo["weight"][part]
            weighted = xh * w
            for j in range(STEP_ROWS // 8):
                memo["grad"] = memo["grad"] + weighted[j * 8 : (j + 1) * 8]
            scaled = memo["dots"][i] * (1.0 / width)
            grad = (memo["inv"][i] * w) * (hg - hg_mean - xh * scaled)
            acc[part, :] = grad
            xb[part, :] = grad.astype(BF16)

        def close():
            total = jnp.sum(memo["grad"], axis=0, keepdims=True)
            acc_ref[16:17, :] += total * gain2 + memo["sum"] * shift2

        return (
            [functools.partial(norm2, part) for part in row_parts]
            + [items]
            + [functools.partial(back2, i, part) for i, part in enumerate(row_parts)]
            + [close]
        )

    def feed_back(u):
        xb, act, slope, acc = xbs[u % 3], acts[u % 2], slopes[u % 2], accs[u % 2]

        def up(r, c):
            back = mm(xb[...], wout[r, c : c + chunk, :], NT)
            act[:, hidden(r, c)] = (back * slope[:, hidden(r, c)].astype(F32)).astype(BF16)

        def down(n, r):
            lanes = slice(n, n + GROUP)
            acc[:, lanes] += mm(
                act[:, r * hidden_part : (r + 1) * hidden_part], win[r, lanes, :], NT
            )

        return [functools.partial(up, r, c) for r, c in chunks] + [
            functools.partial(down, n, r) for n in range(0, width, GROUP) for r in range(parts)
        ]

    def attention_back(u):
        xb, xh1, stat1, acc = xbs[u % 3], xh1s[u % 3], stats[u % 3], accs[u % 2]
        _, k2, v2, red2, pr2, probs2 = bufs[u % 2]
        memo = {}

        def back1(part):
            g = acc[part, :] * gain1
            xh = xh1[part, :]
            grad = stat1[part, :] * (g - row_mean(g) - xh * row_mean(g * xh))
            xb[part, :] = grad.astype(BF16)

        def project(n):
            mixed[:, n : n + GROUP] = mm(xb[...], wo[n : n + GROUP, :], NT).astype(BF16)

        def begin(g):
            lanes = slice(g * GROUP, (g + 1) * GROUP)
            memo["grads"] = stacked_scores(mixed[:, lanes], v2[:, lanes], keep)
            memo["out"] = jnp.zeros((rows, GROUP), F32)

        def one_head(g, h):
            lanes = slice(g * GROUP, (g + 1) * GROUP)
            score_tiles = [[] for _ in range(tiles)]
            for b in range(blocks):
                found = []
                for t, lo, hi in block_pieces(b, blocks):
                    first, last = tile_rows(t, rows)
                    top = b * BLOCK - first
                    lane_at = slice((lo - 2 * t) * BLOCK, (hi + 1 - 2 * t) * BLOCK)
                    here = h * (last - first) + top
                    dp = memo["grads"][t][here : here + BLOCK, lane_at]
                    p = probs2[g * PER_GROUP + h, t, top : top + BLOCK, lane_at]
                    found.append((p.astype(F32), dp))
                shared = add_all([jnp.sum(p * dp, axis=1, keepdims=True) for p, dp in found])
                for (t, lo, hi), (p, dp) in zip(block_pieces(b, blocks), found):
                    score_tiles[t].append(spread((p * (dp - shared)).astype(BF16), t, lo, hi))
            tiles_ = [jnp.concatenate(tile, axis=0) for tile in score_tiles]
            memo["out"] = jnp.where(in_head[h], tile_product(tiles_, k2[:, lanes]), memo["out"])

        def end(g):
            lanes = slice(g * GROUP, (g + 1) * GROUP)
            query_part = mm(red2[...], memo["out"].astype(BF16), TN)[0:8]
            acc_ref[0:8, lanes] += query_part * (2.0 * HEAD_DIM**-0.5)
            cross = mm(pr2[:, lanes], mixed[:, lanes], TN)
            value_part = jnp.zeros((8, GROUP), F32)
            for h in range(PER_GROUP):
                top = ((h + 1) % PER_GROUP) * HEAD_DIM + 8
                value_part = jnp.where(in_head[h], cross[top : top + 8], value_part)
            acc_ref[8:16, lanes] += 2.0 * value_part

        steps = [functools.partial(back1, part) for part in row_parts]
        if u == 0:
            steps.append(lambda: wait(weight_copies[3]))
        steps += [functools.partial(project, n) for n in range(0, width, GROUP)]
        steps.append(lambda: wait(state_copies[u][1:]))
        for g in range(groups):
            steps.append(functools.partial(begin, g))
            steps += [functools.partial(one_head, g, h) for h in range(PER_GROUP)]
            steps.append(functools.partial(end, g))
        return steps

    interleave(norm1(0))
    wait(weight_copies[2] + weight_copies[0])
    interleave(feed_in(0))
    wait(weight_copies[1])
    interleave(feed_out(0), norm1(1) if units > 1 else [])
    for u in range(units):
        later = u + 1 < units
        if u + 2 < units:
            start(state_copies[u + 2][:1])
        if later:
            start(state_copies[u + 1][1:])
        interleave(head_part(u), feed_in(u + 1) if later else [])
        interleave(feed_back(u), norm1(u + 2) if u + 2 < units else [])
        interleave(attention_back(u), feed_out(u + 1) if later else [])

    slabs = width // LANES
    for j in range(slabs):
        lanes = slice(j * LANES, (j + 1) * LANES)
        packed_ref[j * ADAPTER_ROWS : (j + 1) * ADAPTER_ROWS, :] = acc_ref[0:ADAPTER_ROWS, lanes]
    rest = [acc_ref[16:17, j * LANES : (j + 1) * LANES] for j in range(slabs)]
    rest.append(acc_ref[17:18, 0:LANES])
    empty = packed_ref.shape[0] - slabs * ADAPTER_ROWS - len(rest)
    if empty:
        rest.append(jnp.zeros((empty, LANES), F32))
    packed_ref[slabs * ADAPTER_ROWS :, :] = jnp.concatenate(rest, axis=0)


def packed_rows(width):
    slabs = width // LANES
    return pl.cdiv(slabs * ADAPTER_ROWS + slabs + 1, 8) * 8


def finish_call(segs, labels, small, wo, arrays, plan, kept, parts):
    gain, shift, bias, head = small
    units, rows, width = kept[0].shape
    hidden_part = arrays[0].shape[1]
    hidden = hidden_part * parts
    scratch = [pltpu.VMEM((ACC_ROWS, width), F32)]
    scratch += [pltpu.VMEM(a.shape[1:], a.dtype) for a in kept] * 2
    scratch += [pltpu.VMEM((rows, width), BF16)] * 3
    scratch += [pltpu.VMEM((rows, width), F32)] * 3
    scratch += [pltpu.VMEM((rows, 1), F32)] * 3
    scratch += [pltpu.VMEM((rows, width), F32)] * 2
    scratch += [pltpu.VMEM((rows, hidden), BF16)] * 4
    scratch += [
        pltpu.VMEM(wo.shape, BF16),
        pltpu.VMEM((parts, width, hidden_part), BF16),
        pltpu.VMEM((parts, hidden_part, width), BF16),
        pltpu.VMEM((parts, BIAS_ROWS, hidden_part), BF16),
        pltpu.VMEM((rows, width), BF16),
        pltpu.SemaphoreType.DMA((2, len(kept))),
        pltpu.SemaphoreType.DMA((len(plan) + 1,)),
    ]
    return pl.pallas_call(
        functools.partial(finish_kernel, plan=plan, arrays=len(arrays), parts=parts),
        out_shape=jax.ShapeDtypeStruct((packed_rows(width), LANES), F32),
        in_specs=[VMEM] * 6 + [ANY] * (1 + len(arrays) + len(kept)),
        out_specs=VMEM,
        scratch_shapes=scratch,
        compiler_params=pltpu.CompilerParams(vmem_limit_bytes=62 * MIB),
        name="finish",
    )(segs, labels, gain, shift, bias, head, wo, *arrays, *kept)


def update_kernel(
    acc_ref,
    other_ref,
    up_ref,
    momentum_ref,
    head_ref,
    first_ref,
    second_ref,
    loss_ref,
    items_ref,
    norm_ref,
    moment_out,
    up_out,
    low_out,
    first_out,
    second_out,
    head_out,
    head_low_out,
):
    total = acc_ref[...] + other_ref[...]
    width = up_ref.shape[1]
    rank = up_ref.shape[0] // 2
    slabs = width // LANES
    top = slabs * ADAPTER_ROWS
    sums = total[top + slabs : top + slabs + 1]
    items = sums[:, 1:2]
    loss_ref[...] = sums[:, 0:1]
    items_ref[...] = items
    adapter = (
        jnp.concatenate(
            [total[j * ADAPTER_ROWS : (j + 1) * ADAPTER_ROWS] for j in range(slabs)], axis=1
        )
        / items
    )
    head_grad = [total[top + j : top + j + 1] for j in range(slabs)] + [sums[:, 2:3]]
    head_grad = jnp.concatenate(head_grad, axis=1) / items
    norm = jnp.sqrt(jnp.sum(adapter * adapter) + jnp.sum(head_grad * head_grad))
    norm_ref[...] = jnp.full((1, 1), norm, F32)
    factor = jnp.minimum(1.0, CLIP_NORM / (norm_ref[...] + 1e-06))
    moment = ORTHO_MOMENTUM * momentum_ref[...] + factor * adapter
    moment_out[...] = moment

    def dot(left, right, dims=NN):
        return lax.dot_general(
            left, right, dims, preferred_element_type=F32, precision=lax.Precision.HIGHEST
        )

    basis = []
    for i in range(2):
        part = moment[i * rank : (i + 1) * rank]
        size = jnp.sqrt(jnp.sum(jnp.sum(part * part, axis=1, keepdims=True), axis=0, keepdims=True))
        basis.append(part / (size + 1e-07))
    for sweep in range(5):
        gram = [dot(x, x, NT) for x in basis]
        poly = [NS_B * g + NS_C * dot(g, g) for g in gram]
        basis = [NS_A * x + dot(p, x) for x, p in zip(basis, poly)]
    up = up_ref[...] - ORTHO_STEP_SIZE * jnp.concatenate(basis, axis=0)
    up_out[...] = up
    low_out[...] = up.astype(BF16)

    clipped = factor * head_grad
    def as_row(ref):
        return ref[...].reshape(1, width + 1)

    first = BETA_ONE * as_row(first_ref) + (1.0 - BETA_ONE) * clipped
    second = BETA_TWO * as_row(second_ref) + (1.0 - BETA_TWO) * clipped * clipped
    first_hat = first / (1.0 - BETA_ONE**STEP)
    second_hat = second / (1.0 - BETA_TWO**STEP)
    head = as_row(head_ref)
    new_head = head - ADAM_RATE * (first_hat / (jnp.sqrt(second_hat) + ADAM_EPS) + DECAY * head)
    first_out[...] = first[0]
    second_out[...] = second[0]
    head_out[...] = new_head[0]
    head_low_out[...] = new_head[0].astype(BF16)


def update_call(acc, other, up, momentum, head, first, second):
    one = jax.ShapeDtypeStruct((1, 1), F32)
    flat = jax.ShapeDtypeStruct(up.shape, F32)
    row = jax.ShapeDtypeStruct(head.shape, F32)
    return pl.pallas_call(
        update_kernel,
        out_shape=[
            one,
            one,
            one,
            flat,
            flat,
            jax.ShapeDtypeStruct(up.shape, BF16),
            row,
            row,
            row,
            jax.ShapeDtypeStruct(head.shape, BF16),
        ],
        in_specs=[VMEM] * 7,
        out_specs=[VMEM] * 10,
        name="update",
    )(acc, other, up, momentum, head, first, second)


def swap(value, axis, bit):
    size = lax.axis_size(axis)
    return lax.ppermute(value, axis, [(i, i ^ bit) for i in range(size)])


class Weights:
    def __init__(self, owns, bias, after):
        parts = lax.axis_size("tensor")
        half = lax.rem(lax.axis_index("dp"), 2)
        self.owns = owns
        self.sizes = [own.shape[0] // 2 for own in owns]
        self.bias = jnp.pad(bias[None, :], ((0, BIAS_ROWS - 1), (0, 0)))
        cuts = [
            lax.dynamic_slice_in_dim(own, half * n, n, 0) for own, n in zip(owns, self.sizes)
        ]
        if cuts[0].shape[1] == cuts[1].shape[1]:
            cuts = [jnp.concatenate([*cuts, self.bias], axis=0)]
        else:
            cuts.append(self.bias)
        self.one = len(cuts) == 1
        cuts, self.first = lax.optimization_barrier((cuts, after))
        mine = {0: cuts}
        bit = parts // 2
        while bit > 1:
            mine.update({r ^ bit: [swap(a, "tensor", bit) for a in mine[r]] for r in list(mine)})
            bit //= 2
        del mine[0]
        self.mine = mine

    def core(self, pieces):
        return {r ^ 1: [swap(a, "tensor", 1) for a in arrays] for r, arrays in pieces.items()}

    def across(self, pieces):
        return {r: [swap(a, "dp", 1) for a in arrays] for r, arrays in pieces.items()}

    def operands(self):
        arrays = [*self.owns, *self.core_own, self.bias, self.core_bias]
        plan = [(2, 4, 0, BIAS_ROWS, 0, None), (2, 5, 0, BIAS_ROWS, 1, None)]
        for i in range(2):
            n = 2 * self.sizes[i]
            plan += [(i, i, 0, n, 0, None), (i, 2 + i, 0, n, 1, None)]
        for pieces, is_mine in (
            (self.mine, True),
            (self.core_mine, True),
            (self.other, False),
            (self.core_other, False),
        ):
            for r, found in pieces.items():
                first = 0
                for i, n in enumerate([*self.sizes, BIAS_ROWS]):
                    array = len(arrays) + (0 if self.one else i)
                    if i < 2:
                        plan.append((i, array, first, n, r, is_mine))
                    elif is_mine:
                        plan.append((i, array, first, n, r, None))
                    first += n if self.one else 0
                arrays += found
        return arrays, tuple(sorted(plan, key=lambda step: step[0]))


def local(
    input_token_ids,
    segments,
    labels,
    embedding,
    position_embedding_table,
    norm_gain_rows,
    norm_shift_rows,
    query_key_value_weight,
    attention_output_weight,
    attention_bias_stack,
    feedforward_in_weight,
    feedforward_bias,
    feedforward_out_weight,
    adapter_down_weight,
    adapter_up_weight,
    adapter_momentum,
    head,
    head_first_moment,
    head_second_moment,
):
    length = input_token_ids.shape[-1]
    slots = labels.shape[-1]
    width = position_embedding_table.shape[1]
    rank = adapter_up_weight.shape[1]
    parts = lax.axis_size("tensor")
    ids = input_token_ids.reshape(-1, 1, length)
    all_ids = [ids] + [swap(ids, "tensor", r) for r in range(1, parts)]
    segs = segments.reshape(-1, 1, length)
    labs = labels.reshape(-1, 1, slots)
    units = ids.shape[0]


    weights = Weights([feedforward_in_weight, feedforward_out_weight], feedforward_bias, all_ids)
    all_ids, owns = lax.optimization_barrier((weights.first, weights.owns))
    weights.core_own = [swap(own, "tensor", 1) for own in owns]
    weights.core_bias = swap(weights.bias, "tensor", 1)
    picked = embed_call(all_ids, embedding)
    (
        picked,
        weights.mine,
        weights.core_own,
        weights.core_bias,
        head_rows,
    ) = lax.optimization_barrier(
        (
            picked,
            weights.mine,
            weights.core_own,
            weights.core_bias,
            (head, head_first_moment, head_second_moment),
        )
    )
    picked = [picked[u * parts : (u + 1) * parts] for u in range(units)]

    small = (
        position_embedding_table,
        norm_gain_rows,
        norm_shift_rows,
        attention_bias_stack,
        jnp.swapaxes(adapter_down_weight, 1, 2),
        adapter_up_weight,
    )
    kept = None
    moved = []
    for u in range(units):
        while len(moved) < min(u + 2, units):
            sends = picked[len(moved)][1:]
            if moved:
                sends = lax.optimization_barrier((sends, moved[-1], kept))[0]
            moved.append([swap(a, "tensor", r + 1) for r, a in enumerate(sends)])
        if u == units - 1:
            other, moved[u], weights.core_mine, _ = lax.optimization_barrier(
                (weights.other, moved[u], weights.core_mine, kept)
            )
            weights.core_other = weights.core(other)
        if u == 0:
            mine, moved[0] = lax.optimization_barrier((weights.mine, moved[0]))
            weights.other = weights.across(mine)
            weights.core_mine = weights.core(mine)
        kept = attend_call(
            [picked[u][0], *moved[u]],
            segs,
            small,
            query_key_value_weight,
            attention_output_weight,
            kept,
            u,
            units,
        )

    arrays, plan = weights.operands()
    acc = finish_call(
        segs,
        labs,
        (norm_gain_rows, norm_shift_rows, attention_bias_stack, head_rows[0]),
        attention_output_weight,
        arrays,
        plan,
        kept,
        parts,
    )
    steps = []
    for axis in ("tensor", "dp"):
        bit = 1
        while bit < lax.axis_size(axis):
            steps.append((axis, bit))
            bit *= 2
    for axis, bit in steps[:-1]:
        acc = acc + swap(acc, axis, bit)
    other = swap(acc, *steps[-1])

    flat = (2 * rank, width)
    outs = update_call(
        acc,
        other,
        adapter_up_weight.reshape(flat),
        adapter_momentum.reshape(flat),
        *head_rows,
    )
    loss, items, norm, moment, new_up, low, first, second, new_head, head_low = outs
    shape = adapter_up_weight.shape
    return (
        loss[0, 0],
        items[0, 0],
        norm[0, 0],
        moment.reshape(shape),
        new_up.reshape(shape),
        low.reshape(shape),
        first,
        second,
        new_head,
        head_low,
    )


def solution(mesh):
    rows = P(None, ("dp", "tensor"), None)
    placed = (
        (rows, rows, rows, P("tensor", None))
        + (P(),) * 6
        + (P(None, "tensor"), P("tensor"), P("tensor", None))
        + (P(),) * 6
    )
    return jax.shard_map(
        local, mesh=mesh, in_specs=placed, out_specs=(P(),) * 10, check_vma=False
    )
```
